256 devices in a mesh: seq: 64 (over z, x, core), head: 4 (over y).
Axes of the slice: x: 4, y: 4, z: 8, core: 2. Of those that a mesh axis runs over, the one named last changes fastest.
Arguments:
- queries: bfloat16 [16384, 2048], P('seq', 'head'), may hold values from -30 to 30
- key_rows: bfloat16 [16384, 2048], P('seq', 'head'), may hold values from -5 to 5
- value_rows: bfloat16 [16384, 2048], P('seq', 'head'), may hold values from -6 to 6
- out_grad: bfloat16 [16384, 2048], P('seq', 'head'), may hold values from -6 to 6
- random_blocks: int32 [4, 256, 3], P('head'), may hold values from 0 to 255, as said below
- global_blocks: int32 [2], replicated, may hold values from 0 to 255, as said below
Outputs:
- attended: bfloat16 [16384, 2048], P('seq', 'head')
- query_grad: bfloat16 [16384, 2048], P('seq', 'head')
- key_grad: bfloat16 [16384, 2048], P('seq', 'head')
- value_grad: bfloat16 [16384, 2048], P('seq', 'head')
The draws below stay inside these ranges and needn't reach their ends.
Inputs may be any that keep to these rules, and one draw needn't show every extreme that they name: `random_blocks`: in each head group, the query blocks s * 4 to s * 4 + 3 of one segment name at most 1 random entries inside any one segment of 4 key blocks, and for every such query segment some key segment is named exactly 1 times. `global_blocks`: the global blocks are different from each other, and one of them is the last block, 255.
All inputs are finite; a program needn't handle non-finite values.
Results may differ from the reference program's by a relative error of at most 0.039.
Values may be sent and summed in bfloat16 or wider, within the bound.
A program may use at most 128 MiB of HBM per device.

```python
import math
import jax
import jax.numpy as jnp
from jax import lax

HEADS = 16
HEAD_DIM = 128
BLK = 64
GLOBALS = 2
RANDOMS = 3
BLK_DEV = 4
HG = 4
NB = 256
SEQ_LEN = 16384


def draw_queries(key, part):
    shape = (SEQ_LEN, HEADS * HEAD_DIM)
    drawn = jnp.clip(jax.random.normal(jax.random.fold_in(key, 1), shape, jnp.float32), -4.0, 4.0)
    return drawn.astype(jnp.bfloat16)


def draw_key_rows(key, part):
    shape = (SEQ_LEN, HEADS * HEAD_DIM)
    drawn = jnp.clip(jax.random.normal(jax.random.fold_in(key, 2), shape, jnp.float32), -4.0, 4.0)
    return drawn.astype(jnp.bfloat16)


def draw_random_blocks(key, part):
    segments = NB // BLK_DEV
    request_count = BLK_DEV * RANDOMS
    perm_keys = jax.random.split(jax.random.fold_in(key, 11), HG * segments)
    owners_perm = jax.vmap(lambda single: jax.random.permutation(single, segments))(perm_keys)
    order_keys = jax.random.split(jax.random.fold_in(key, 12), HG * segments)
    orders = jax.vmap(lambda single: jax.random.permutation(single, request_count))(order_keys)
    owners = jnp.take_along_axis(owners_perm, orders % segments, axis=1)
    inside = jax.random.randint(jax.random.fold_in(key, 13), (HG * segments, request_count), 0, BLK_DEV)
    blocks = owners * BLK_DEV + inside
    return blocks.reshape(HG, NB, RANDOMS).astype(jnp.int32)


def draw_global_blocks(key, part):
    first = jax.random.randint(jax.random.fold_in(key, 21), (), 0, NB - 1)
    flipped = jax.random.randint(jax.random.fold_in(key, 22), (), 0, 2)
    last = jnp.asarray(NB - 1, jnp.int32)
    return jnp.where(flipped == 1, jnp.stack([last, first]), jnp.stack([first, last])).astype(jnp.int32)


def shard_levels(stream_key, shape, cuts, smallest, largest):
    loudness = 1.0
    for position, blocks in cuts:
        heights = jax.random.uniform(jax.random.fold_in(jax.random.fold_in(stream_key, 6), position), (blocks,), jnp.float32, smallest / len(cuts), largest / len(cuts))
        loudness = loudness * jnp.repeat(jnp.exp(heights), shape[position] // blocks).reshape((-1,) + (1,) * (len(shape) - 1 - position))
    return loudness


def bell_draw(own_key, shape, spread, reach, pieces=(), kind=jnp.bfloat16):
    gain = shard_levels(own_key, shape, pieces, -0.22, 0.18) if pieces else 1.0
    array = jax.random.normal(own_key, shape, jnp.float32) * spread * gain
    return jnp.minimum(jnp.maximum(array, -reach), reach).astype(kind)


def setup_inputs(seed: int = 0) -> dict:
    seeds = jax.random.split(jax.random.key(seed), 7)
    return {
        "queries": draw_queries(jax.random.fold_in(seeds[6], 71), 0),
        "key_rows": draw_key_rows(jax.random.fold_in(seeds[6], 71), 0),
        "value_rows": bell_draw(seeds[2], (SEQ_LEN, HEADS * HEAD_DIM), 1.0, 6.0, ((0, 64), (1, 4))),
        "out_grad": bell_draw(seeds[3], (SEQ_LEN, HEADS * HEAD_DIM), 1.0, 6.0, ((0, 64), (1, 4))),
        "random_blocks": draw_random_blocks(jax.random.fold_in(seeds[6], 71), 0),
        "global_blocks": draw_global_blocks(jax.random.fold_in(seeds[6], 71), 0),
    }


def key_table(global_blocks):
    blocks = jnp.arange(NB, dtype=jnp.int32)
    window = jnp.stack([blocks - 1, blocks, blocks + 1], axis=1)
    window_ok = (window >= 0) & (window < NB)
    window = jnp.clip(window, 0, NB - 1).astype(jnp.int32)
    global_ids = jnp.broadcast_to(global_blocks.astype(jnp.int32)[None, :], (NB, GLOBALS))
    return (window, window_ok, global_ids)

def group_pass(query_grp, key_grp, value_grp, grad_grp, table, valid):
    score_scale = 1.0 / math.sqrt(HEAD_DIM)
    width_shape = key_grp.shape

    def step(carry, inputs):
        key_acc, value_acc = carry
        query_block, grad_block, index_list, index_ok = inputs
        key_sel = key_grp[index_list].astype(jnp.float32)
        value_sel = value_grp[index_list].astype(jnp.float32)
        query_f = query_block.astype(jnp.float32)
        grad_f = grad_block.astype(jnp.float32)
        scores = jnp.einsum('qhd,ekhd->hqek', query_f, key_sel) * score_scale
        scores = jnp.where(index_ok[None, None, :, None], scores, -jnp.inf)
        row_max = lax.optimization_barrier(jnp.max(scores, axis=(2, 3), keepdims=True))
        raw = jnp.exp(scores - row_max)
        weights = raw / lax.optimization_barrier(jnp.sum(raw, axis=(2, 3), keepdims=True))
        weights_b = weights.astype(jnp.bfloat16).astype(jnp.float32)
        attended = jnp.einsum('hqek,ekhd->qhd', weights_b, value_sel).astype(jnp.bfloat16)
        row_dot = lax.optimization_barrier(jnp.sum(grad_f * attended.astype(jnp.float32), axis=-1))
        weight_grads = jnp.einsum('qhd,ekhd->hqek', grad_f, value_sel)
        score_grads = (weights * (weight_grads - jnp.transpose(row_dot)[:, :, None, None]) * score_scale).astype(jnp.bfloat16)
        score_f = score_grads.astype(jnp.float32)
        query_grad = jnp.einsum('hqek,ekhd->qhd', score_f, key_sel).astype(jnp.bfloat16)
        key_terms = jnp.einsum('hqek,qhd->ekhd', score_f, query_f).astype(jnp.bfloat16)
        value_terms = jnp.einsum('hqek,qhd->ekhd', weights_b, grad_f).astype(jnp.bfloat16)
        key_acc = key_acc.at[index_list].add(key_terms.astype(jnp.float32))
        value_acc = value_acc.at[index_list].add(value_terms.astype(jnp.float32))
        return ((key_acc, value_acc), (attended, query_grad))
    start = (jnp.zeros(width_shape, jnp.float32), jnp.zeros(width_shape, jnp.float32))
    (key_acc, value_acc), (attended, query_grad) = lax.scan(step, start, (query_grp, grad_grp, table, valid))
    return (attended, query_grad, key_acc.astype(jnp.bfloat16), value_acc.astype(jnp.bfloat16))

def reference(queries, key_rows, value_rows, out_grad, random_blocks, global_blocks):
    group_heads = HEADS // HG
    features = group_heads * HEAD_DIM
    window, window_ok, global_ids = key_table(global_blocks)
    shape = (NB, BLK, group_heads, HEAD_DIM)
    results = [[], [], [], []]
    for group in range(HG):
        lo = group * features
        hi = lo + features
        table = jnp.concatenate([window, global_ids, random_blocks[group].astype(jnp.int32)], axis=1)
        extra_ok = table[:, 3:] >= 0
        valid = jnp.concatenate([window_ok, extra_ok], axis=1)
        parts = group_pass(queries[:, lo:hi].reshape(shape), key_rows[:, lo:hi].reshape(shape), value_rows[:, lo:hi].reshape(shape), out_grad[:, lo:hi].reshape(shape), table, valid)
        for slot in range(4):
            results[slot].append(parts[slot].reshape(SEQ_LEN, features))
    return (jnp.concatenate(results[0], axis=1), jnp.concatenate(results[1], axis=1), jnp.concatenate(results[2], axis=1), jnp.concatenate(results[3], axis=1))
```

```python
import functools
import math

import jax
import jax.numpy as jnp
from jax import lax
from jax.experimental import pallas as pl
from jax.experimental.pallas import tpu as pltpu
from jax.sharding import PartitionSpec as P

HEAD_DIM = 128
BLK = 64
NZ = 8
NX = 4
NC = 2
NSEQ = NZ * NX * NC
BLK_DEV = 4
REQ = 12
SLOTS = 2 * REQ + 2
VMEM_LIMIT = 56 * 1024 * 1024


def seq_of(z, x, c):
    return (lax.rem(z + NZ, NZ) * NX + lax.rem(x + NX, NX)) * NC + c


def place():
    me = lax.axis_index("seq")
    z = me // (NX * NC)
    x = lax.rem(me // NC, NX)
    c = lax.rem(me, NC)
    return me, z, x, c


def remote(src, dst, send_sem, recv_sem, target):
    return pltpu.make_async_remote_copy(
        src_ref=src,
        dst_ref=dst,
        send_sem=send_sem,
        recv_sem=recv_sem,
        device_id={"seq": target},
        device_id_type=pl.DeviceIdType.MESH,
    )


def greet(partners):
    barrier = pltpu.get_barrier_semaphore()
    for partner in partners:
        pl.semaphore_signal(
            barrier, inc=1, device_id={"seq": partner}, device_id_type=pl.DeviceIdType.MESH
        )
    pl.semaphore_wait(barrier, len(partners))


def gather_kernel(
    table, globals_, k_ref, v_ref, out_ref, halo_ref,
    ag, s1_out, s1_in, s2_out, s2_in, s3_out, s3_in, give,
    pair_sem, halo_send, halo_recv, z_send, z_recv, x_send, x_recv, give_sem,
):
    me, z, x, c = place()
    other = 1 - c
    sibling = seq_of(z, x, other)
    after = lax.rem(me + 1, NSEQ)
    before = lax.rem(me + NSEQ - 1, NSEQ)
    sigma = 1 - 2 * c
    far = seq_of(z, x + sigma, c)
    near = seq_of(z, x - sigma, c)
    zs = (seq_of(z + 1, x, c), seq_of(z - 1, x, c))
    greet((after, before, zs[0], zs[1], far, near))

    def pair_copy(src):
        return remote(
            src, ag.at[pl.ds(z * 8 + c * 4, 4)], pair_sem.at[0], pair_sem.at[1], sibling
        )

    own = ag.at[pl.ds(z * 8 + c * 4, 4)]

    @pl.when(c == 0)
    def _():
        pair_copy(v_ref).start()
        own[...] = k_ref[...]

    @pl.when(c == 1)
    def _():
        pair_copy(k_ref).start()
        own[...] = v_ref[...]

    def z_piece(direction, step, half):
        origin = lax.rem(z + NZ - (step - 1), NZ) if direction == 0 else lax.rem(z + step - 1, NZ)
        piece = ag.at[pl.ds(origin * 8 + half * 4, 4)]
        return remote(
            piece,
            piece,
            z_send.at[direction, step - 1, half],
            z_recv.at[direction, step - 1, half],
            zs[direction],
        )

    for direction in range(2):
        z_piece(direction, 1, c).start()
    pair_copy(v_ref).wait()
    for direction in range(2):
        z_piece(direction, 1, other).start()

    halos = []
    for number, ref in enumerate((k_ref, v_ref)):
        halos.append(
            remote(
                ref.at[3], halo_ref.at[number, 0], halo_send.at[number, 0],
                halo_recv.at[number, 0], after,
            )
        )
        halos.append(
            remote(
                ref.at[0], halo_ref.at[number, 1], halo_send.at[number, 1],
                halo_recv.at[number, 1], before,
            )
        )
    for copy in halos:
        copy.start()

    last = {(0, 0): 4, (0, 1): 3, (1, 0): 3, (1, 1): 4}
    for step in range(1, 5):
        for half in range(2):
            for direction in range(2):
                if step <= last[direction, half]:
                    z_piece(direction, step, half).wait_recv()
                    if step + 1 <= last[direction, half]:
                        z_piece(direction, step + 1, half).start()

    def request(chip, slot):
        if slot < 2 * REQ:
            return table[seq_of(z, chip, 0) * REQ + slot]
        return globals_[slot - 2 * REQ]

    def wanted(chip, slot):
        block = request(chip, slot)
        source = lax.rem(lax.div(block, 8), NX)
        return source, ag[lax.div(block, 32) * 8 + lax.rem(block, 8)]

    def x_copy(number, src, dst, target):
        return remote(src, dst, x_send.at[number], x_recv.at[number], target)

    first = x_copy(0, s1_out, s1_in, far)
    for slot in range(SLOTS):
        s1_out[slot] = wanted(x + 2, slot)[1]
    first.start()
    third = x_copy(2, s3_out, s3_in, near)
    for slot in range(SLOTS):
        s3_out[slot] = wanted(x - sigma, slot)[1]
    third.start()
    first.wait_recv()
    second = x_copy(1, s2_out, s2_in, far)
    for slot in range(SLOTS):
        source, mine = wanted(x + sigma, slot)
        s2_out[slot] = jnp.where(source == x, mine, s1_in[slot])
    second.start()
    third.wait_recv()
    second.wait_recv()

    here = lax.rem(x + sigma + NX, NX)

    def chosen(slot_of_table, slot):
        block = slot_of_table
        source = lax.rem(lax.div(block, 8), NX)
        mine = ag[lax.div(block, 32) * 8 + lax.rem(block, 8)]
        return jnp.where(
            source == x, mine, jnp.where(source == here, s3_in[slot], s2_in[slot])
        )

    for i in range(REQ):
        slot = other * REQ + i
        give[i] = chosen(table[seq_of(z, x, 0) * REQ + slot], slot)
    for i in range(2):
        value = chosen(globals_[i], 2 * REQ + i)
        give[REQ + i] = value
        out_ref[c, REQ + i] = value
    handed = remote(give, out_ref.at[c], give_sem.at[0], give_sem.at[1], sibling)
    handed.start()
    for i in range(REQ):
        slot = c * REQ + i
        out_ref[c, i] = chosen(table[seq_of(z, x, 0) * REQ + slot], slot)

    for copy in halos:
        copy.wait()
    for step in range(1, 5):
        for half in range(2):
            for direction in range(2):
                if step <= last[direction, half]:
                    z_piece(direction, step, half).wait_send()
    first.wait_send()
    second.wait_send()
    third.wait_send()
    handed.wait()


def gather(table, globals_, k, v):
    features = k.shape[-1]
    big = pltpu.VMEM((SLOTS, BLK, features), jnp.bfloat16)
    vmem = pl.BlockSpec(memory_space=pltpu.VMEM)
    smem = pl.BlockSpec(memory_space=pltpu.SMEM)
    dma = pltpu.SemaphoreType.DMA
    return pl.pallas_call(
        gather_kernel,
        out_shape=(
            jax.ShapeDtypeStruct((2, REQ + 2, BLK, features), jnp.bfloat16),
            jax.ShapeDtypeStruct((2, 2, BLK, features), jnp.bfloat16),
        ),
        in_specs=[smem, smem, vmem, vmem],
        out_specs=(vmem, vmem),
        scratch_shapes=[
            pltpu.VMEM((NZ * 8, BLK, features), jnp.bfloat16),
            big, big, big, big, big, big,
            pltpu.VMEM((REQ + 2, BLK, features), jnp.bfloat16),
            dma((2,)), dma((2, 2)), dma((2, 2)), dma((2, 4, 2)), dma((2, 4, 2)),
            dma((3,)), dma((3,)), dma((2,)),
        ],
        compiler_params=pltpu.CompilerParams(
            collective_id=0, has_side_effects=True, vmem_limit_bytes=VMEM_LIMIT
        ),
        name="gather_blocks",
    )(table, globals_, k, v)


def nt(a, b):
    return lax.dot_general(a, b, (((1,), (1,)), ((), ())), preferred_element_type=jnp.float32)


def tn(a, b):
    return lax.dot_general(a, b, (((0,), (0,)), ((), ())), preferred_element_type=jnp.float32)


def nn(a, b):
    return lax.dot_general(a, b, (((1,), (0,)), ((), ())), preferred_element_type=jnp.float32)


def attend_kernel(
    q_ref, g_ref, k_ref, v_ref, halo_ref, slot_ref,
    att_ref, qg_ref, wacc_ref, term_ref, rim_ref, acc, gacc,
):
    me = lax.axis_index("seq")
    features = q_ref.shape[-1]
    heads = features // HEAD_DIM
    scale = 1.0 / math.sqrt(HEAD_DIM)
    lane_head = lax.broadcasted_iota(jnp.int32, (BLK, features), 1) // HEAD_DIM
    acc[...] = jnp.zeros_like(acc)
    gacc[...] = jnp.zeros_like(gacc)

    def spread(rows):
        zero = jnp.zeros_like(rows)
        return jnp.concatenate(
            [jnp.where(lane_head == h, rows, zero) for h in range(heads)], axis=0
        )

    def diagonal(full):
        return jnp.concatenate(
            [
                full[h * BLK : (h + 1) * BLK, h * HEAD_DIM : (h + 1) * HEAD_DIM]
                for h in range(heads)
            ],
            axis=1,
        )

    for b in range(BLK_DEV):
        def listed(number, own):
            window = [
                halo_ref[number, 0] if b == 0 else own[b - 1],
                own[b],
                halo_ref[number, 1] if b == BLK_DEV - 1 else own[b + 1],
            ]
            extra = [slot_ref[number, REQ], slot_ref[number, REQ + 1]]
            random = [slot_ref[number, 3 * b + i] for i in range(3)]
            return jnp.concatenate(window + extra + random, axis=0)

        keys = listed(0, k_ref)
        values = listed(1, v_ref)
        query = spread(q_ref[b])
        grad = spread(g_ref[b])
        scores = nt(keys, query) * scale
        if b == 0:
            scores = jnp.concatenate(
                [jnp.where(me == 0, -jnp.inf, scores[:BLK]), scores[BLK:]], axis=0
            )
        if b == BLK_DEV - 1:
            scores = jnp.concatenate(
                [
                    scores[: 2 * BLK],
                    jnp.where(me == NSEQ - 1, -jnp.inf, scores[2 * BLK : 3 * BLK]),
                    scores[3 * BLK :],
                ],
                axis=0,
            )
        row_max = jnp.max(scores, axis=0, keepdims=True)
        raw = jnp.exp(scores - row_max)
        weights = raw * (1.0 / jnp.sum(raw, axis=0, keepdims=True))
        weights_b = weights.astype(jnp.bfloat16)
        weight_grads = nt(values, grad)
        row_dot = jnp.sum(weights_b.astype(jnp.float32) * weight_grads, axis=0, keepdims=True)
        score_grads = (weights * (weight_grads - row_dot) * scale).astype(jnp.bfloat16)
        att_ref[b] = diagonal(tn(weights_b, values)).astype(jnp.bfloat16)
        qg_ref[b] = diagonal(tn(score_grads, keys)).astype(jnp.bfloat16)
        for number, terms in enumerate((nn(score_grads, query), nn(weights_b, grad))):
            for i in range(3):
                acc[number, b + i] += terms[i * BLK : (i + 1) * BLK]
            for i in range(2):
                gacc[number, i] += terms[(3 + i) * BLK : (4 + i) * BLK]
            for i in range(3):
                term_ref[number, 3 * b + i] = terms[(5 + i) * BLK : (6 + i) * BLK].astype(
                    jnp.bfloat16
                )
    for number in range(2):
        for i in range(2):
            term_ref[number, REQ + i] = gacc[number, i].astype(jnp.bfloat16)
        rim_ref[number, 0] = acc[number, 0].astype(jnp.bfloat16)
        rim_ref[number, 1] = acc[number, BLK_DEV + 1].astype(jnp.bfloat16)
        for i in range(BLK_DEV):
            wacc_ref[number, i] = acc[number, i + 1]


def attend(q, g, k, v, halo, slots):
    features = q.shape[-1]
    vmem = pl.BlockSpec(memory_space=pltpu.VMEM)
    own = jax.ShapeDtypeStruct((BLK_DEV, BLK, features), jnp.bfloat16)
    return pl.pallas_call(
        attend_kernel,
        out_shape=(
            own,
            own,
            jax.ShapeDtypeStruct((2, BLK_DEV, BLK, features), jnp.float32),
            jax.ShapeDtypeStruct((2, REQ + 2, BLK, features), jnp.bfloat16),
            jax.ShapeDtypeStruct((2, 2, BLK, features), jnp.bfloat16),
        ),
        in_specs=[vmem] * 6,
        out_specs=(vmem,) * 5,
        scratch_shapes=[
            pltpu.VMEM((2, BLK_DEV + 2, BLK, features), jnp.float32),
            pltpu.VMEM((2, 2, BLK, features), jnp.float32),
        ],
        compiler_params=pltpu.CompilerParams(vmem_limit_bytes=VMEM_LIMIT),
        name="attend_blocks",
    )(q, g, k, v, halo, slots)


def spread_kernel(
    term_ref, rim_ref, all_ref, edge_ref, theirs,
    pair_sem, rim_send, rim_recv, x_send, x_recv, g_send, g_recv,
):
    me, z, x, c = place()
    other = 1 - c
    sibling = seq_of(z, x, other)
    after = lax.rem(me + 1, NSEQ)
    before = lax.rem(me + NSEQ - 1, NSEQ)
    sigma = 1 - 2 * c
    xs = (seq_of(z, x + sigma, c), seq_of(z, x - sigma, c))
    greet((after, before, xs[0], xs[1]))
    pair = remote(term_ref.at[other], theirs, pair_sem.at[0], pair_sem.at[1], sibling)
    pair.start()

    def part(chip, core):
        return all_ref.at[lax.rem(chip + NX, NX), pl.ds(core * REQ, REQ)]

    def rest(chip):
        return all_ref.at[lax.rem(chip + NX, NX), pl.ds(2 * REQ, 2)]

    def send(number, ref, direction, core):
        return remote(
            ref, ref, x_send.at[number, core], x_recv.at[number, core], xs[direction]
        )

    for i in range(REQ):
        all_ref[x, c * REQ + i] = term_ref[c, i]
    for number in range(2):
        send(number, part(x, c), number, c).start()
    edges = []
    for number in range(2):
        edges.append(
            remote(
                rim_ref.at[number, 1], edge_ref.at[number, 0], rim_send.at[number, 0],
                rim_recv.at[number, 0], after,
            )
        )
        edges.append(
            remote(
                rim_ref.at[number, 0], edge_ref.at[number, 1], rim_send.at[number, 1],
                rim_recv.at[number, 1], before,
            )
        )
    pair.wait_recv()
    for i in range(REQ):
        all_ref[x, other * REQ + i] = theirs[i]
    for number in range(2):
        send(number, part(x, other), number, other).start()
    for i in range(2):
        total = term_ref[c, REQ + i].astype(jnp.float32) + theirs[REQ + i].astype(jnp.float32)
        all_ref[x, 2 * REQ + i] = total.astype(jnp.bfloat16)
    for number in range(2):
        remote(rest(x), rest(x), g_send.at[number], g_recv.at[number], xs[number]).start()
    for copy in edges:
        copy.start()
    for core in (c, other):
        send(0, part(x - sigma, core), 0, core).wait_recv()
        send(2, part(x - sigma, core), 0, core).start()
    remote(rest(x), rest(x - sigma), g_send.at[0], g_recv.at[0], xs[0]).wait_recv()
    remote(rest(x - sigma), rest(x - sigma), g_send.at[2], g_recv.at[2], xs[0]).start()
    for number in (1, 2):
        for core in (c, other):
            send(number, part(x, core), 0, core).wait_recv()
        remote(rest(x), rest(x), g_send.at[number], g_recv.at[number], xs[0]).wait_recv()
    for number in range(3):
        for core in (c, other):
            send(number, part(x, core), 0, core).wait_send()
        remote(rest(x), rest(x), g_send.at[number], g_recv.at[number], xs[0]).wait_send()
    pair.wait_send()
    for copy in edges:
        copy.wait()


def spread_terms(terms, rims):
    features = terms.shape[-1]
    vmem = pl.BlockSpec(memory_space=pltpu.VMEM)
    dma = pltpu.SemaphoreType.DMA
    return pl.pallas_call(
        spread_kernel,
        out_shape=(
            jax.ShapeDtypeStruct((NX, SLOTS, BLK, features), jnp.bfloat16),
            jax.ShapeDtypeStruct((2, 2, BLK, features), jnp.bfloat16),
        ),
        in_specs=[vmem, vmem],
        out_specs=(vmem, vmem),
        scratch_shapes=[
            pltpu.VMEM((REQ + 2, BLK, features), jnp.bfloat16),
            dma((2,)), dma((2, 2)), dma((2, 2)), dma((3, 2)), dma((3, 2)), dma((3,)), dma((3,)),
        ],
        compiler_params=pltpu.CompilerParams(
            collective_id=1, has_side_effects=True, vmem_limit_bytes=VMEM_LIMIT
        ),
        name="spread_terms",
    )(terms, rims)


def land_kernel(table, globals_, all_ref, acc_ref):
    me, z, x, c = place()
    acc_ref[...] = jnp.zeros_like(acc_ref)

    def add(chip, slot, block):
        @pl.when(lax.rem(lax.div(block, 8), NX) == x)
        def _():
            at = lax.div(block, 32) * 8 + lax.rem(block, 8)
            acc_ref[at] += all_ref[chip, slot].astype(jnp.float32)

    @pl.loop(0, NX)
    def _(chip):
        @pl.loop(0, 2 * REQ)
        def _(slot):
            add(chip, slot, table[seq_of(z, chip, 0) * REQ + slot])

        for i in range(2):
            add(chip, 2 * REQ + i, globals_[i])


def land(table, globals_, everything):
    features = everything.shape[-1]
    vmem = pl.BlockSpec(memory_space=pltpu.VMEM)
    smem = pl.BlockSpec(memory_space=pltpu.SMEM)
    return pl.pallas_call(
        land_kernel,
        out_shape=jax.ShapeDtypeStruct((NZ * 8, BLK, features), jnp.float32),
        in_specs=[smem, smem, vmem],
        out_specs=vmem,
        compiler_params=pltpu.CompilerParams(vmem_limit_bytes=VMEM_LIMIT),
        name="land_terms",
    )(table, globals_, everything)


def scatter_kernel(acc_ref, out_ref, send_buf, recv_buf, give, z_send, z_recv, give_sem):
    me, z, x, c = place()
    other = 1 - c
    sibling = seq_of(z, x, other)
    zs = (seq_of(z + 1, x, c), seq_of(z - 1, x, c))
    greet((sibling, zs[0], zs[1]))
    start = {(0, 0): 4, (0, 1): 3, (1, 0): 3, (1, 1): 4}

    def piece(direction, distance, half):
        return remote(
            send_buf.at[direction, distance - 1, half],
            recv_buf.at[direction, distance - 1, half],
            z_send.at[direction, distance - 1, half],
            z_recv.at[direction, distance - 1, half],
            zs[direction],
        )

    for distance in range(4, 0, -1):
        for half in range(2):
            for direction in range(2):
                if distance > start[direction, half]:
                    continue
                target = lax.rem(z + (distance if direction == 0 else NZ - distance), NZ)
                total = acc_ref[pl.ds(target * 8 + half * 4, 4)]
                if distance < start[direction, half]:
                    piece(direction, distance + 1, half).wait_recv()
                    total += recv_buf[direction, distance, half].astype(jnp.float32)
                send_buf[direction, distance - 1, half] = total.astype(jnp.bfloat16)
                piece(direction, distance, half).start()

    def finished(half):
        total = acc_ref[pl.ds(z * 8 + half * 4, 4)]
        for direction in range(2):
            total += recv_buf[direction, 0, half].astype(jnp.float32)
        return total.astype(jnp.bfloat16)

    for half in range(2):
        for direction in range(2):
            piece(direction, 1, half).wait_recv()
    give[...] = finished(other)
    handed = remote(give, out_ref.at[c], give_sem.at[0], give_sem.at[1], sibling)
    handed.start()
    out_ref[c] = finished(c)
    for distance in range(4, 0, -1):
        for half in range(2):
            for direction in range(2):
                if distance <= start[direction, half]:
                    piece(direction, distance, half).wait_send()
    handed.wait()


def scatter(acc):
    features = acc.shape[-1]
    vmem = pl.BlockSpec(memory_space=pltpu.VMEM)
    dma = pltpu.SemaphoreType.DMA
    ring = pltpu.VMEM((2, 4, 2, BLK_DEV, BLK, features), jnp.bfloat16)
    return pl.pallas_call(
        scatter_kernel,
        out_shape=jax.ShapeDtypeStruct((2, BLK_DEV, BLK, features), jnp.bfloat16),
        in_specs=[vmem],
        out_specs=vmem,
        scratch_shapes=[
            ring, ring,
            pltpu.VMEM((BLK_DEV, BLK, features), jnp.bfloat16),
            dma((2, 4, 2)), dma((2, 4, 2)), dma((2,)),
        ],
        compiler_params=pltpu.CompilerParams(
            collective_id=2, has_side_effects=True, vmem_limit_bytes=VMEM_LIMIT
        ),
        name="scatter_sums",
    )(acc)


def per_device(queries, key_rows, value_rows, out_grad, random_blocks, global_blocks):
    row_count, features = queries.shape
    blocks = (BLK_DEV, BLK, features)
    table = random_blocks.reshape(-1)
    k = key_rows.reshape(blocks)
    v = value_rows.reshape(blocks)
    slots, halo = gather(table, global_blocks, k, v)
    attended, query_grad, wacc, terms, rims = attend(
        queries.reshape(blocks), out_grad.reshape(blocks), k, v, halo, slots
    )
    everything, edges = spread_terms(terms, rims)
    total = scatter(land(table, global_blocks, everything))
    gradient = wacc + total.astype(jnp.float32)
    gradient = gradient.at[:, 0].add(edges[:, 0].astype(jnp.float32))
    gradient = gradient.at[:, BLK_DEV - 1].add(edges[:, 1].astype(jnp.float32))
    gradient = gradient.astype(jnp.bfloat16)
    return (
        attended.reshape(row_count, features),
        query_grad.reshape(row_count, features),
        gradient[0].reshape(row_count, features),
        gradient[1].reshape(row_count, features),
    )


def solution(mesh):
    in_specs = (
        P("seq", "head"),
        P("seq", "head"),
        P("seq", "head"),
        P("seq", "head"),
        P("head", None, None),
        P(),
    )
    out_specs = (P("seq", "head"), P("seq", "head"), P("seq", "head"), P("seq", "head"))
    return jax.shard_map(
        per_device, mesh=mesh, in_specs=in_specs, out_specs=out_specs, check_vma=False
    )
```

```python
import math

import jax
import jax.numpy as jnp
from jax import lax
from jax.experimental import pallas as pl
from jax.experimental.pallas import tpu as pltpu
from jax.sharding import PartitionSpec as P

HEAD_DIM = 128
BLK = 64
NZ = 8
NX = 4
NC = 2
NSEQ = NZ * NX * NC
BLK_DEV = 4
REQ = 12
SLOTS = 2 * REQ + 2
ENTRIES = NX * SLOTS
PARTS = 4
PART = 128
VMEM_LIMIT = 56 * 1024 * 1024


def seq_of(z, x, c):
    return (lax.rem(z + NZ, NZ) * NX + lax.rem(x + NX, NX)) * NC + c


def place():
    me = lax.axis_index("seq")
    z = me // (NX * NC)
    x = lax.rem(me // NC, NX)
    c = lax.rem(me, NC)
    return me, z, x, c


def remote(src, dst, send_sem, recv_sem, target):
    return pltpu.make_async_remote_copy(
        src_ref=src,
        dst_ref=dst,
        send_sem=send_sem,
        recv_sem=recv_sem,
        device_id={"seq": target},
        device_id_type=pl.DeviceIdType.MESH,
    )


def greet(partners):
    barrier = pltpu.get_barrier_semaphore()
    for partner in partners:
        pl.semaphore_signal(
            barrier, inc=1, device_id={"seq": partner}, device_id_type=pl.DeviceIdType.MESH
        )
    pl.semaphore_wait(barrier, len(partners))


def block_place(block):
    return lax.rem(lax.div(block, 8), NX), lax.div(block, 32) * 8 + lax.rem(block, 8)


Z_LAST = {(0, 0): 4, (0, 1): 3, (1, 0): 3, (1, 1): 4}


def gather_kernel(
    table, k_ref, v_ref, out_ref, halo_ref,
    s1_out, s1_in, s2_out, s2_in, s3_out, s3_in, give,
    pair_sem, halo_send, halo_recv, z_send, z_recv, x_send, x_recv, give_sem, *ag,
):
    me, z, x, c = place()
    other = 1 - c
    sibling = seq_of(z, x, other)
    after = lax.rem(me + 1, NSEQ)
    before = lax.rem(me + NSEQ - 1, NSEQ)
    sigma = 1 - 2 * c
    far = seq_of(z, x + sigma, c)
    near = seq_of(z, x - sigma, c)
    zs = (seq_of(z + 1, x, c), seq_of(z - 1, x, c))
    greet((after, before, zs[0], zs[1], far, near))

    def lanes(p):
        return pl.ds(p * PART, PART)

    def pair_copy(src, p):
        return remote(
            src.at[:, :, lanes(p)], ag[p].at[pl.ds(z * 8 + c * 4, 4)],
            pair_sem.at[0, p], pair_sem.at[1, p], sibling,
        )

    @pl.when(c == 0)
    def _():
        for p in range(PARTS):
            pair_copy(v_ref, p).start()
        for p in range(PARTS):
            ag[p][pl.ds(z * 8, 4)] = k_ref[:, :, p * PART : (p + 1) * PART]

    @pl.when(c == 1)
    def _():
        for p in range(PARTS):
            pair_copy(k_ref, p).start()
        for p in range(PARTS):
            ag[p][pl.ds(z * 8 + 4, 4)] = v_ref[:, :, p * PART : (p + 1) * PART]

    def z_piece(p, direction, step, half):
        origin = lax.rem(z + NZ - (step - 1), NZ) if direction == 0 else lax.rem(z + step - 1, NZ)
        piece = ag[p].at[pl.ds(origin * 8 + half * 4, 4)]
        return remote(
            piece,
            piece,
            z_send.at[p, direction, step - 1, half],
            z_recv.at[p, direction, step - 1, half],
            zs[direction],
        )

    def z_start(p):
        for direction in range(2):
            z_piece(p, direction, 1, c).start()
        pair_copy(v_ref, p).wait()
        for direction in range(2):
            z_piece(p, direction, 1, other).start()

    def z_step(p, step):
        for half in range(2):
            for direction in range(2):
                if step <= Z_LAST[direction, half]:
                    z_piece(p, direction, step, half).wait_recv()
                    if step + 1 <= Z_LAST[direction, half]:
                        z_piece(p, direction, step + 1, half).start()

    def wanted(p, chip, slot):
        source, at = block_place(table[(z * NX + lax.rem(chip + NX, NX)) * SLOTS + slot])
        return source, ag[p][at]

    def x_copy(p, number):
        src, dst, target = (
            (s1_out, s1_in, far), (s2_out, s2_in, far), (s3_out, s3_in, near)
        )[number]
        return remote(
            src.at[p], dst.at[p], x_send.at[p, number], x_recv.at[p, number], target
        )

    def x_first(p):
        @pl.loop(0, SLOTS, unroll=2)
        def _(slot):
            s1_out[p, slot] = wanted(p, x + 2, slot)[1]

        x_copy(p, 0).start()

        @pl.loop(0, SLOTS, unroll=2)
        def _(slot):
            s3_out[p, slot] = wanted(p, x - sigma, slot)[1]

        x_copy(p, 2).start()

    def x_second(p):
        x_copy(p, 0).wait_recv()

        @pl.loop(0, SLOTS, unroll=2)
        def _(slot):
            source, mine = wanted(p, x + sigma, slot)
            s2_out[p, slot] = jnp.where(source == x, mine, s1_in[p, slot])

        x_copy(p, 1).start()

    here = lax.rem(x + sigma + NX, NX)

    def chosen(p, slot):
        source, mine = wanted(p, x, slot)
        return jnp.where(
            source == x, mine, jnp.where(source == here, s3_in[p, slot], s2_in[p, slot])
        )

    def handed(p):
        return remote(
            give.at[p], out_ref.at[c, :, :, lanes(p)], give_sem.at[0, p], give_sem.at[1, p],
            sibling,
        )

    def finish(p):
        x_copy(p, 2).wait_recv()
        x_copy(p, 1).wait_recv()
        columns = slice(p * PART, (p + 1) * PART)

        @pl.loop(0, REQ, unroll=2)
        def _(i):
            give[p, i] = chosen(p, other * (REQ + 2) + i)

        for i in range(2):
            value = chosen(p, REQ + i)
            give[p, REQ + i] = value
            out_ref[c, REQ + i, :, columns] = value
        handed(p).start()

        @pl.loop(0, REQ, unroll=2)
        def _(i):
            out_ref[c, i, :, columns] = chosen(p, c * (REQ + 2) + i)

    halos = []
    for number, ref in enumerate((k_ref, v_ref)):
        for side, (row, target) in enumerate(((BLK_DEV - 1, after), (0, before))):
            halos.append(
                remote(
                    ref.at[row], halo_ref.at[number, side], halo_send.at[number, side],
                    halo_recv.at[number, side], target,
                )
            )

    z_start(0)
    for step in range(1, 5):
        z_step(0, step)
    if PARTS > 1:
        z_start(1)
    x_first(0)
    for p in range(PARTS):
        more = p + 1 < PARTS
        if more:
            z_step(p + 1, 1)
            z_step(p + 1, 2)
        x_second(p)
        if more:
            z_step(p + 1, 3)
            z_step(p + 1, 4)
            if p + 2 < PARTS:
                z_start(p + 2)
            x_first(p + 1)
        else:
            for copy in halos:
                copy.start()
        finish(p)

    for copy in halos:
        copy.wait()
    for p in range(PARTS):
        for (direction, half), last in Z_LAST.items():
            for step in range(1, last + 1):
                z_piece(p, direction, step, half).wait_send()
        for number in range(3):
            x_copy(p, number).wait_send()
        handed(p).wait()


def gather(table, k, v):
    features = k.shape[-1]
    big = pltpu.VMEM((PARTS, SLOTS, BLK, PART), jnp.bfloat16)
    vmem = pl.BlockSpec(memory_space=pltpu.VMEM)
    smem = pl.BlockSpec(memory_space=pltpu.SMEM)
    dma = pltpu.SemaphoreType.DMA
    return pl.pallas_call(
        gather_kernel,
        out_shape=(
            jax.ShapeDtypeStruct((2, REQ + 2, BLK, features), jnp.bfloat16),
            jax.ShapeDtypeStruct((2, 2, BLK, features), jnp.bfloat16),
        ),
        in_specs=[smem, vmem, vmem],
        out_specs=(vmem, vmem),
        scratch_shapes=[
            big, big, big, big, big, big,
            pltpu.VMEM((PARTS, REQ + 2, BLK, PART), jnp.bfloat16),
            dma((2, PARTS)), dma((2, 2)), dma((2, 2)), dma((PARTS, 2, 4, 2)), dma((PARTS, 2, 4, 2)),
            dma((PARTS, 3)), dma((PARTS, 3)), dma((2, PARTS)),
        ]
        + [pltpu.VMEM((NZ * 8, BLK, PART), jnp.bfloat16)] * PARTS,
        compiler_params=pltpu.CompilerParams(
            collective_id=0, has_side_effects=True, vmem_limit_bytes=VMEM_LIMIT
        ),
        name="gather_blocks",
    )(table, k, v)


def nt(a, b):
    return lax.dot_general(a, b, (((1,), (1,)), ((), ())), preferred_element_type=jnp.float32)


def tn(a, b):
    return lax.dot_general(a, b, (((0,), (0,)), ((), ())), preferred_element_type=jnp.float32)


def nn(a, b):
    return lax.dot_general(a, b, (((1,), (0,)), ((), ())), preferred_element_type=jnp.float32)


def attend_kernel(
    q_ref, g_ref, k_ref, v_ref, halo_ref, slot_ref,
    att_ref, qg_ref, wacc_ref, term_ref, rim_ref, acc, gacc,
):
    me = lax.axis_index("seq")
    features = q_ref.shape[-1]
    heads = features // HEAD_DIM
    scale = 1.0 / math.sqrt(HEAD_DIM)
    lane_head = lax.broadcasted_iota(jnp.int32, (BLK, features), 1) // HEAD_DIM
    acc[...] = jnp.zeros_like(acc)
    gacc[...] = jnp.zeros_like(gacc)

    def spread(rows):
        zero = jnp.zeros_like(rows)
        return jnp.concatenate(
            [jnp.where(lane_head == h, rows, zero) for h in range(heads)], axis=0
        )

    def diagonal(full):
        return jnp.concatenate(
            [
                full[h * BLK : (h + 1) * BLK, h * HEAD_DIM : (h + 1) * HEAD_DIM]
                for h in range(heads)
            ],
            axis=1,
        )

    for b in range(BLK_DEV):
        def listed(number, own):
            window = [
                halo_ref[number, 0] if b == 0 else own[b - 1],
                own[b],
                halo_ref[number, 1] if b == BLK_DEV - 1 else own[b + 1],
            ]
            extra = [slot_ref[number, REQ], slot_ref[number, REQ + 1]]
            random = [slot_ref[number, 3 * b + i] for i in range(3)]
            return jnp.concatenate(window + extra + random, axis=0)

        keys = listed(0, k_ref)
        values = listed(1, v_ref)
        query = spread(q_ref[b])
        grad = spread(g_ref[b])
        scores = nt(keys, query) * scale
        if b == 0:
            scores = jnp.concatenate(
                [jnp.where(me == 0, -jnp.inf, scores[:BLK]), scores[BLK:]], axis=0
            )
        if b == BLK_DEV - 1:
            scores = jnp.concatenate(
                [
                    scores[: 2 * BLK],
                    jnp.where(me == NSEQ - 1, -jnp.inf, scores[2 * BLK : 3 * BLK]),
                    scores[3 * BLK :],
                ],
                axis=0,
            )
        row_max = jnp.max(scores, axis=0, keepdims=True)
        raw = jnp.exp(scores - row_max)
        weights = raw * (1.0 / jnp.sum(raw, axis=0, keepdims=True))
        weights_b = weights.astype(jnp.bfloat16)
        weight_grads = nt(values, grad)
        row_dot = jnp.sum(weights_b.astype(jnp.float32) * weight_grads, axis=0, keepdims=True)
        score_grads = (weights * (weight_grads - row_dot) * scale).astype(jnp.bfloat16)
        att_ref[b] = diagonal(tn(weights_b, values)).astype(jnp.bfloat16)
        qg_ref[b] = diagonal(tn(score_grads, keys)).astype(jnp.bfloat16)
        for number, terms in enumerate((nn(score_grads, query), nn(weights_b, grad))):
            for i in range(3):
                acc[number, b + i] += terms[i * BLK : (i + 1) * BLK]
            for i in range(2):
                gacc[number, i] += terms[(3 + i) * BLK : (4 + i) * BLK]
            for i in range(3):
                term_ref[number, 3 * b + i] = terms[(5 + i) * BLK : (6 + i) * BLK].astype(
                    jnp.bfloat16
                )
    for number in range(2):
        for i in range(2):
            term_ref[number, REQ + i] = gacc[number, i].astype(jnp.bfloat16)
        rim_ref[number, 0] = acc[number, 0].astype(jnp.bfloat16)
        rim_ref[number, 1] = acc[number, BLK_DEV + 1].astype(jnp.bfloat16)
        for i in range(BLK_DEV):
            wacc_ref[number, i] = acc[number, i + 1]


def attend(q, g, k, v, halo, slots):
    features = q.shape[-1]
    vmem = pl.BlockSpec(memory_space=pltpu.VMEM)
    own = jax.ShapeDtypeStruct((BLK_DEV, BLK, features), jnp.bfloat16)
    return pl.pallas_call(
        attend_kernel,
        out_shape=(
            own,
            own,
            jax.ShapeDtypeStruct((2, BLK_DEV, BLK, features), jnp.float32),
            jax.ShapeDtypeStruct((2, REQ + 2, BLK, features), jnp.bfloat16),
            jax.ShapeDtypeStruct((2, 2, BLK, features), jnp.bfloat16),
        ),
        in_specs=[vmem] * 6,
        out_specs=(vmem,) * 5,
        scratch_shapes=[
            pltpu.VMEM((2, BLK_DEV + 2, BLK, features), jnp.float32),
            pltpu.VMEM((2, 2, BLK, features), jnp.float32),
        ],
        compiler_params=pltpu.CompilerParams(vmem_limit_bytes=VMEM_LIMIT),
        name="attend_blocks",
    )(q, g, k, v, halo, slots)


def plan_kernel(table, prev_ref, last_ref):
    me, z, x, c = place()

    @pl.loop(0, NZ * 8)
    def _(at):
        last_ref[at] = ENTRIES

    @pl.loop(0, ENTRIES)
    def _(n):
        source, at = block_place(table[z * ENTRIES + n])
        prev_ref[n] = ENTRIES

        @pl.when(source == x)
        def _():
            prev_ref[n] = last_ref[at]
            last_ref[at] = n


def plan(table):
    smem = pl.BlockSpec(memory_space=pltpu.SMEM)
    return pl.pallas_call(
        plan_kernel,
        out_shape=(
            jax.ShapeDtypeStruct((ENTRIES,), jnp.int32),
            jax.ShapeDtypeStruct((NZ * 8,), jnp.int32),
        ),
        in_specs=[smem],
        out_specs=(smem, smem),
        name="plan_sums",
    )(table)


def back_kernel(
    prev, last, term_ref, rim_ref, out_ref, edge_ref,
    theirs, everything, chain, landed, send_buf, recv_buf, give,
    pair_sem, rim_send, rim_recv, x_send, x_recv, z_send, z_recv, give_sem,
):
    me, z, x, c = place()
    other = 1 - c
    sibling = seq_of(z, x, other)
    after = lax.rem(me + 1, NSEQ)
    before = lax.rem(me + NSEQ - 1, NSEQ)
    sigma = 1 - 2 * c
    xs = (seq_of(z, x + sigma, c), seq_of(z, x - sigma, c))
    zs = (seq_of(z + 1, x, c), seq_of(z - 1, x, c))
    greet((after, before, xs[0], xs[1], zs[0], zs[1]))

    def lanes(p):
        return pl.ds(p * PART, PART)

    def pair(p):
        return remote(
            term_ref.at[other, :, :, lanes(p)], theirs.at[p], pair_sem.at[0, p],
            pair_sem.at[1, p], sibling,
        )

    for p in range(PARTS):
        pair(p).start()

    def own(p, chip):
        base = lax.rem(chip + NX, NX) * SLOTS
        return everything.at[p, pl.ds(base + c * (REQ + 2), REQ)]

    def rest(p, chip):
        base = lax.rem(chip + NX, NX) * SLOTS
        return everything.at[p, pl.ds(base + other * REQ, REQ + 2)]

    def send(p, number, chip, which):
        ref = (own, rest)[which](p, chip)
        return remote(
            ref, ref, x_send.at[p, number, which], x_recv.at[p, number, which],
            xs[(0, 1, 0)[number]],
        )

    def x_first(p):
        columns = slice(p * PART, (p + 1) * PART)
        base = x * SLOTS

        @pl.loop(0, REQ, unroll=2)
        def _(i):
            everything[p, base + c * (REQ + 2) + i] = term_ref[c, i, :, columns]

        for number in range(2):
            send(p, number, x, 0).start()
        pair(p).wait_recv()

        @pl.loop(0, REQ, unroll=2)
        def _(i):
            everything[p, base + other * (REQ + 2) + i] = theirs[p, i]

        for i in range(2):
            total = term_ref[c, REQ + i, :, columns].astype(jnp.float32) + theirs[
                p, REQ + i
            ].astype(jnp.float32)
            everything[p, base + REQ + i] = total.astype(jnp.bfloat16)
        for number in range(2):
            send(p, number, x, 1).start()

    def x_second(p):
        for which in range(2):
            send(p, 0, x - sigma, which).wait_recv()
            send(p, 2, x - sigma, which).start()

    def x_wait(p, number):
        for which in range(2):
            send(p, number, x, which).wait_recv()

    chain[ENTRIES] = jnp.zeros((BLK, PART), jnp.float32)

    def land(p):
        @pl.loop(0, ENTRIES, unroll=4)
        def _(n):
            chain[n] = everything[p, n].astype(jnp.float32) + chain[prev[n]]

        @pl.loop(0, NZ * 8, unroll=4)
        def _(at):
            landed[p, at] = chain[last[at]]

    def piece(p, direction, distance, half):
        return remote(
            send_buf.at[p, direction, distance - 1, half],
            recv_buf.at[p, direction, distance - 1, half],
            z_send.at[p, direction, distance - 1, half],
            z_recv.at[p, direction, distance - 1, half],
            zs[direction],
        )

    def z_step(p, distance):
        for half in range(2):
            for direction in range(2):
                if distance > Z_LAST[direction, half]:
                    continue
                target = lax.rem(z + (distance if direction == 0 else NZ - distance), NZ)
                first = target * 8 + half * 4
                waits = distance < Z_LAST[direction, half]
                if waits:
                    piece(p, direction, distance + 1, half).wait_recv()
                for i in range(BLK_DEV):
                    total = landed[p, first + i]
                    if waits:
                        total += recv_buf[p, direction, distance, half, i].astype(jnp.float32)
                    send_buf[p, direction, distance - 1, half, i] = total.astype(jnp.bfloat16)
                piece(p, direction, distance, half).start()

    def handed(p):
        return remote(
            give.at[p], out_ref.at[c, :, :, lanes(p)], give_sem.at[0, p], give_sem.at[1, p],
            sibling,
        )

    def finish(p):
        columns = slice(p * PART, (p + 1) * PART)
        for half in range(2):
            for direction in range(2):
                piece(p, direction, 1, half).wait_recv()

        def finished(half, i):
            total = landed[p, z * 8 + half * 4 + i]
            for direction in range(2):
                total += recv_buf[p, direction, 0, half, i].astype(jnp.float32)
            return total.astype(jnp.bfloat16)

        for i in range(BLK_DEV):
            give[p, i] = finished(other, i)
        handed(p).start()
        for i in range(BLK_DEV):
            out_ref[c, i, :, columns] = finished(c, i)

    edges = []
    for number in range(2):
        for side, target in enumerate((after, before)):
            edges.append(
                remote(
                    rim_ref.at[number, 1 - side], edge_ref.at[number, side],
                    rim_send.at[number, side], rim_recv.at[number, side], target,
                )
            )

    x_first(0)
    for p in range(PARTS):
        x_second(p)
        if p + 1 < PARTS:
            x_first(p + 1)
        else:
            for copy in edges:
                copy.start()
        if p:
            z_step(p - 1, 3)
        x_wait(p, 1)
        if p:
            z_step(p - 1, 2)
        x_wait(p, 2)
        if p:
            z_step(p - 1, 1)
        land(p)
        z_step(p, 4)
        if p:
            finish(p - 1)
    for distance in (3, 2, 1):
        z_step(PARTS - 1, distance)
    finish(PARTS - 1)

    for copy in edges:
        copy.wait()
    for p in range(PARTS):
        pair(p).wait_send()
        for number in range(3):
            for which in range(2):
                send(p, number, x, which).wait_send()
        for (direction, half), most in Z_LAST.items():
            for distance in range(1, most + 1):
                piece(p, direction, distance, half).wait_send()
        handed(p).wait()


def send_back(prev, last, terms, rims):
    features = terms.shape[-1]
    vmem = pl.BlockSpec(memory_space=pltpu.VMEM)
    smem = pl.BlockSpec(memory_space=pltpu.SMEM)
    dma = pltpu.SemaphoreType.DMA
    ring = pltpu.VMEM((PARTS, 2, 4, 2, BLK_DEV, BLK, PART), jnp.bfloat16)
    return pl.pallas_call(
        back_kernel,
        out_shape=(
            jax.ShapeDtypeStruct((2, BLK_DEV, BLK, features), jnp.bfloat16),
            jax.ShapeDtypeStruct((2, 2, BLK, features), jnp.bfloat16),
        ),
        in_specs=[smem, smem, vmem, vmem],
        out_specs=(vmem, vmem),
        scratch_shapes=[
            pltpu.VMEM((PARTS, REQ + 2, BLK, PART), jnp.bfloat16),
            pltpu.VMEM((PARTS, ENTRIES, BLK, PART), jnp.bfloat16),
            pltpu.VMEM((ENTRIES + 1, BLK, PART), jnp.float32),
            pltpu.VMEM((PARTS, NZ * 8, BLK, PART), jnp.float32),
            ring, ring,
            pltpu.VMEM((PARTS, BLK_DEV, BLK, PART), jnp.bfloat16),
            dma((2, PARTS)), dma((2, 2)), dma((2, 2)), dma((PARTS, 3, 2)), dma((PARTS, 3, 2)),
            dma((PARTS, 2, 4, 2)), dma((PARTS, 2, 4, 2)), dma((2, PARTS)),
        ],
        compiler_params=pltpu.CompilerParams(
            collective_id=1, has_side_effects=True, vmem_limit_bytes=VMEM_LIMIT
        ),
        name="send_back",
    )(prev, last, terms, rims)


def per_device(queries, key_rows, value_rows, out_grad, random_blocks, global_blocks):
    row_count, features = queries.shape
    blocks = (BLK_DEV, BLK, features)
    lists = random_blocks.reshape(NZ * NX, NC, REQ)
    shared = jnp.broadcast_to(global_blocks[None], (NZ * NX, 2))
    table = jnp.concatenate([lists[:, 0], shared, lists[:, 1]], axis=1).reshape(-1)
    k = key_rows.reshape(blocks)
    v = value_rows.reshape(blocks)
    prev, last = plan(table)
    slots, halo = gather(table, k, v)
    attended, query_grad, wacc, terms, rims = attend(
        queries.reshape(blocks), out_grad.reshape(blocks), k, v, halo, slots
    )
    total, edges = send_back(prev, last, terms, rims)
    gradient = wacc + total.astype(jnp.float32)
    gradient = gradient.at[:, 0].add(edges[:, 0].astype(jnp.float32))
    gradient = gradient.at[:, BLK_DEV - 1].add(edges[:, 1].astype(jnp.float32))
    gradient = gradient.astype(jnp.bfloat16)
    return (
        attended.reshape(row_count, features),
        query_grad.reshape(row_count, features),
        gradient[0].reshape(row_count, features),
        gradient[1].reshape(row_count, features),
    )


def solution(mesh):
    in_specs = (
        P("seq", "head"),
        P("seq", "head"),
        P("seq", "head"),
        P("seq", "head"),
        P("head", None, None),
        P(),
    )
    out_specs = (P("seq", "head"), P("seq", "head"), P("seq", "head"), P("seq", "head"))
    return jax.shard_map(
        per_device, mesh=mesh, in_specs=in_specs, out_specs=out_specs, check_vma=False
    )
```

```python
import math

import jax
import jax.numpy as jnp
from jax import lax
from jax.experimental import pallas as pl
from jax.experimental.pallas import tpu as pltpu
from jax.sharding import PartitionSpec as P

HEAD_DIM = 128
BLK = 64
NZ = 8
NX = 4
NC = 2
NSEQ = NZ * NX * NC
BLK_DEV = 4
REQ = 12
SLOTS = 2 * REQ + 2
ENTRIES = NX * SLOTS
PARTS = 4
PART = 128
ROWS = BLK // 2
VMEM_LIMIT = 56 * 1024 * 1024


def seq_of(z, x, c):
    return (lax.rem(z + NZ, NZ) * NX + lax.rem(x + NX, NX)) * NC + c


def place():
    me = lax.axis_index("seq")
    z = me // (NX * NC)
    x = lax.rem(me // NC, NX)
    c = lax.rem(me, NC)
    return me, z, x, c


def remote(src, dst, send_sem, recv_sem, target):
    return pltpu.make_async_remote_copy(
        src_ref=src,
        dst_ref=dst,
        send_sem=send_sem,
        recv_sem=recv_sem,
        device_id={"seq": target},
        device_id_type=pl.DeviceIdType.MESH,
    )


def greet(partners):
    barrier = pltpu.get_barrier_semaphore()
    for partner in partners:
        pl.semaphore_signal(
            barrier, inc=1, device_id={"seq": partner}, device_id_type=pl.DeviceIdType.MESH
        )
    pl.semaphore_wait(barrier, len(partners))


def block_place(block):
    return lax.rem(lax.div(block, 8), NX), lax.div(block, 32) * 8 + lax.rem(block, 8)


Z_LAST = {(0, 0): 4, (0, 1): 3, (1, 0): 3, (1, 1): 4}


def gather_kernel(
    table, k_ref, v_ref, out_ref, halo_ref,
    s1_out, s1_in, s2_out, s2_in, s3_out, s3_in, give,
    pair_sem, halo_send, halo_recv, z_send, z_recv, x_send, x_recv, give_sem, *ag,
):
    me, z, x, c = place()
    other = 1 - c
    sibling = seq_of(z, x, other)
    after = lax.rem(me + 1, NSEQ)
    before = lax.rem(me + NSEQ - 1, NSEQ)
    xs = (seq_of(z, x + 1, c), seq_of(z, x - 1, c))
    zs = (seq_of(z + 1, x, c), seq_of(z - 1, x, c))
    greet((after, before, zs[0], zs[1], xs[0], xs[1]))

    def lanes(p):
        return pl.ds(p * PART, PART)

    def pair_copy(src, p):
        return remote(
            src.at[:, :, lanes(p)], ag[p].at[pl.ds(z * 8 + c * 4, 4)],
            pair_sem.at[0, p], pair_sem.at[1, p], sibling,
        )

    @pl.when(c == 0)
    def _():
        for p in range(PARTS):
            pair_copy(v_ref, p).start()
        for p in range(PARTS):
            ag[p][pl.ds(z * 8, 4)] = k_ref[:, :, p * PART : (p + 1) * PART]

    @pl.when(c == 1)
    def _():
        for p in range(PARTS):
            pair_copy(k_ref, p).start()
        for p in range(PARTS):
            ag[p][pl.ds(z * 8 + 4, 4)] = v_ref[:, :, p * PART : (p + 1) * PART]

    def z_piece(p, direction, step, half):
        origin = lax.rem(z + NZ - (step - 1), NZ) if direction == 0 else lax.rem(z + step - 1, NZ)
        piece = ag[p].at[pl.ds(origin * 8 + half * 4, 4)]
        return remote(
            piece,
            piece,
            z_send.at[p, direction, step - 1, half],
            z_recv.at[p, direction, step - 1, half],
            zs[direction],
        )

    def z_start(p):
        for direction in range(2):
            z_piece(p, direction, 1, c).start()
        pair_copy(v_ref, p).wait()
        for direction in range(2):
            z_piece(p, direction, 1, other).start()

    def z_step(p, step):
        for half in range(2):
            for direction in range(2):
                if step <= Z_LAST[direction, half]:
                    z_piece(p, direction, step, half).wait_recv()
                    if step + 1 <= Z_LAST[direction, half]:
                        z_piece(p, direction, step + 1, half).start()

    def wanted(p, chip, slot):
        source, at = block_place(table[(z * NX + lax.rem(chip + NX, NX)) * SLOTS + slot])
        return source, ag[p][at]

    def x_copy(p, number, g):
        src, dst, way = ((s1_out, s1_in, g), (s2_out, s2_in, g), (s3_out, s3_in, 1 - g))[number]
        return remote(
            src.at[p, g], dst.at[p, g], x_send.at[p, number, g], x_recv.at[p, number, g], xs[way]
        )

    def x_first(p):
        @pl.loop(0, SLOTS, unroll=2)
        def _(slot):
            mine = wanted(p, x + 2, slot)[1]
            s1_out[p, 0, slot] = mine[:ROWS]
            s1_out[p, 1, slot] = mine[ROWS:]

        for g in range(2):
            x_copy(p, 0, g).start()

        @pl.loop(0, SLOTS, unroll=2)
        def _(slot):
            s3_out[p, 0, slot] = wanted(p, x - 1, slot)[1][:ROWS]
            s3_out[p, 1, slot] = wanted(p, x + 1, slot)[1][ROWS:]

        for g in range(2):
            x_copy(p, 2, g).start()

    def x_second(p):
        for g in range(2):
            x_copy(p, 0, g).wait_recv()

        @pl.loop(0, SLOTS, unroll=2)
        def _(slot):
            source, mine = wanted(p, x + 1, slot)
            s2_out[p, 0, slot] = jnp.where(source == x, mine[:ROWS], s1_in[p, 0, slot])
            source, mine = wanted(p, x - 1, slot)
            s2_out[p, 1, slot] = jnp.where(source == x, mine[ROWS:], s1_in[p, 1, slot])

        for g in range(2):
            x_copy(p, 1, g).start()

    here = (lax.rem(x + 1, NX), lax.rem(x + NX - 1, NX))

    def chosen(p, slot):
        source, mine = wanted(p, x, slot)
        passed = [
            jnp.where(source == here[g], s3_in[p, g, slot], s2_in[p, g, slot]) for g in range(2)
        ]
        return jnp.where(source == x, mine, jnp.concatenate(passed, axis=0))

    def handed(p):
        return remote(
            give.at[p], out_ref.at[c, :, :, lanes(p)], give_sem.at[0, p], give_sem.at[1, p],
            sibling,
        )

    def finish(p):
        for number in (2, 1):
            for g in range(2):
                x_copy(p, number, g).wait_recv()
        columns = slice(p * PART, (p + 1) * PART)

        @pl.loop(0, REQ, unroll=2)
        def _(i):
            give[p, i] = chosen(p, other * (REQ + 2) + i)

        for i in range(2):
            value = chosen(p, REQ + i)
            give[p, REQ + i] = value
            out_ref[c, REQ + i, :, columns] = value
        handed(p).start()

        @pl.loop(0, REQ, unroll=2)
        def _(i):
            out_ref[c, i, :, columns] = chosen(p, c * (REQ + 2) + i)

    halos = []
    for number, ref in enumerate((k_ref, v_ref)):
        for side, (row, target) in enumerate(((BLK_DEV - 1, after), (0, before))):
            halos.append(
                remote(
                    ref.at[row], halo_ref.at[number, side], halo_send.at[number, side],
                    halo_recv.at[number, side], target,
                )
            )

    z_start(0)
    for step in range(1, 5):
        z_step(0, step)
    if PARTS > 1:
        z_start(1)
    x_first(0)
    for p in range(PARTS):
        more = p + 1 < PARTS
        if more:
            z_step(p + 1, 1)
            z_step(p + 1, 2)
        x_second(p)
        if more:
            z_step(p + 1, 3)
            z_step(p + 1, 4)
            if p + 2 < PARTS:
                z_start(p + 2)
            x_first(p + 1)
        else:
            for copy in halos:
                copy.start()
        finish(p)

    for copy in halos:
        copy.wait()
    for p in range(PARTS):
        for (direction, half), last in Z_LAST.items():
            for step in range(1, last + 1):
                z_piece(p, direction, step, half).wait_send()
        for number in range(3):
            for g in range(2):
                x_copy(p, number, g).wait_send()
        handed(p).wait()


def gather(table, k, v):
    features = k.shape[-1]
    big = pltpu.VMEM((PARTS, 2, SLOTS, ROWS, PART), jnp.bfloat16)
    vmem = pl.BlockSpec(memory_space=pltpu.VMEM)
    smem = pl.BlockSpec(memory_space=pltpu.SMEM)
    dma = pltpu.SemaphoreType.DMA
    return pl.pallas_call(
        gather_kernel,
        out_shape=(
            jax.ShapeDtypeStruct((2, REQ + 2, BLK, features), jnp.bfloat16),
            jax.ShapeDtypeStruct((2, 2, BLK, features), jnp.bfloat16),
        ),
        in_specs=[smem, vmem, vmem],
        out_specs=(vmem, vmem),
        scratch_shapes=[
            big, big, big, big, big, big,
            pltpu.VMEM((PARTS, REQ + 2, BLK, PART), jnp.bfloat16),
            dma((2, PARTS)), dma((2, 2)), dma((2, 2)), dma((PARTS, 2, 4, 2)), dma((PARTS, 2, 4, 2)),
            dma((PARTS, 3, 2)), dma((PARTS, 3, 2)), dma((2, PARTS)),
        ]
        + [pltpu.VMEM((NZ * 8, BLK, PART), jnp.bfloat16)] * PARTS,
        compiler_params=pltpu.CompilerParams(
            collective_id=0, has_side_effects=True, vmem_limit_bytes=VMEM_LIMIT
        ),
        name="gather_blocks",
    )(table, k, v)


def nt(a, b):
    return lax.dot_general(a, b, (((1,), (1,)), ((), ())), preferred_element_type=jnp.float32)


def tn(a, b):
    return lax.dot_general(a, b, (((0,), (0,)), ((), ())), preferred_element_type=jnp.float32)


def nn(a, b):
    return lax.dot_general(a, b, (((1,), (0,)), ((), ())), preferred_element_type=jnp.float32)


def attend_kernel(
    q_ref, g_ref, k_ref, v_ref, halo_ref, slot_ref,
    att_ref, qg_ref, wacc_ref, term_ref, rim_ref, acc, gacc,
):
    me = lax.axis_index("seq")
    features = q_ref.shape[-1]
    heads = features // HEAD_DIM
    scale = 1.0 / math.sqrt(HEAD_DIM)
    lane_head = lax.broadcasted_iota(jnp.int32, (BLK, features), 1) // HEAD_DIM
    acc[...] = jnp.zeros_like(acc)
    gacc[...] = jnp.zeros_like(gacc)

    def spread(rows):
        zero = jnp.zeros_like(rows)
        return jnp.concatenate(
            [jnp.where(lane_head == h, rows, zero) for h in range(heads)], axis=0
        )

    def diagonal(full):
        return jnp.concatenate(
            [
                full[h * BLK : (h + 1) * BLK, h * HEAD_DIM : (h + 1) * HEAD_DIM]
                for h in range(heads)
            ],
            axis=1,
        )

    for b in range(BLK_DEV):
        def listed(number, own):
            window = [
                halo_ref[number, 0] if b == 0 else own[b - 1],
                own[b],
                halo_ref[number, 1] if b == BLK_DEV - 1 else own[b + 1],
            ]
            extra = [slot_ref[number, REQ], slot_ref[number, REQ + 1]]
            random = [slot_ref[number, 3 * b + i] for i in range(3)]
            return jnp.concatenate(window + extra + random, axis=0)

        keys = listed(0, k_ref)
        values = listed(1, v_ref)
        query = spread(q_ref[b])
        grad = spread(g_ref[b])
        scores = nt(keys, query) * scale
        if b == 0:
            scores = jnp.concatenate(
                [jnp.where(me == 0, -jnp.inf, scores[:BLK]), scores[BLK:]], axis=0
            )
        if b == BLK_DEV - 1:
            scores = jnp.concatenate(
                [
                    scores[: 2 * BLK],
                    jnp.where(me == NSEQ - 1, -jnp.inf, scores[2 * BLK : 3 * BLK]),
                    scores[3 * BLK :],
                ],
                axis=0,
            )
        row_max = jnp.max(scores, axis=0, keepdims=True)
        raw = jnp.exp(scores - row_max)
        weights = raw * (1.0 / jnp.sum(raw, axis=0, keepdims=True))
        weights_b = weights.astype(jnp.bfloat16)
        weight_grads = nt(values, grad)
        row_dot = jnp.sum(weights_b.astype(jnp.float32) * weight_grads, axis=0, keepdims=True)
        score_grads = (weights * (weight_grads - row_dot) * scale).astype(jnp.bfloat16)
        att_ref[b] = diagonal(tn(weights_b, values)).astype(jnp.bfloat16)
        qg_ref[b] = diagonal(tn(score_grads, keys)).astype(jnp.bfloat16)
        for number, terms in enumerate((nn(score_grads, query), nn(weights_b, grad))):
            for i in range(3):
                acc[number, b + i] += terms[i * BLK : (i + 1) * BLK]
            for i in range(2):
                gacc[number, i] += terms[(3 + i) * BLK : (4 + i) * BLK]
            for i in range(3):
                term_ref[number, 3 * b + i] = terms[(5 + i) * BLK : (6 + i) * BLK].astype(
                    jnp.bfloat16
                )
    for number in range(2):
        for i in range(2):
            term_ref[number, REQ + i] = gacc[number, i].astype(jnp.bfloat16)
        rim_ref[number, 0] = acc[number, 0].astype(jnp.bfloat16)
        rim_ref[number, 1] = acc[number, BLK_DEV + 1].astype(jnp.bfloat16)
        for i in range(BLK_DEV):
            wacc_ref[number, i] = acc[number, i + 1]


def attend(q, g, k, v, halo, slots):
    features = q.shape[-1]
    vmem = pl.BlockSpec(memory_space=pltpu.VMEM)
    own = jax.ShapeDtypeStruct((BLK_DEV, BLK, features), jnp.bfloat16)
    return pl.pallas_call(
        attend_kernel,
        out_shape=(
            own,
            own,
            jax.ShapeDtypeStruct((2, BLK_DEV, BLK, features), jnp.float32),
            jax.ShapeDtypeStruct((2, REQ + 2, BLK, features), jnp.bfloat16),
            jax.ShapeDtypeStruct((2, 2, BLK, features), jnp.bfloat16),
        ),
        in_specs=[vmem] * 6,
        out_specs=(vmem,) * 5,
        scratch_shapes=[
            pltpu.VMEM((2, BLK_DEV + 2, BLK, features), jnp.float32),
            pltpu.VMEM((2, 2, BLK, features), jnp.float32),
        ],
        compiler_params=pltpu.CompilerParams(vmem_limit_bytes=VMEM_LIMIT),
        name="attend_blocks",
    )(q, g, k, v, halo, slots)


def plan_kernel(table, prev_ref, last_ref):
    me, z, x, c = place()

    @pl.loop(0, NZ * 8)
    def _(at):
        last_ref[at] = ENTRIES

    @pl.loop(0, ENTRIES)
    def _(n):
        source, at = block_place(table[z * ENTRIES + n])
        prev_ref[n] = ENTRIES

        @pl.when(source == x)
        def _():
            prev_ref[n] = last_ref[at]
            last_ref[at] = n


def plan(table):
    smem = pl.BlockSpec(memory_space=pltpu.SMEM)
    return pl.pallas_call(
        plan_kernel,
        out_shape=(
            jax.ShapeDtypeStruct((ENTRIES,), jnp.int32),
            jax.ShapeDtypeStruct((NZ * 8,), jnp.int32),
        ),
        in_specs=[smem],
        out_specs=(smem, smem),
        name="plan_sums",
    )(table)


def back_kernel(
    prev, last, term_ref, rim_ref, out_ref, edge_ref,
    theirs, everything, chain, landed, send_buf, recv_buf, give,
    pair_sem, rim_send, rim_recv, x_send, x_recv, z_send, z_recv, give_sem,
):
    me, z, x, c = place()
    other = 1 - c
    sibling = seq_of(z, x, other)
    after = lax.rem(me + 1, NSEQ)
    before = lax.rem(me + NSEQ - 1, NSEQ)
    xs = (seq_of(z, x + 1, c), seq_of(z, x - 1, c))
    zs = (seq_of(z + 1, x, c), seq_of(z - 1, x, c))
    greet((after, before, xs[0], xs[1], zs[0], zs[1]))

    def lanes(p):
        return pl.ds(p * PART, PART)

    def pair(p):
        return remote(
            term_ref.at[other, :, :, lanes(p)], theirs.at[p], pair_sem.at[0, p],
            pair_sem.at[1, p], sibling,
        )

    for p in range(PARTS):
        pair(p).start()

    def own(p, chip, g):
        base = lax.rem(chip + NX, NX) * SLOTS
        return everything.at[p, pl.ds(base + c * (REQ + 2), REQ), pl.ds(g * ROWS, ROWS)]

    def rest(p, chip, g):
        base = lax.rem(chip + NX, NX) * SLOTS
        return everything.at[p, pl.ds(base + other * REQ, REQ + 2), pl.ds(g * ROWS, ROWS)]

    def send(p, number, chip, which, g):
        ref = (own, rest)[which](p, chip, g)
        return remote(
            ref, ref, x_send.at[p, number, which, g], x_recv.at[p, number, which, g],
            xs[(g, 1 - g, g)[number]],
        )

    def x_first(p):
        columns = slice(p * PART, (p + 1) * PART)
        base = x * SLOTS

        @pl.loop(0, REQ, unroll=2)
        def _(i):
            everything[p, base + c * (REQ + 2) + i] = term_ref[c, i, :, columns]

        for number in range(2):
            for g in range(2):
                send(p, number, x, 0, g).start()
        pair(p).wait_recv()

        @pl.loop(0, REQ, unroll=2)
        def _(i):
            everything[p, base + other * (REQ + 2) + i] = theirs[p, i]

        for i in range(2):
            total = term_ref[c, REQ + i, :, columns].astype(jnp.float32) + theirs[
                p, REQ + i
            ].astype(jnp.float32)
            everything[p, base + REQ + i] = total.astype(jnp.bfloat16)
        for number in range(2):
            for g in range(2):
                send(p, number, x, 1, g).start()

    def x_second(p):
        for which in range(2):
            for g, behind in enumerate((x - 1, x + 1)):
                send(p, 0, behind, which, g).wait_recv()
                send(p, 2, behind, which, g).start()

    def x_wait(p, number):
        for which in range(2):
            for g in range(2):
                send(p, number, x, which, g).wait_recv()

    chain[ENTRIES] = jnp.zeros((BLK, PART), jnp.float32)

    def land(p):
        @pl.loop(0, ENTRIES, unroll=4)
        def _(n):
            chain[n] = everything[p, n].astype(jnp.float32) + chain[prev[n]]

        @pl.loop(0, NZ * 8, unroll=4)
        def _(at):
            landed[p, at] = chain[last[at]]

    def piece(p, direction, distance, half):
        return remote(
            send_buf.at[p, direction, distance - 1, half],
            recv_buf.at[p, direction, distance - 1, half],
            z_send.at[p, direction, distance - 1, half],
            z_recv.at[p, direction, distance - 1, half],
            zs[direction],
        )

    def z_step(p, distance):
        for half in range(2):
            for direction in range(2):
                if distance > Z_LAST[direction, half]:
                    continue
                target = lax.rem(z + (distance if direction == 0 else NZ - distance), NZ)
                first = target * 8 + half * 4
                waits = distance < Z_LAST[direction, half]
                if waits:
                    piece(p, direction, distance + 1, half).wait_recv()
                for i in range(BLK_DEV):
                    total = landed[p, first + i]
                    if waits:
                        total += recv_buf[p, direction, distance, half, i].astype(jnp.float32)
                    send_buf[p, direction, distance - 1, half, i] = total.astype(jnp.bfloat16)
                piece(p, direction, distance, half).start()

    def handed(p):
        return remote(
            give.at[p], out_ref.at[c, :, :, lanes(p)], give_sem.at[0, p], give_sem.at[1, p],
            sibling,
        )

    def finish(p):
        columns = slice(p * PART, (p + 1) * PART)
        for half in range(2):
            for direction in range(2):
                piece(p, direction, 1, half).wait_recv()

        def finished(half, i):
            total = landed[p, z * 8 + half * 4 + i]
            for direction in range(2):
                total += recv_buf[p, direction, 0, half, i].astype(jnp.float32)
            return total.astype(jnp.bfloat16)

        for i in range(BLK_DEV):
            give[p, i] = finished(other, i)
        handed(p).start()
        for i in range(BLK_DEV):
            out_ref[c, i, :, columns] = finished(c, i)

    edges = []
    for number in range(2):
        for side, target in enumerate((after, before)):
            edges.append(
                remote(
                    rim_ref.at[number, 1 - side], edge_ref.at[number, side],
                    rim_send.at[number, side], rim_recv.at[number, side], target,
                )
            )

    x_first(0)
    for p in range(PARTS):
        x_second(p)
        if p + 1 < PARTS:
            x_first(p + 1)
        else:
            for copy in edges:
                copy.start()
        if p:
            z_step(p - 1, 3)
        x_wait(p, 1)
        if p:
            z_step(p - 1, 2)
        x_wait(p, 2)
        if p:
            z_step(p - 1, 1)
        land(p)
        z_step(p, 4)
        if p:
            finish(p - 1)
    for distance in (3, 2, 1):
        z_step(PARTS - 1, distance)
    finish(PARTS - 1)

    for copy in edges:
        copy.wait()
    for p in range(PARTS):
        pair(p).wait_send()
        for number in range(3):
            for which in range(2):
                for g in range(2):
                    send(p, number, x, which, g).wait_send()
        for (direction, half), most in Z_LAST.items():
            for distance in range(1, most + 1):
                piece(p, direction, distance, half).wait_send()
        handed(p).wait()


def send_back(prev, last, terms, rims):
    features = terms.shape[-1]
    vmem = pl.BlockSpec(memory_space=pltpu.VMEM)
    smem = pl.BlockSpec(memory_space=pltpu.SMEM)
    dma = pltpu.SemaphoreType.DMA
    ring = pltpu.VMEM((PARTS, 2, 4, 2, BLK_DEV, BLK, PART), jnp.bfloat16)
    return pl.pallas_call(
        back_kernel,
        out_shape=(
            jax.ShapeDtypeStruct((2, BLK_DEV, BLK, features), jnp.bfloat16),
            jax.ShapeDtypeStruct((2, 2, BLK, features), jnp.bfloat16),
        ),
        in_specs=[smem, smem, vmem, vmem],
        out_specs=(vmem, vmem),
        scratch_shapes=[
            pltpu.VMEM((PARTS, REQ + 2, BLK, PART), jnp.bfloat16),
            pltpu.VMEM((PARTS, ENTRIES, BLK, PART), jnp.bfloat16),
            pltpu.VMEM((ENTRIES + 1, BLK, PART), jnp.float32),
            pltpu.VMEM((PARTS, NZ * 8, BLK, PART), jnp.float32),
            ring, ring,
            pltpu.VMEM((PARTS, BLK_DEV, BLK, PART), jnp.bfloat16),
            dma((2, PARTS)), dma((2, 2)), dma((2, 2)), dma((PARTS, 3, 2, 2)), dma((PARTS, 3, 2, 2)),
            dma((PARTS, 2, 4, 2)), dma((PARTS, 2, 4, 2)), dma((2, PARTS)),
        ],
        compiler_params=pltpu.CompilerParams(
            collective_id=1, has_side_effects=True, vmem_limit_bytes=VMEM_LIMIT
        ),
        name="send_back",
    )(prev, last, terms, rims)


def per_device(queries, key_rows, value_rows, out_grad, random_blocks, global_blocks):
    row_count, features = queries.shape
    blocks = (BLK_DEV, BLK, features)
    lists = random_blocks.reshape(NZ * NX, NC, REQ)
    shared = jnp.broadcast_to(global_blocks[None], (NZ * NX, 2))
    table = jnp.concatenate([lists[:, 0], shared, lists[:, 1]], axis=1).reshape(-1)
    k = key_rows.reshape(blocks)
    v = value_rows.reshape(blocks)
    prev, last = plan(table)
    slots, halo = gather(table, k, v)
    attended, query_grad, wacc, terms, rims = attend(
        queries.reshape(blocks), out_grad.reshape(blocks), k, v, halo, slots
    )
    total, edges = send_back(prev, last, terms, rims)
    gradient = wacc + total.astype(jnp.float32)
    gradient = gradient.at[:, 0].add(edges[:, 0].astype(jnp.float32))
    gradient = gradient.at[:, BLK_DEV - 1].add(edges[:, 1].astype(jnp.float32))
    gradient = gradient.astype(jnp.bfloat16)
    return (
        attended.reshape(row_count, features),
        query_grad.reshape(row_count, features),
        gradient[0].reshape(row_count, features),
        gradient[1].reshape(row_count, features),
    )


def solution(mesh):
    in_specs = (
        P("seq", "head"),
        P("seq", "head"),
        P("seq", "head"),
        P("seq", "head"),
        P("head", None, None),
        P(),
    )
    out_specs = (P("seq", "head"), P("seq", "head"), P("seq", "head"), P("seq", "head"))
    return jax.shard_map(
        per_device, mesh=mesh, in_specs=in_specs, out_specs=out_specs, check_vma=False
    )
```

```python
import math

import jax
import jax.numpy as jnp
from jax import lax
from jax.experimental import pallas as pl
from jax.experimental.pallas import tpu as pltpu
from jax.sharding import PartitionSpec as P

HEAD_DIM = 128
BLK = 64
NZ = 8
NX = 4
NC = 2
NSEQ = NZ * NX * NC
BLK_DEV = 4
REQ = 12
SLOTS = 2 * REQ + 2
ENTRIES = NX * SLOTS
PARTS = 4
PART = 128
ROWS = BLK // 2
CAP = 15
TERMS = SLOTS + 3 * CAP
VMEM_LIMIT = 56 * 1024 * 1024


def seq_of(z, x, c):
    return (lax.rem(z + NZ, NZ) * NX + lax.rem(x + NX, NX)) * NC + c


def place():
    me = lax.axis_index("seq")
    z = me // (NX * NC)
    x = lax.rem(me // NC, NX)
    c = lax.rem(me, NC)
    return me, z, x, c


def remote(src, dst, send_sem, recv_sem, target):
    return pltpu.make_async_remote_copy(
        src_ref=src,
        dst_ref=dst,
        send_sem=send_sem,
        recv_sem=recv_sem,
        device_id={"seq": target},
        device_id_type=pl.DeviceIdType.MESH,
    )


def greet(partners):
    barrier = pltpu.get_barrier_semaphore()
    for partner in partners:
        pl.semaphore_signal(
            barrier, inc=1, device_id={"seq": partner}, device_id_type=pl.DeviceIdType.MESH
        )
    pl.semaphore_wait(barrier, len(partners))


def block_place(block):
    return lax.rem(lax.div(block, 8), NX), lax.div(block, 32) * 8 + lax.rem(block, 8)


Z_LAST = {(0, 0): 4, (0, 1): 3, (1, 0): 3, (1, 1): 4}


def gather_kernel(
    table, k_ref, v_ref, out_ref, halo_ref,
    s1_out, s1_in, s2_out, s2_in, s3_out, s3_in, give,
    pair_sem, halo_send, halo_recv, z_send, z_recv, x_send, x_recv, give_sem, *ag,
):
    me, z, x, c = place()
    other = 1 - c
    sibling = seq_of(z, x, other)
    after = lax.rem(me + 1, NSEQ)
    before = lax.rem(me + NSEQ - 1, NSEQ)
    xs = (seq_of(z, x + 1, c), seq_of(z, x - 1, c))
    zs = (seq_of(z + 1, x, c), seq_of(z - 1, x, c))
    greet((after, before, zs[0], zs[1], xs[0], xs[1]))

    def lanes(p):
        return pl.ds(p * PART, PART)

    def pair_copy(src, p):
        return remote(
            src.at[:, :, lanes(p)], ag[p].at[pl.ds(z * 8 + c * 4, 4)],
            pair_sem.at[0, p], pair_sem.at[1, p], sibling,
        )

    @pl.when(c == 0)
    def _():
        for p in range(PARTS):
            pair_copy(v_ref, p).start()
        for p in range(PARTS):
            ag[p][pl.ds(z * 8, 4)] = k_ref[:, :, p * PART : (p + 1) * PART]

    @pl.when(c == 1)
    def _():
        for p in range(PARTS):
            pair_copy(k_ref, p).start()
        for p in range(PARTS):
            ag[p][pl.ds(z * 8 + 4, 4)] = v_ref[:, :, p * PART : (p + 1) * PART]

    def z_piece(p, direction, step, half):
        origin = lax.rem(z + NZ - (step - 1), NZ) if direction == 0 else lax.rem(z + step - 1, NZ)
        piece = ag[p].at[pl.ds(origin * 8 + half * 4, 4)]
        return remote(
            piece,
            piece,
            z_send.at[p, direction, step - 1, half],
            z_recv.at[p, direction, step - 1, half],
            zs[direction],
        )

    def z_start(p):
        for direction in range(2):
            z_piece(p, direction, 1, c).start()
        pair_copy(v_ref, p).wait()
        for direction in range(2):
            z_piece(p, direction, 1, other).start()

    def z_step(p, step):
        for half in range(2):
            for direction in range(2):
                if step <= Z_LAST[direction, half]:
                    z_piece(p, direction, step, half).wait_recv()
                    if step + 1 <= Z_LAST[direction, half]:
                        z_piece(p, direction, step + 1, half).start()

    def wanted(p, chip, slot):
        source, at = block_place(table[(z * NX + lax.rem(chip + NX, NX)) * SLOTS + slot])
        return source, ag[p][at]

    def x_copy(p, number, g):
        src, dst, way = ((s1_out, s1_in, g), (s2_out, s2_in, g), (s3_out, s3_in, 1 - g))[number]
        return remote(
            src.at[p, g], dst.at[p, g], x_send.at[p, number, g], x_recv.at[p, number, g], xs[way]
        )

    def x_first(p):
        @pl.loop(0, SLOTS, unroll=2)
        def _(slot):
            mine = wanted(p, x + 2, slot)[1]
            s1_out[p, 0, slot] = mine[:ROWS]
            s1_out[p, 1, slot] = mine[ROWS:]

        for g in range(2):
            x_copy(p, 0, g).start()

        @pl.loop(0, SLOTS, unroll=2)
        def _(slot):
            s3_out[p, 0, slot] = wanted(p, x - 1, slot)[1][:ROWS]
            s3_out[p, 1, slot] = wanted(p, x + 1, slot)[1][ROWS:]

        for g in range(2):
            x_copy(p, 2, g).start()

    def x_second(p):
        for g in range(2):
            x_copy(p, 0, g).wait_recv()

        @pl.loop(0, SLOTS, unroll=2)
        def _(slot):
            source, mine = wanted(p, x + 1, slot)
            s2_out[p, 0, slot] = jnp.where(source == x, mine[:ROWS], s1_in[p, 0, slot])
            source, mine = wanted(p, x - 1, slot)
            s2_out[p, 1, slot] = jnp.where(source == x, mine[ROWS:], s1_in[p, 1, slot])

        for g in range(2):
            x_copy(p, 1, g).start()

    here = (lax.rem(x + 1, NX), lax.rem(x + NX - 1, NX))

    def chosen(p, slot):
        source, mine = wanted(p, x, slot)
        passed = [
            jnp.where(source == here[g], s3_in[p, g, slot], s2_in[p, g, slot]) for g in range(2)
        ]
        return jnp.where(source == x, mine, jnp.concatenate(passed, axis=0))

    def handed(p):
        return remote(
            give.at[p], out_ref.at[c, :, :, lanes(p)], give_sem.at[0, p], give_sem.at[1, p],
            sibling,
        )

    def finish(p):
        for number in (2, 1):
            for g in range(2):
                x_copy(p, number, g).wait_recv()
        columns = slice(p * PART, (p + 1) * PART)

        @pl.loop(0, REQ, unroll=2)
        def _(i):
            give[p, i] = chosen(p, other * (REQ + 2) + i)

        for i in range(2):
            value = chosen(p, REQ + i)
            give[p, REQ + i] = value
            out_ref[c, REQ + i, :, columns] = value
        handed(p).start()

        @pl.loop(0, REQ, unroll=2)
        def _(i):
            out_ref[c, i, :, columns] = chosen(p, c * (REQ + 2) + i)

    halos = []
    for number, ref in enumerate((k_ref, v_ref)):
        for side, (row, target) in enumerate(((BLK_DEV - 1, after), (0, before))):
            halos.append(
                remote(
                    ref.at[row], halo_ref.at[number, side], halo_send.at[number, side],
                    halo_recv.at[number, side], target,
                )
            )

    z_start(0)
    for step in range(1, 5):
        z_step(0, step)
    if PARTS > 1:
        z_start(1)
    x_first(0)
    for p in range(PARTS):
        more = p + 1 < PARTS
        if more:
            z_step(p + 1, 1)
            z_step(p + 1, 2)
        x_second(p)
        if more:
            z_step(p + 1, 3)
            z_step(p + 1, 4)
            if p + 2 < PARTS:
                z_start(p + 2)
            x_first(p + 1)
        else:
            for copy in halos:
                copy.start()
        finish(p)

    for copy in halos:
        copy.wait()
    for p in range(PARTS):
        for (direction, half), last in Z_LAST.items():
            for step in range(1, last + 1):
                z_piece(p, direction, step, half).wait_send()
        for number in range(3):
            for g in range(2):
                x_copy(p, number, g).wait_send()
        handed(p).wait()


def gather(table, k, v):
    features = k.shape[-1]
    big = pltpu.VMEM((PARTS, 2, SLOTS, ROWS, PART), jnp.bfloat16)
    vmem = pl.BlockSpec(memory_space=pltpu.VMEM)
    smem = pl.BlockSpec(memory_space=pltpu.SMEM)
    dma = pltpu.SemaphoreType.DMA
    return pl.pallas_call(
        gather_kernel,
        out_shape=(
            jax.ShapeDtypeStruct((2, REQ + 2, BLK, features), jnp.bfloat16),
            jax.ShapeDtypeStruct((2, 2, BLK, features), jnp.bfloat16),
        ),
        in_specs=[smem, vmem, vmem],
        out_specs=(vmem, vmem),
        scratch_shapes=[
            big, big, big, big, big, big,
            pltpu.VMEM((PARTS, REQ + 2, BLK, PART), jnp.bfloat16),
            dma((2, PARTS)), dma((2, 2)), dma((2, 2)), dma((PARTS, 2, 4, 2)), dma((PARTS, 2, 4, 2)),
            dma((PARTS, 3, 2)), dma((PARTS, 3, 2)), dma((2, PARTS)),
        ]
        + [pltpu.VMEM((NZ * 8, BLK, PART), jnp.bfloat16)] * PARTS,
        compiler_params=pltpu.CompilerParams(
            collective_id=0, has_side_effects=True, vmem_limit_bytes=VMEM_LIMIT
        ),
        name="gather_blocks",
    )(table, k, v)


def nt(a, b):
    return lax.dot_general(a, b, (((1,), (1,)), ((), ())), preferred_element_type=jnp.float32)


def tn(a, b):
    return lax.dot_general(a, b, (((0,), (0,)), ((), ())), preferred_element_type=jnp.float32)


def nn(a, b):
    return lax.dot_general(a, b, (((1,), (0,)), ((), ())), preferred_element_type=jnp.float32)


def attend_kernel(
    q_ref, g_ref, k_ref, v_ref, halo_ref, slot_ref,
    att_ref, qg_ref, wacc_ref, term_ref, rim_ref, acc, gacc,
):
    me = lax.axis_index("seq")
    features = q_ref.shape[-1]
    heads = features // HEAD_DIM
    scale = 1.0 / math.sqrt(HEAD_DIM)
    lane_head = lax.broadcasted_iota(jnp.int32, (BLK, features), 1) // HEAD_DIM
    acc[...] = jnp.zeros_like(acc)
    gacc[...] = jnp.zeros_like(gacc)

    def spread(rows):
        zero = jnp.zeros_like(rows)
        return jnp.concatenate(
            [jnp.where(lane_head == h, rows, zero) for h in range(heads)], axis=0
        )

    def diagonal(full):
        return jnp.concatenate(
            [
                full[h * BLK : (h + 1) * BLK, h * HEAD_DIM : (h + 1) * HEAD_DIM]
                for h in range(heads)
            ],
            axis=1,
        )

    for b in range(BLK_DEV):
        def listed(number, own):
            window = [
                halo_ref[number, 0] if b == 0 else own[b - 1],
                own[b],
                halo_ref[number, 1] if b == BLK_DEV - 1 else own[b + 1],
            ]
            extra = [slot_ref[number, REQ], slot_ref[number, REQ + 1]]
            random = [slot_ref[number, 3 * b + i] for i in range(3)]
            return jnp.concatenate(window + extra + random, axis=0)

        keys = listed(0, k_ref)
        values = listed(1, v_ref)
        query = spread(q_ref[b])
        grad = spread(g_ref[b])
        scores = nt(keys, query) * scale
        if b == 0:
            scores = jnp.concatenate(
                [jnp.where(me == 0, -jnp.inf, scores[:BLK]), scores[BLK:]], axis=0
            )
        if b == BLK_DEV - 1:
            scores = jnp.concatenate(
                [
                    scores[: 2 * BLK],
                    jnp.where(me == NSEQ - 1, -jnp.inf, scores[2 * BLK : 3 * BLK]),
                    scores[3 * BLK :],
                ],
                axis=0,
            )
        row_max = jnp.max(scores, axis=0, keepdims=True)
        raw = jnp.exp(scores - row_max)
        weights = raw * (1.0 / jnp.sum(raw, axis=0, keepdims=True))
        weights_b = weights.astype(jnp.bfloat16)
        weight_grads = nt(values, grad)
        row_dot = jnp.sum(weights_b.astype(jnp.float32) * weight_grads, axis=0, keepdims=True)
        score_grads = (weights * (weight_grads - row_dot) * scale).astype(jnp.bfloat16)
        att_ref[b] = diagonal(tn(weights_b, values)).astype(jnp.bfloat16)
        qg_ref[b] = diagonal(tn(score_grads, keys)).astype(jnp.bfloat16)
        for number, terms in enumerate((nn(score_grads, query), nn(weights_b, grad))):
            for i in range(3):
                acc[number, b + i] += terms[i * BLK : (i + 1) * BLK]
            for i in range(2):
                gacc[number, i] += terms[(3 + i) * BLK : (4 + i) * BLK]
            for i in range(3):
                term_ref[number, 3 * b + i] = terms[(5 + i) * BLK : (6 + i) * BLK].astype(
                    jnp.bfloat16
                )
    for number in range(2):
        for i in range(2):
            term_ref[number, REQ + i] = gacc[number, i].astype(jnp.bfloat16)
        rim_ref[number, 0] = acc[number, 0].astype(jnp.bfloat16)
        rim_ref[number, 1] = acc[number, BLK_DEV + 1].astype(jnp.bfloat16)
        for i in range(BLK_DEV):
            wacc_ref[number, i] = acc[number, i + 1]


def attend(q, g, k, v, halo, slots):
    features = q.shape[-1]
    vmem = pl.BlockSpec(memory_space=pltpu.VMEM)
    own = jax.ShapeDtypeStruct((BLK_DEV, BLK, features), jnp.bfloat16)
    return pl.pallas_call(
        attend_kernel,
        out_shape=(
            own,
            own,
            jax.ShapeDtypeStruct((2, BLK_DEV, BLK, features), jnp.float32),
            jax.ShapeDtypeStruct((2, REQ + 2, BLK, features), jnp.bfloat16),
            jax.ShapeDtypeStruct((2, 2, BLK, features), jnp.bfloat16),
        ),
        in_specs=[vmem] * 6,
        out_specs=(vmem,) * 5,
        scratch_shapes=[
            pltpu.VMEM((2, BLK_DEV + 2, BLK, features), jnp.float32),
            pltpu.VMEM((2, 2, BLK, features), jnp.float32),
        ],
        compiler_params=pltpu.CompilerParams(vmem_limit_bytes=VMEM_LIMIT),
        name="attend_blocks",
    )(q, g, k, v, halo, slots)


def plan_kernel(table, prev_ref, last_ref):
    me, z, x, c = place()

    @pl.loop(0, NZ * 8)
    def _(at):
        last_ref[at] = ENTRIES

    @pl.loop(0, ENTRIES)
    def _(n):
        source, at = block_place(table[z * ENTRIES + n])
        prev_ref[n] = ENTRIES

        @pl.when(source == x)
        def _():
            prev_ref[n] = last_ref[at]
            last_ref[at] = n


def plan(table):
    smem = pl.BlockSpec(memory_space=pltpu.SMEM)
    return pl.pallas_call(
        plan_kernel,
        out_shape=(
            jax.ShapeDtypeStruct((ENTRIES,), jnp.int32),
            jax.ShapeDtypeStruct((NZ * 8,), jnp.int32),
        ),
        in_specs=[smem],
        out_specs=(smem, smem),
        name="plan_sums",
    )(table)


def back_kernel(
    prev, last, term_ref, rim_ref, out_ref, edge_ref,
    theirs, everything, chain, landed, send_buf, recv_buf, give,
    pair_sem, rim_send, rim_recv, x_send, x_recv, z_send, z_recv, give_sem,
):
    me, z, x, c = place()
    other = 1 - c
    sibling = seq_of(z, x, other)
    after = lax.rem(me + 1, NSEQ)
    before = lax.rem(me + NSEQ - 1, NSEQ)
    xs = (seq_of(z, x + 1, c), seq_of(z, x - 1, c))
    zs = (seq_of(z + 1, x, c), seq_of(z - 1, x, c))
    greet((after, before, xs[0], xs[1], zs[0], zs[1]))

    def lanes(p):
        return pl.ds(p * PART, PART)

    def pair(p):
        return remote(
            term_ref.at[other, :, :, lanes(p)], theirs.at[p], pair_sem.at[0, p],
            pair_sem.at[1, p], sibling,
        )

    for p in range(PARTS):
        pair(p).start()

    def own(p, chip, g):
        base = lax.rem(chip + NX, NX) * SLOTS
        return everything.at[p, pl.ds(base + c * (REQ + 2), REQ), pl.ds(g * ROWS, ROWS)]

    def rest(p, chip, g):
        base = lax.rem(chip + NX, NX) * SLOTS
        return everything.at[p, pl.ds(base + other * REQ, REQ + 2), pl.ds(g * ROWS, ROWS)]

    def send(p, number, chip, which, g):
        ref = (own, rest)[which](p, chip, g)
        return remote(
            ref, ref, x_send.at[p, number, which, g], x_recv.at[p, number, which, g],
            xs[(g, 1 - g, g)[number]],
        )

    def x_first(p):
        columns = slice(p * PART, (p + 1) * PART)
        base = x * SLOTS

        @pl.loop(0, REQ, unroll=2)
        def _(i):
            everything[p, base + c * (REQ + 2) + i] = term_ref[c, i, :, columns]

        for number in range(2):
            for g in range(2):
                send(p, number, x, 0, g).start()
        pair(p).wait_recv()

        @pl.loop(0, REQ, unroll=2)
        def _(i):
            everything[p, base + other * (REQ + 2) + i] = theirs[p, i]

        for i in range(2):
            total = term_ref[c, REQ + i, :, columns].astype(jnp.float32) + theirs[
                p, REQ + i
            ].astype(jnp.float32)
            everything[p, base + REQ + i] = total.astype(jnp.bfloat16)
        for number in range(2):
            for g in range(2):
                send(p, number, x, 1, g).start()

    def x_second(p):
        for which in range(2):
            for g, behind in enumerate((x - 1, x + 1)):
                send(p, 0, behind, which, g).wait_recv()
                send(p, 2, behind, which, g).start()

    def x_wait(p, number):
        for which in range(2):
            for g in range(2):
                send(p, number, x, which, g).wait_recv()

    chain[ENTRIES] = jnp.zeros((BLK, PART), jnp.float32)

    def land(p):
        @pl.loop(0, ENTRIES, unroll=4)
        def _(n):
            chain[n] = everything[p, n].astype(jnp.float32) + chain[prev[n]]

        @pl.loop(0, NZ * 8, unroll=4)
        def _(at):
            landed[p, at] = chain[last[at]]

    def piece(p, direction, distance, half):
        return remote(
            send_buf.at[p, direction, distance - 1, half],
            recv_buf.at[p, direction, distance - 1, half],
            z_send.at[p, direction, distance - 1, half],
            z_recv.at[p, direction, distance - 1, half],
            zs[direction],
        )

    def z_step(p, distance):
        for half in range(2):
            for direction in range(2):
                if distance > Z_LAST[direction, half]:
                    continue
                target = lax.rem(z + (distance if direction == 0 else NZ - distance), NZ)
                first = target * 8 + half * 4
                waits = distance < Z_LAST[direction, half]
                if waits:
                    piece(p, direction, distance + 1, half).wait_recv()
                for i in range(BLK_DEV):
                    total = landed[p, first + i]
                    if waits:
                        total += recv_buf[p, direction, distance, half, i].astype(jnp.float32)
                    send_buf[p, direction, distance - 1, half, i] = total.astype(jnp.bfloat16)
                piece(p, direction, distance, half).start()

    def handed(p):
        return remote(
            give.at[p], out_ref.at[c, :, :, lanes(p)], give_sem.at[0, p], give_sem.at[1, p],
            sibling,
        )

    def finish(p):
        columns = slice(p * PART, (p + 1) * PART)
        for half in range(2):
            for direction in range(2):
                piece(p, direction, 1, half).wait_recv()

        def finished(half, i):
            total = landed[p, z * 8 + half * 4 + i]
            for direction in range(2):
                total += recv_buf[p, direction, 0, half, i].astype(jnp.float32)
            return total.astype(jnp.bfloat16)

        for i in range(BLK_DEV):
            give[p, i] = finished(other, i)
        handed(p).start()
        for i in range(BLK_DEV):
            out_ref[c, i, :, columns] = finished(c, i)

    edges = []
    for number in range(2):
        for side, target in enumerate((after, before)):
            edges.append(
                remote(
                    rim_ref.at[number, 1 - side], edge_ref.at[number, side],
                    rim_send.at[number, side], rim_recv.at[number, side], target,
                )
            )

    x_first(0)
    for p in range(PARTS):
        x_second(p)
        if p + 1 < PARTS:
            x_first(p + 1)
        else:
            for copy in edges:
                copy.start()
        if p:
            z_step(p - 1, 3)
        x_wait(p, 1)
        if p:
            z_step(p - 1, 2)
        x_wait(p, 2)
        if p:
            z_step(p - 1, 1)
        land(p)
        z_step(p, 4)
        if p:
            finish(p - 1)
    for distance in (3, 2, 1):
        z_step(PARTS - 1, distance)
    finish(PARTS - 1)

    for copy in edges:
        copy.wait()
    for p in range(PARTS):
        pair(p).wait_send()
        for number in range(3):
            for which in range(2):
                for g in range(2):
                    send(p, number, x, which, g).wait_send()
        for (direction, half), most in Z_LAST.items():
            for distance in range(1, most + 1):
                piece(p, direction, distance, half).wait_send()
        handed(p).wait()


def send_back(prev, last, terms, rims):
    features = terms.shape[-1]
    vmem = pl.BlockSpec(memory_space=pltpu.VMEM)
    smem = pl.BlockSpec(memory_space=pltpu.SMEM)
    dma = pltpu.SemaphoreType.DMA
    ring = pltpu.VMEM((PARTS, 2, 4, 2, BLK_DEV, BLK, PART), jnp.bfloat16)
    return pl.pallas_call(
        back_kernel,
        out_shape=(
            jax.ShapeDtypeStruct((2, BLK_DEV, BLK, features), jnp.bfloat16),
            jax.ShapeDtypeStruct((2, 2, BLK, features), jnp.bfloat16),
        ),
        in_specs=[smem, smem, vmem, vmem],
        out_specs=(vmem, vmem),
        scratch_shapes=[
            pltpu.VMEM((PARTS, REQ + 2, BLK, PART), jnp.bfloat16),
            pltpu.VMEM((PARTS, ENTRIES, BLK, PART), jnp.bfloat16),
            pltpu.VMEM((ENTRIES + 1, BLK, PART), jnp.float32),
            pltpu.VMEM((PARTS, NZ * 8, BLK, PART), jnp.float32),
            ring, ring,
            pltpu.VMEM((PARTS, BLK_DEV, BLK, PART), jnp.bfloat16),
            dma((2, PARTS)), dma((2, 2)), dma((2, 2)), dma((PARTS, 3, 2, 2)), dma((PARTS, 3, 2, 2)),
            dma((PARTS, 2, 4, 2)), dma((PARTS, 2, 4, 2)), dma((2, PARTS)),
        ],
        compiler_params=pltpu.CompilerParams(
            collective_id=1, has_side_effects=True, vmem_limit_bytes=VMEM_LIMIT
        ),
        name="send_back",
    )(prev, last, terms, rims)


def list_kernel(table, wide_ref, at_ref, pos_ref, back_ref, prev_ref, last_ref, most_ref, count):
    me, z, x, c = place()

    source = lax.rem(lax.div(wide_ref[...], 8), NX)
    chip = lax.rem(lax.broadcasted_iota(jnp.int32, source.shape, 0), NX)
    most = jnp.int32(0)
    for s in range(NX):
        hits = ((source == s) & (chip != s)).astype(jnp.int32)
        most = jnp.maximum(most, jnp.max(jnp.sum(hits, axis=1, keepdims=True)))
    most_ref[0] = most

    @pl.loop(0, NZ * 8)
    def _(at):
        last_ref[at] = TERMS

    @pl.loop(0, 3 * CAP)
    def _(n):
        at_ref[n] = 0
        back_ref[n] = 0
        prev_ref[SLOTS + n] = TERMS

    for r in range(NX):
        count[r] = 0

    @pl.loop(0, SLOTS)
    def _(slot):
        holder, at = block_place(table[(z * NX + x) * SLOTS + slot])
        pos_ref[slot] = 0
        prev_ref[slot] = TERMS
        r = lax.rem(holder - x + NX, NX)

        @pl.when(r == 0)
        def _():
            prev_ref[slot] = last_ref[at]
            last_ref[at] = slot

        @pl.when(r > 0)
        def _():
            j = count[r]
            count[r] = j + 1

            @pl.when(j < CAP)
            def _():
                pos_ref[slot] = (r - 1) * CAP + j
                back_ref[(r - 1) * CAP + j] = slot

    for r in range(1, NX):
        count[0] = 0

        @pl.loop(0, SLOTS)
        def _(slot):
            holder, at = block_place(table[(z * NX + lax.rem(x + r, NX)) * SLOTS + slot])

            @pl.when(holder == x)
            def _():
                j = count[0]
                count[0] = j + 1

                @pl.when(j < CAP)
                def _():
                    n = (r - 1) * CAP + j
                    at_ref[n] = at
                    prev_ref[SLOTS + n] = last_ref[at]
                    last_ref[at] = SLOTS + n


def make_lists(table):
    smem = pl.BlockSpec(memory_space=pltpu.SMEM)
    vmem = pl.BlockSpec(memory_space=pltpu.VMEM)
    sizes = (3 * CAP, SLOTS, 3 * CAP, TERMS, NZ * 8, 1)
    return pl.pallas_call(
        list_kernel,
        out_shape=tuple(jax.ShapeDtypeStruct((size,), jnp.int32) for size in sizes),
        in_specs=[smem, vmem],
        out_specs=(smem,) * 6,
        scratch_shapes=[pltpu.SMEM((NX,), jnp.int32)],
        name="make_lists",
    )(table.reshape(-1), table)


def packed_gather_kernel(
    table, at_list, pos_list, k_ref, v_ref, out_ref, halo_ref,
    packed, give, pair_sem, halo_send, halo_recv, z_send, z_recv, x_send, x_recv, give_sem, *bufs,
):
    ag, landing = bufs[:PARTS], bufs[PARTS:]
    me, z, x, c = place()
    other = 1 - c
    sibling = seq_of(z, x, other)
    after = lax.rem(me + 1, NSEQ)
    before = lax.rem(me + NSEQ - 1, NSEQ)
    zs = (seq_of(z + 1, x, c), seq_of(z - 1, x, c))
    xs = tuple(seq_of(z, x + r, c) for r in range(1, NX))
    greet((after, before) + zs + xs)

    def lanes(p):
        return pl.ds(p * PART, PART)

    def pair_copy(src, p):
        return remote(
            src.at[:, :, lanes(p)], ag[p].at[pl.ds(z * 8 + c * 4, 4)],
            pair_sem.at[0, p], pair_sem.at[1, p], sibling,
        )

    @pl.when(c == 0)
    def _():
        for p in range(PARTS):
            pair_copy(v_ref, p).start()
        for p in range(PARTS):
            ag[p][pl.ds(z * 8, 4)] = k_ref[:, :, p * PART : (p + 1) * PART]

    @pl.when(c == 1)
    def _():
        for p in range(PARTS):
            pair_copy(k_ref, p).start()
        for p in range(PARTS):
            ag[p][pl.ds(z * 8 + 4, 4)] = v_ref[:, :, p * PART : (p + 1) * PART]

    def z_piece(p, direction, step, half):
        origin = lax.rem(z + NZ - (step - 1), NZ) if direction == 0 else lax.rem(z + step - 1, NZ)
        piece = ag[p].at[pl.ds(origin * 8 + half * 4, 4)]
        return remote(
            piece,
            piece,
            z_send.at[p, direction, step - 1, half],
            z_recv.at[p, direction, step - 1, half],
            zs[direction],
        )

    def z_start(p):
        for direction in range(2):
            z_piece(p, direction, 1, c).start()
        pair_copy(v_ref, p).wait()
        for direction in range(2):
            z_piece(p, direction, 1, other).start()

    def z_step(p, step):
        for half in range(2):
            for direction in range(2):
                if step <= Z_LAST[direction, half]:
                    z_piece(p, direction, step, half).wait_recv()
                    if step + 1 <= Z_LAST[direction, half]:
                        z_piece(p, direction, step + 1, half).start()

    def x_copy(p, r):
        return remote(
            packed.at[p, pl.ds((r - 1) * CAP, CAP)],
            landing[p].at[pl.ds((NX - 1 - r) * CAP, CAP)],
            x_send.at[p, r - 1],
            x_recv.at[p, NX - 1 - r],
            xs[r - 1],
        )

    def x_start(p):
        for r in (2, 1, 3):
            @pl.loop(0, CAP, unroll=3)
            def _(j):
                n = (r - 1) * CAP + j
                packed[p, n] = ag[p][at_list[n]]

            x_copy(p, r).start()

    def chosen(p, slot):
        holder, at = block_place(table[(z * NX + x) * SLOTS + slot])
        return jnp.where(holder == x, ag[p][at], landing[p][pos_list[slot]])

    def handed(p):
        return remote(
            give.at[p], out_ref.at[c, :, :, lanes(p)], give_sem.at[0, p], give_sem.at[1, p],
            sibling,
        )

    def finish(p):
        for r in range(1, NX):
            x_copy(p, r).wait_recv()
        columns = slice(p * PART, (p + 1) * PART)

        @pl.loop(0, REQ, unroll=2)
        def _(i):
            give[p, i] = chosen(p, other * (REQ + 2) + i)

        for i in range(2):
            value = chosen(p, REQ + i)
            give[p, REQ + i] = value
            out_ref[c, REQ + i, :, columns] = value
        handed(p).start()

        @pl.loop(0, REQ, unroll=2)
        def _(i):
            out_ref[c, i, :, columns] = chosen(p, c * (REQ + 2) + i)

    halos = []
    for number, ref in enumerate((k_ref, v_ref)):
        for side, (row, target) in enumerate(((BLK_DEV - 1, after), (0, before))):
            halos.append(
                remote(
                    ref.at[row], halo_ref.at[number, side], halo_send.at[number, side],
                    halo_recv.at[number, side], target,
                )
            )

    z_start(0)
    for turn in range(1, 2 * PARTS + 6):
        for p in range(PARTS):
            step = turn - 2 * p
            if step == 0:
                z_start(p)
            if 1 <= step <= 4:
                z_step(p, step)
            if step == 4:
                x_start(p)
            if step == 7:
                finish(p)
        if turn == 3:
            for copy in halos:
                copy.start()

    for copy in halos:
        copy.wait()
    for p in range(PARTS):
        for (direction, half), last in Z_LAST.items():
            for step in range(1, last + 1):
                z_piece(p, direction, step, half).wait_send()
        for r in range(1, NX):
            x_copy(p, r).wait_send()
        handed(p).wait()


def packed_gather(table, at_list, pos_list, k, v):
    features = k.shape[-1]
    vmem = pl.BlockSpec(memory_space=pltpu.VMEM)
    smem = pl.BlockSpec(memory_space=pltpu.SMEM)
    dma = pltpu.SemaphoreType.DMA
    return pl.pallas_call(
        packed_gather_kernel,
        out_shape=(
            jax.ShapeDtypeStruct((2, REQ + 2, BLK, features), jnp.bfloat16),
            jax.ShapeDtypeStruct((2, 2, BLK, features), jnp.bfloat16),
        ),
        in_specs=[smem, smem, smem, vmem, vmem],
        out_specs=(vmem, vmem),
        scratch_shapes=[
            pltpu.VMEM((PARTS, 3 * CAP, BLK, PART), jnp.bfloat16),
            pltpu.VMEM((PARTS, REQ + 2, BLK, PART), jnp.bfloat16),
            dma((2, PARTS)), dma((2, 2)), dma((2, 2)), dma((PARTS, 2, 4, 2)), dma((PARTS, 2, 4, 2)),
            dma((PARTS, 3)), dma((PARTS, 3)), dma((2, PARTS)),
        ]
        + [pltpu.VMEM((NZ * 8, BLK, PART), jnp.bfloat16)] * PARTS
        + [pltpu.VMEM((3 * CAP, BLK, PART), jnp.bfloat16)] * PARTS,
        compiler_params=pltpu.CompilerParams(
            collective_id=2, has_side_effects=True, vmem_limit_bytes=VMEM_LIMIT
        ),
        name="packed_gather",
    )(table, at_list, pos_list, k, v)


def packed_back_kernel(
    back_list, prev, last, term_ref, rim_ref, out_ref, edge_ref,
    theirs, own, packed, arrived, chain, landed, send_buf, recv_buf, give,
    pair_sem, rim_send, rim_recv, x_send, x_recv, z_send, z_recv, give_sem,
):
    me, z, x, c = place()
    other = 1 - c
    sibling = seq_of(z, x, other)
    after = lax.rem(me + 1, NSEQ)
    before = lax.rem(me + NSEQ - 1, NSEQ)
    xs = tuple(seq_of(z, x + r, c) for r in range(1, NX))
    zs = (seq_of(z + 1, x, c), seq_of(z - 1, x, c))
    greet((after, before) + zs + xs)

    def lanes(p):
        return pl.ds(p * PART, PART)

    def pair(p):
        return remote(
            term_ref.at[other, :, :, lanes(p)], theirs.at[p], pair_sem.at[0, p],
            pair_sem.at[1, p], sibling,
        )

    for p in range(PARTS):
        pair(p).start()

    def x_copy(p, r):
        return remote(
            packed.at[p, pl.ds((r - 1) * CAP, CAP)],
            arrived.at[p, pl.ds((NX - 1 - r) * CAP, CAP)],
            x_send.at[p, r - 1],
            x_recv.at[p, NX - 1 - r],
            xs[r - 1],
        )

    def x_start(p):
        columns = slice(p * PART, (p + 1) * PART)

        @pl.loop(0, REQ, unroll=2)
        def _(i):
            own[p, c * (REQ + 2) + i] = term_ref[c, i, :, columns]

        pair(p).wait_recv()

        @pl.loop(0, REQ, unroll=2)
        def _(i):
            own[p, other * (REQ + 2) + i] = theirs[p, i]

        for i in range(2):
            total = term_ref[c, REQ + i, :, columns].astype(jnp.float32) + theirs[
                p, REQ + i
            ].astype(jnp.float32)
            own[p, REQ + i] = total.astype(jnp.bfloat16)
        for r in (2, 1, 3):
            @pl.loop(0, CAP, unroll=3)
            def _(j):
                n = (r - 1) * CAP + j
                packed[p, n] = own[p, back_list[n]]

            x_copy(p, r).start()

    chain[TERMS] = jnp.zeros((BLK, PART), jnp.float32)

    def land(p):
        @pl.loop(0, SLOTS, unroll=2)
        def _(n):
            chain[n] = own[p, n].astype(jnp.float32) + chain[prev[n]]

        for r in range(1, NX):
            x_copy(p, r).wait_recv()

        @pl.loop(0, 3 * CAP, unroll=3)
        def _(n):
            chain[SLOTS + n] = arrived[p, n].astype(jnp.float32) + chain[prev[SLOTS + n]]

        @pl.loop(0, NZ * 8, unroll=4)
        def _(at):
            landed[p, at] = chain[last[at]]

    def piece(p, direction, distance, half):
        return remote(
            send_buf.at[p, direction, distance - 1, half],
            recv_buf.at[p, direction, distance - 1, half],
            z_send.at[p, direction, distance - 1, half],
            z_recv.at[p, direction, distance - 1, half],
            zs[direction],
        )

    def z_step(p, distance):
        for half in range(2):
            for direction in range(2):
                if distance > Z_LAST[direction, half]:
                    continue
                target = lax.rem(z + (distance if direction == 0 else NZ - distance), NZ)
                first = target * 8 + half * 4
                waits = distance < Z_LAST[direction, half]
                if waits:
                    piece(p, direction, distance + 1, half).wait_recv()
                for i in range(BLK_DEV):
                    total = landed[p, first + i]
                    if waits:
                        total += recv_buf[p, direction, distance, half, i].astype(jnp.float32)
                    send_buf[p, direction, distance - 1, half, i] = total.astype(jnp.bfloat16)
                piece(p, direction, distance, half).start()

    def handed(p):
        return remote(
            give.at[p], out_ref.at[c, :, :, lanes(p)], give_sem.at[0, p], give_sem.at[1, p],
            sibling,
        )

    def finish(p):
        columns = slice(p * PART, (p + 1) * PART)
        for half in range(2):
            for direction in range(2):
                piece(p, direction, 1, half).wait_recv()

        def finished(half, i):
            total = landed[p, z * 8 + half * 4 + i]
            for direction in range(2):
                total += recv_buf[p, direction, 0, half, i].astype(jnp.float32)
            return total.astype(jnp.bfloat16)

        for i in range(BLK_DEV):
            give[p, i] = finished(other, i)
        handed(p).start()
        for i in range(BLK_DEV):
            out_ref[c, i, :, columns] = finished(c, i)

    edges = []
    for number in range(2):
        for side, target in enumerate((after, before)):
            edges.append(
                remote(
                    rim_ref.at[number, 1 - side], edge_ref.at[number, side],
                    rim_send.at[number, side], rim_recv.at[number, side], target,
                )
            )

    x_start(0)
    x_start(1)
    for copy in edges:
        copy.start()
    for p in range(PARTS):
        land(p)
        if p + 2 < PARTS:
            x_start(p + 2)
        z_step(p, 4)
        if p:
            z_step(p - 1, 2)
        z_step(p, 3)
        if p:
            z_step(p - 1, 1)
            finish(p - 1)
    z_step(PARTS - 1, 2)
    z_step(PARTS - 1, 1)
    finish(PARTS - 1)

    for copy in edges:
        copy.wait()
    for p in range(PARTS):
        pair(p).wait_send()
        for r in range(1, NX):
            x_copy(p, r).wait_send()
        for (direction, half), most in Z_LAST.items():
            for distance in range(1, most + 1):
                piece(p, direction, distance, half).wait_send()
        handed(p).wait()


def packed_back(back_list, prev, last, terms, rims):
    features = terms.shape[-1]
    vmem = pl.BlockSpec(memory_space=pltpu.VMEM)
    smem = pl.BlockSpec(memory_space=pltpu.SMEM)
    dma = pltpu.SemaphoreType.DMA
    ring = pltpu.VMEM((PARTS, 2, 4, 2, BLK_DEV, BLK, PART), jnp.bfloat16)
    return pl.pallas_call(
        packed_back_kernel,
        out_shape=(
            jax.ShapeDtypeStruct((2, BLK_DEV, BLK, features), jnp.bfloat16),
            jax.ShapeDtypeStruct((2, 2, BLK, features), jnp.bfloat16),
        ),
        in_specs=[smem, smem, smem, vmem, vmem],
        out_specs=(vmem, vmem),
        scratch_shapes=[
            pltpu.VMEM((PARTS, REQ + 2, BLK, PART), jnp.bfloat16),
            pltpu.VMEM((PARTS, SLOTS, BLK, PART), jnp.bfloat16),
            pltpu.VMEM((PARTS, 3 * CAP, BLK, PART), jnp.bfloat16),
            pltpu.VMEM((PARTS, 3 * CAP, BLK, PART), jnp.bfloat16),
            pltpu.VMEM((TERMS + 1, BLK, PART), jnp.float32),
            pltpu.VMEM((PARTS, NZ * 8, BLK, PART), jnp.float32),
            ring, ring,
            pltpu.VMEM((PARTS, BLK_DEV, BLK, PART), jnp.bfloat16),
            dma((2, PARTS)), dma((2, 2)), dma((2, 2)), dma((PARTS, 3)), dma((PARTS, 3)),
            dma((PARTS, 2, 4, 2)), dma((PARTS, 2, 4, 2)), dma((2, PARTS)),
        ],
        compiler_params=pltpu.CompilerParams(
            collective_id=3, has_side_effects=True, vmem_limit_bytes=VMEM_LIMIT
        ),
        name="packed_back",
    )(back_list, prev, last, terms, rims)


def per_device(queries, key_rows, value_rows, out_grad, random_blocks, global_blocks):
    row_count, features = queries.shape
    blocks = (BLK_DEV, BLK, features)
    lists = random_blocks.reshape(NZ * NX, NC, REQ)
    shared = jnp.broadcast_to(global_blocks[None], (NZ * NX, 2))
    table = jnp.concatenate([lists[:, 0], shared, lists[:, 1]], axis=1)
    k = key_rows.reshape(blocks)
    v = value_rows.reshape(blocks)
    q = queries.reshape(blocks)
    g = out_grad.reshape(blocks)
    at_list, pos_list, back_list, chain_prev, chain_last, most = make_lists(table)

    def packed():
        slots, halo = packed_gather(table.reshape(-1), at_list, pos_list, k, v)
        attended, query_grad, wacc, terms, rims = attend(q, g, k, v, halo, slots)
        total, edges = packed_back(back_list, chain_prev, chain_last, terms, rims)
        return attended, query_grad, *joined(wacc, total, edges)

    def unpacked():
        flat = table.reshape(-1)
        prev, last = plan(flat)
        slots, halo = gather(flat, k, v)
        attended, query_grad, wacc, terms, rims = attend(q, g, k, v, halo, slots)
        total, edges = send_back(prev, last, terms, rims)
        return attended, query_grad, *joined(wacc, total, edges)

    results = lax.cond(most[0] <= CAP, packed, unpacked)
    return tuple(result.reshape(row_count, features) for result in results)


def joined(wacc, total, edges):
    gradient = wacc + total.astype(jnp.float32)
    gradient = gradient.at[:, 0].add(edges[:, 0].astype(jnp.float32))
    gradient = gradient.at[:, BLK_DEV - 1].add(edges[:, 1].astype(jnp.float32))
    gradient = gradient.astype(jnp.bfloat16)
    return gradient[0], gradient[1]


def solution(mesh):
    in_specs = (
        P("seq", "head"),
        P("seq", "head"),
        P("seq", "head"),
        P("seq", "head"),
        P("head", None, None),
        P(),
    )
    out_specs = (P("seq", "head"), P("seq", "head"), P("seq", "head"), P("seq", "head"))
    return jax.shard_map(
        per_device, mesh=mesh, in_specs=in_specs, out_specs=out_specs, check_vma=False
    )
```

```python
import math

import jax
import jax.numpy as jnp
from jax import lax
from jax.experimental import pallas as pl
from jax.experimental.pallas import tpu as pltpu
from jax.sharding import PartitionSpec as P

HEAD_DIM = 128
BLK = 64
NZ = 8
NX = 4
NC = 2
NSEQ = NZ * NX * NC
BLK_DEV = 4
REQ = 12
SLOTS = 2 * REQ + 2
ENTRIES = NX * SLOTS
PARTS = 4
PART = 128
ROWS = BLK // 2
CAP = 15
TERMS = SLOTS + 3 * CAP
VMEM_LIMIT = 56 * 1024 * 1024


def seq_of(z, x, c):
    return (lax.rem(z + NZ, NZ) * NX + lax.rem(x + NX, NX)) * NC + c


def place():
    me = lax.axis_index("seq")
    z = me // (NX * NC)
    x = lax.rem(me // NC, NX)
    c = lax.rem(me, NC)
    return me, z, x, c


def remote(src, dst, send_sem, recv_sem, target):
    return pltpu.make_async_remote_copy(
        src_ref=src,
        dst_ref=dst,
        send_sem=send_sem,
        recv_sem=recv_sem,
        device_id={"seq": target},
        device_id_type=pl.DeviceIdType.MESH,
    )


def greet(partners):
    barrier = pltpu.get_barrier_semaphore()
    for partner in partners:
        pl.semaphore_signal(
            barrier, inc=1, device_id={"seq": partner}, device_id_type=pl.DeviceIdType.MESH
        )
    pl.semaphore_wait(barrier, len(partners))


def block_place(block):
    return lax.rem(lax.div(block, 8), NX), lax.div(block, 32) * 8 + lax.rem(block, 8)


Z_LAST = {(0, 0): 4, (0, 1): 3, (1, 0): 3, (1, 1): 4}


def gather_kernel(
    table, k_ref, v_ref, out_ref, halo_ref,
    s1_out, s1_in, s2_out, s2_in, s3_out, s3_in, give,
    pair_sem, halo_send, halo_recv, z_send, z_recv, x_send, x_recv, give_sem, *ag,
):
    me, z, x, c = place()
    other = 1 - c
    sibling = seq_of(z, x, other)
    after = lax.rem(me + 1, NSEQ)
    before = lax.rem(me + NSEQ - 1, NSEQ)
    xs = (seq_of(z, x + 1, c), seq_of(z, x - 1, c))
    zs = (seq_of(z + 1, x, c), seq_of(z - 1, x, c))
    greet((after, before, zs[0], zs[1], xs[0], xs[1]))

    def lanes(p):
        return pl.ds(p * PART, PART)

    def pair_copy(src, p):
        return remote(
            src.at[:, :, lanes(p)], ag[p].at[pl.ds(z * 8 + c * 4, 4)],
            pair_sem.at[0, p], pair_sem.at[1, p], sibling,
        )

    @pl.when(c == 0)
    def _():
        for p in range(PARTS):
            pair_copy(v_ref, p).start()
        for p in range(PARTS):
            ag[p][pl.ds(z * 8, 4)] = k_ref[:, :, p * PART : (p + 1) * PART]

    @pl.when(c == 1)
    def _():
        for p in range(PARTS):
            pair_copy(k_ref, p).start()
        for p in range(PARTS):
            ag[p][pl.ds(z * 8 + 4, 4)] = v_ref[:, :, p * PART : (p + 1) * PART]

    def z_piece(p, direction, step, half):
        origin = lax.rem(z + NZ - (step - 1), NZ) if direction == 0 else lax.rem(z + step - 1, NZ)
        piece = ag[p].at[pl.ds(origin * 8 + half * 4, 4)]
        return remote(
            piece,
            piece,
            z_send.at[p, direction, step - 1, half],
            z_recv.at[p, direction, step - 1, half],
            zs[direction],
        )

    def z_start(p):
        for direction in range(2):
            z_piece(p, direction, 1, c).start()
        pair_copy(v_ref, p).wait()
        for direction in range(2):
            z_piece(p, direction, 1, other).start()

    def z_step(p, step):
        for half in range(2):
            for direction in range(2):
                if step <= Z_LAST[direction, half]:
                    z_piece(p, direction, step, half).wait_recv()
                    if step + 1 <= Z_LAST[direction, half]:
                        z_piece(p, direction, step + 1, half).start()

    def wanted(p, chip, slot):
        source, at = block_place(table[(z * NX + lax.rem(chip + NX, NX)) * SLOTS + slot])
        return source, ag[p][at]

    def x_copy(p, number, g):
        src, dst, way = ((s1_out, s1_in, g), (s2_out, s2_in, g), (s3_out, s3_in, 1 - g))[number]
        return remote(
            src.at[p, g], dst.at[p, g], x_send.at[p, number, g], x_recv.at[p, number, g], xs[way]
        )

    def x_first(p):
        @pl.loop(0, SLOTS, unroll=2)
        def _(slot):
            mine = wanted(p, x + 2, slot)[1]
            s1_out[p, 0, slot] = mine[:ROWS]
            s1_out[p, 1, slot] = mine[ROWS:]

        for g in range(2):
            x_copy(p, 0, g).start()

        @pl.loop(0, SLOTS, unroll=2)
        def _(slot):
            s3_out[p, 0, slot] = wanted(p, x - 1, slot)[1][:ROWS]
            s3_out[p, 1, slot] = wanted(p, x + 1, slot)[1][ROWS:]

        for g in range(2):
            x_copy(p, 2, g).start()

    def x_second(p):
        for g in range(2):
            x_copy(p, 0, g).wait_recv()

        @pl.loop(0, SLOTS, unroll=2)
        def _(slot):
            source, mine = wanted(p, x + 1, slot)
            s2_out[p, 0, slot] = jnp.where(source == x, mine[:ROWS], s1_in[p, 0, slot])
            source, mine = wanted(p, x - 1, slot)
            s2_out[p, 1, slot] = jnp.where(source == x, mine[ROWS:], s1_in[p, 1, slot])

        for g in range(2):
            x_copy(p, 1, g).start()

    here = (lax.rem(x + 1, NX), lax.rem(x + NX - 1, NX))

    def chosen(p, slot):
        source, mine = wanted(p, x, slot)
        passed = [
            jnp.where(source == here[g], s3_in[p, g, slot], s2_in[p, g, slot]) for g in range(2)
        ]
        return jnp.where(source == x, mine, jnp.concatenate(passed, axis=0))

    def handed(p):
        return remote(
            give.at[p], out_ref.at[c, :, :, lanes(p)], give_sem.at[0, p], give_sem.at[1, p],
            sibling,
        )

    def finish(p):
        for number in (2, 1):
            for g in range(2):
                x_copy(p, number, g).wait_recv()
        columns = slice(p * PART, (p + 1) * PART)

        @pl.loop(0, REQ, unroll=2)
        def _(i):
            give[p, i] = chosen(p, other * (REQ + 2) + i)

        for i in range(2):
            value = chosen(p, REQ + i)
            give[p, REQ + i] = value
            out_ref[c, REQ + i, :, columns] = value
        handed(p).start()

        @pl.loop(0, REQ, unroll=2)
        def _(i):
            out_ref[c, i, :, columns] = chosen(p, c * (REQ + 2) + i)

    halos = []
    for number, ref in enumerate((k_ref, v_ref)):
        for side, (row, target) in enumerate(((BLK_DEV - 1, after), (0, before))):
            halos.append(
                remote(
                    ref.at[row], halo_ref.at[number, side], halo_send.at[number, side],
                    halo_recv.at[number, side], target,
                )
            )

    z_start(0)
    for step in range(1, 5):
        z_step(0, step)
    if PARTS > 1:
        z_start(1)
    x_first(0)
    for p in range(PARTS):
        more = p + 1 < PARTS
        if more:
            z_step(p + 1, 1)
            z_step(p + 1, 2)
        x_second(p)
        if more:
            z_step(p + 1, 3)
            z_step(p + 1, 4)
            if p + 2 < PARTS:
                z_start(p + 2)
            x_first(p + 1)
        else:
            for copy in halos:
                copy.start()
        finish(p)

    for copy in halos:
        copy.wait()
    for p in range(PARTS):
        for (direction, half), last in Z_LAST.items():
            for step in range(1, last + 1):
                z_piece(p, direction, step, half).wait_send()
        for number in range(3):
            for g in range(2):
                x_copy(p, number, g).wait_send()
        handed(p).wait()


def gather(table, k, v):
    features = k.shape[-1]
    big = pltpu.VMEM((PARTS, 2, SLOTS, ROWS, PART), jnp.bfloat16)
    vmem = pl.BlockSpec(memory_space=pltpu.VMEM)
    smem = pl.BlockSpec(memory_space=pltpu.SMEM)
    dma = pltpu.SemaphoreType.DMA
    return pl.pallas_call(
        gather_kernel,
        out_shape=(
            jax.ShapeDtypeStruct((2, REQ + 2, BLK, features), jnp.bfloat16),
            jax.ShapeDtypeStruct((2, 2, BLK, features), jnp.bfloat16),
        ),
        in_specs=[smem, vmem, vmem],
        out_specs=(vmem, vmem),
        scratch_shapes=[
            big, big, big, big, big, big,
            pltpu.VMEM((PARTS, REQ + 2, BLK, PART), jnp.bfloat16),
            dma((2, PARTS)), dma((2, 2)), dma((2, 2)), dma((PARTS, 2, 4, 2)), dma((PARTS, 2, 4, 2)),
            dma((PARTS, 3, 2)), dma((PARTS, 3, 2)), dma((2, PARTS)),
        ]
        + [pltpu.VMEM((NZ * 8, BLK, PART), jnp.bfloat16)] * PARTS,
        compiler_params=pltpu.CompilerParams(
            collective_id=0, has_side_effects=True, vmem_limit_bytes=VMEM_LIMIT
        ),
        name="gather_blocks",
    )(table, k, v)


def nt(a, b):
    return lax.dot_general(a, b, (((1,), (1,)), ((), ())), preferred_element_type=jnp.float32)


def tn(a, b):
    return lax.dot_general(a, b, (((0,), (0,)), ((), ())), preferred_element_type=jnp.float32)


def nn(a, b):
    return lax.dot_general(a, b, (((1,), (0,)), ((), ())), preferred_element_type=jnp.float32)


def attend_kernel(
    q_ref, g_ref, k_ref, v_ref, halo_ref, slot_ref,
    att_ref, qg_ref, wacc_ref, term_ref, rim_ref, acc, gacc,
):
    me = lax.axis_index("seq")
    features = q_ref.shape[-1]
    heads = features // HEAD_DIM
    scale = 1.0 / math.sqrt(HEAD_DIM)
    lane_head = lax.broadcasted_iota(jnp.int32, (BLK, features), 1) // HEAD_DIM
    acc[...] = jnp.zeros_like(acc)
    gacc[...] = jnp.zeros_like(gacc)

    def spread(rows):
        zero = jnp.zeros_like(rows)
        return jnp.concatenate(
            [jnp.where(lane_head == h, rows, zero) for h in range(heads)], axis=0
        )

    def diagonal(full):
        return jnp.concatenate(
            [
                full[h * BLK : (h + 1) * BLK, h * HEAD_DIM : (h + 1) * HEAD_DIM]
                for h in range(heads)
            ],
            axis=1,
        )

    for b in range(BLK_DEV):
        def listed(number, own):
            window = [
                halo_ref[number, 0] if b == 0 else own[b - 1],
                own[b],
                halo_ref[number, 1] if b == BLK_DEV - 1 else own[b + 1],
            ]
            extra = [slot_ref[number, REQ], slot_ref[number, REQ + 1]]
            random = [slot_ref[number, 3 * b + i] for i in range(3)]
            return jnp.concatenate(window + extra + random, axis=0)

        keys = listed(0, k_ref)
        values = listed(1, v_ref)
        query = spread(q_ref[b])
        grad = spread(g_ref[b])
        scores = nt(keys, query) * scale
        if b == 0:
            scores = jnp.concatenate(
                [jnp.where(me == 0, -jnp.inf, scores[:BLK]), scores[BLK:]], axis=0
            )
        if b == BLK_DEV - 1:
            scores = jnp.concatenate(
                [
                    scores[: 2 * BLK],
                    jnp.where(me == NSEQ - 1, -jnp.inf, scores[2 * BLK : 3 * BLK]),
                    scores[3 * BLK :],
                ],
                axis=0,
            )
        row_max = jnp.max(scores, axis=0, keepdims=True)
        raw = jnp.exp(scores - row_max)
        weights = raw * (1.0 / jnp.sum(raw, axis=0, keepdims=True))
        weights_b = weights.astype(jnp.bfloat16)
        weight_grads = nt(values, grad)
        row_dot = jnp.sum(weights_b.astype(jnp.float32) * weight_grads, axis=0, keepdims=True)
        score_grads = (weights * (weight_grads - row_dot) * scale).astype(jnp.bfloat16)
        att_ref[b] = diagonal(tn(weights_b, values)).astype(jnp.bfloat16)
        qg_ref[b] = diagonal(tn(score_grads, keys)).astype(jnp.bfloat16)
        for number, terms in enumerate((nn(score_grads, query), nn(weights_b, grad))):
            for i in range(3):
                acc[number, b + i] += terms[i * BLK : (i + 1) * BLK]
            for i in range(2):
                gacc[number, i] += terms[(3 + i) * BLK : (4 + i) * BLK]
            for i in range(3):
                term_ref[number, 3 * b + i] = terms[(5 + i) * BLK : (6 + i) * BLK].astype(
                    jnp.bfloat16
                )
    for number in range(2):
        for i in range(2):
            term_ref[number, REQ + i] = gacc[number, i].astype(jnp.bfloat16)
        rim_ref[number, 0] = acc[number, 0].astype(jnp.bfloat16)
        rim_ref[number, 1] = acc[number, BLK_DEV + 1].astype(jnp.bfloat16)
        for i in range(BLK_DEV):
            wacc_ref[number, i] = acc[number, i + 1]


def attend(q, g, k, v, halo, slots):
    features = q.shape[-1]
    vmem = pl.BlockSpec(memory_space=pltpu.VMEM)
    own = jax.ShapeDtypeStruct((BLK_DEV, BLK, features), jnp.bfloat16)
    return pl.pallas_call(
        attend_kernel,
        out_shape=(
            own,
            own,
            jax.ShapeDtypeStruct((2, BLK_DEV, BLK, features), jnp.float32),
            jax.ShapeDtypeStruct((2, REQ + 2, BLK, features), jnp.bfloat16),
            jax.ShapeDtypeStruct((2, 2, BLK, features), jnp.bfloat16),
        ),
        in_specs=[vmem] * 6,
        out_specs=(vmem,) * 5,
        scratch_shapes=[
            pltpu.VMEM((2, BLK_DEV + 2, BLK, features), jnp.float32),
            pltpu.VMEM((2, 2, BLK, features), jnp.float32),
        ],
        compiler_params=pltpu.CompilerParams(vmem_limit_bytes=VMEM_LIMIT),
        name="attend_blocks",
    )(q, g, k, v, halo, slots)


def plan_kernel(table, prev_ref, last_ref):
    me, z, x, c = place()

    @pl.loop(0, NZ * 8)
    def _(at):
        last_ref[at] = ENTRIES

    @pl.loop(0, ENTRIES)
    def _(n):
        source, at = block_place(table[z * ENTRIES + n])
        prev_ref[n] = ENTRIES

        @pl.when(source == x)
        def _():
            prev_ref[n] = last_ref[at]
            last_ref[at] = n


def plan(table):
    smem = pl.BlockSpec(memory_space=pltpu.SMEM)
    return pl.pallas_call(
        plan_kernel,
        out_shape=(
            jax.ShapeDtypeStruct((ENTRIES,), jnp.int32),
            jax.ShapeDtypeStruct((NZ * 8,), jnp.int32),
        ),
        in_specs=[smem],
        out_specs=(smem, smem),
        name="plan_sums",
    )(table)


def back_kernel(
    prev, last, term_ref, rim_ref, out_ref, edge_ref,
    theirs, everything, chain, landed, send_buf, recv_buf, give,
    pair_sem, rim_send, rim_recv, x_send, x_recv, z_send, z_recv, give_sem,
):
    me, z, x, c = place()
    other = 1 - c
    sibling = seq_of(z, x, other)
    after = lax.rem(me + 1, NSEQ)
    before = lax.rem(me + NSEQ - 1, NSEQ)
    xs = (seq_of(z, x + 1, c), seq_of(z, x - 1, c))
    zs = (seq_of(z + 1, x, c), seq_of(z - 1, x, c))
    greet((after, before, xs[0], xs[1], zs[0], zs[1]))

    def lanes(p):
        return pl.ds(p * PART, PART)

    def pair(p):
        return remote(
            term_ref.at[other, :, :, lanes(p)], theirs.at[p], pair_sem.at[0, p],
            pair_sem.at[1, p], sibling,
        )

    for p in range(PARTS):
        pair(p).start()

    def own(p, chip, g):
        base = lax.rem(chip + NX, NX) * SLOTS
        return everything.at[p, pl.ds(base + c * (REQ + 2), REQ), pl.ds(g * ROWS, ROWS)]

    def rest(p, chip, g):
        base = lax.rem(chip + NX, NX) * SLOTS
        return everything.at[p, pl.ds(base + other * REQ, REQ + 2), pl.ds(g * ROWS, ROWS)]

    def send(p, number, chip, which, g):
        ref = (own, rest)[which](p, chip, g)
        return remote(
            ref, ref, x_send.at[p, number, which, g], x_recv.at[p, number, which, g],
            xs[(g, 1 - g, g)[number]],
        )

    def x_first(p):
        columns = slice(p * PART, (p + 1) * PART)
        base = x * SLOTS

        @pl.loop(0, REQ, unroll=2)
        def _(i):
            everything[p, base + c * (REQ + 2) + i] = term_ref[c, i, :, columns]

        for number in range(2):
            for g in range(2):
                send(p, number, x, 0, g).start()
        pair(p).wait_recv()

        @pl.loop(0, REQ, unroll=2)
        def _(i):
            everything[p, base + other * (REQ + 2) + i] = theirs[p, i]

        for i in range(2):
            total = term_ref[c, REQ + i, :, columns].astype(jnp.float32) + theirs[
                p, REQ + i
            ].astype(jnp.float32)
            everything[p, base + REQ + i] = total.astype(jnp.bfloat16)
        for number in range(2):
            for g in range(2):
                send(p, number, x, 1, g).start()

    def x_second(p):
        for which in range(2):
            for g, behind in enumerate((x - 1, x + 1)):
                send(p, 0, behind, which, g).wait_recv()
                send(p, 2, behind, which, g).start()

    def x_wait(p, number):
        for which in range(2):
            for g in range(2):
                send(p, number, x, which, g).wait_recv()

    chain[ENTRIES] = jnp.zeros((BLK, PART), jnp.float32)

    def land(p):
        @pl.loop(0, ENTRIES, unroll=4)
        def _(n):
            chain[n] = everything[p, n].astype(jnp.float32) + chain[prev[n]]

        @pl.loop(0, NZ * 8, unroll=4)
        def _(at):
            landed[p, at] = chain[last[at]]

    def piece(p, direction, distance, half):
        return remote(
            send_buf.at[p, direction, distance - 1, half],
            recv_buf.at[p, direction, distance - 1, half],
            z_send.at[p, direction, distance - 1, half],
            z_recv.at[p, direction, distance - 1, half],
            zs[direction],
        )

    def z_step(p, distance):
        for half in range(2):
            for direction in range(2):
                if distance > Z_LAST[direction, half]:
                    continue
                target = lax.rem(z + (distance if direction == 0 else NZ - distance), NZ)
                first = target * 8 + half * 4
                waits = distance < Z_LAST[direction, half]
                if waits:
                    piece(p, direction, distance + 1, half).wait_recv()
                for i in range(BLK_DEV):
                    total = landed[p, first + i]
                    if waits:
                        total += recv_buf[p, direction, distance, half, i].astype(jnp.float32)
                    send_buf[p, direction, distance - 1, half, i] = total.astype(jnp.bfloat16)
                piece(p, direction, distance, half).start()

    def handed(p):
        return remote(
            give.at[p], out_ref.at[c, :, :, lanes(p)], give_sem.at[0, p], give_sem.at[1, p],
            sibling,
        )

    def finish(p):
        columns = slice(p * PART, (p + 1) * PART)
        for half in range(2):
            for direction in range(2):
                piece(p, direction, 1, half).wait_recv()

        def finished(half, i):
            total = landed[p, z * 8 + half * 4 + i]
            for direction in range(2):
                total += recv_buf[p, direction, 0, half, i].astype(jnp.float32)
            return total.astype(jnp.bfloat16)

        for i in range(BLK_DEV):
            give[p, i] = finished(other, i)
        handed(p).start()
        for i in range(BLK_DEV):
            out_ref[c, i, :, columns] = finished(c, i)

    edges = []
    for number in range(2):
        for side, target in enumerate((after, before)):
            edges.append(
                remote(
                    rim_ref.at[number, 1 - side], edge_ref.at[number, side],
                    rim_send.at[number, side], rim_recv.at[number, side], target,
                )
            )

    x_first(0)
    for p in range(PARTS):
        x_second(p)
        if p + 1 < PARTS:
            x_first(p + 1)
        else:
            for copy in edges:
                copy.start()
        if p:
            z_step(p - 1, 3)
        x_wait(p, 1)
        if p:
            z_step(p - 1, 2)
        x_wait(p, 2)
        if p:
            z_step(p - 1, 1)
        land(p)
        z_step(p, 4)
        if p:
            finish(p - 1)
    for distance in (3, 2, 1):
        z_step(PARTS - 1, distance)
    finish(PARTS - 1)

    for copy in edges:
        copy.wait()
    for p in range(PARTS):
        pair(p).wait_send()
        for number in range(3):
            for which in range(2):
                for g in range(2):
                    send(p, number, x, which, g).wait_send()
        for (direction, half), most in Z_LAST.items():
            for distance in range(1, most + 1):
                piece(p, direction, distance, half).wait_send()
        handed(p).wait()


def send_back(prev, last, terms, rims):
    features = terms.shape[-1]
    vmem = pl.BlockSpec(memory_space=pltpu.VMEM)
    smem = pl.BlockSpec(memory_space=pltpu.SMEM)
    dma = pltpu.SemaphoreType.DMA
    ring = pltpu.VMEM((PARTS, 2, 4, 2, BLK_DEV, BLK, PART), jnp.bfloat16)
    return pl.pallas_call(
        back_kernel,
        out_shape=(
            jax.ShapeDtypeStruct((2, BLK_DEV, BLK, features), jnp.bfloat16),
            jax.ShapeDtypeStruct((2, 2, BLK, features), jnp.bfloat16),
        ),
        in_specs=[smem, smem, vmem, vmem],
        out_specs=(vmem, vmem),
        scratch_shapes=[
            pltpu.VMEM((PARTS, REQ + 2, BLK, PART), jnp.bfloat16),
            pltpu.VMEM((PARTS, ENTRIES, BLK, PART), jnp.bfloat16),
            pltpu.VMEM((ENTRIES + 1, BLK, PART), jnp.float32),
            pltpu.VMEM((PARTS, NZ * 8, BLK, PART), jnp.float32),
            ring, ring,
            pltpu.VMEM((PARTS, BLK_DEV, BLK, PART), jnp.bfloat16),
            dma((2, PARTS)), dma((2, 2)), dma((2, 2)), dma((PARTS, 3, 2, 2)), dma((PARTS, 3, 2, 2)),
            dma((PARTS, 2, 4, 2)), dma((PARTS, 2, 4, 2)), dma((2, PARTS)),
        ],
        compiler_params=pltpu.CompilerParams(
            collective_id=1, has_side_effects=True, vmem_limit_bytes=VMEM_LIMIT
        ),
        name="send_back",
    )(prev, last, terms, rims)


def list_kernel(table, wide_ref, at_ref, pos_ref, back_ref, prev_ref, last_ref, most_ref, count):
    me, z, x, c = place()

    source = lax.rem(lax.div(wide_ref[...], 8), NX)
    chip = lax.rem(lax.broadcasted_iota(jnp.int32, source.shape, 0), NX)
    most = jnp.int32(0)
    for s in range(NX):
        hits = ((source == s) & (chip != s)).astype(jnp.int32)
        most = jnp.maximum(most, jnp.max(jnp.sum(hits, axis=1, keepdims=True)))
    most_ref[0] = most

    @pl.loop(0, NZ * 8)
    def _(at):
        last_ref[at] = TERMS

    @pl.loop(0, 3 * CAP)
    def _(n):
        at_ref[n] = 0
        back_ref[n] = 0
        prev_ref[SLOTS + n] = TERMS

    for r in range(NX):
        count[r] = 0

    @pl.loop(0, SLOTS)
    def _(slot):
        holder, at = block_place(table[(z * NX + x) * SLOTS + slot])
        pos_ref[slot] = 0
        prev_ref[slot] = TERMS
        r = lax.rem(holder - x + NX, NX)

        @pl.when(r == 0)
        def _():
            prev_ref[slot] = last_ref[at]
            last_ref[at] = slot

        @pl.when(r > 0)
        def _():
            j = count[r]
            count[r] = j + 1

            @pl.when(j < CAP)
            def _():
                pos_ref[slot] = (r - 1) * CAP + j
                back_ref[(r - 1) * CAP + j] = slot

    for r in range(1, NX):
        count[0] = 0

        @pl.loop(0, SLOTS)
        def _(slot):
            holder, at = block_place(table[(z * NX + lax.rem(x + r, NX)) * SLOTS + slot])

            @pl.when(holder == x)
            def _():
                j = count[0]
                count[0] = j + 1

                @pl.when(j < CAP)
                def _():
                    n = (r - 1) * CAP + j
                    at_ref[n] = at
                    prev_ref[SLOTS + n] = last_ref[at]
                    last_ref[at] = SLOTS + n


def make_lists(table):
    smem = pl.BlockSpec(memory_space=pltpu.SMEM)
    vmem = pl.BlockSpec(memory_space=pltpu.VMEM)
    sizes = (3 * CAP, SLOTS, 3 * CAP, TERMS, NZ * 8, 1)
    return pl.pallas_call(
        list_kernel,
        out_shape=tuple(jax.ShapeDtypeStruct((size,), jnp.int32) for size in sizes),
        in_specs=[smem, vmem],
        out_specs=(smem,) * 6,
        scratch_shapes=[pltpu.SMEM((NX,), jnp.int32)],
        name="make_lists",
    )(table.reshape(-1), table)


def layer_kernel(
    table, at_list, pos_list, back_list, prev, last, q_ref, g_ref, k_ref, v_ref,
    att_ref, qg_ref, wacc_ref, out_ref, edge_ref,
    packed, give, kv, halo, wide, window, shared, terms, rim,
    theirs, own, back_packed, arrived, chain, landed, send_buf, recv_buf, give_back,
    pair_sem, halo_send, halo_recv, z_send, z_recv, x_send, x_recv, give_sem,
    back_pair, rim_send, rim_recv, bx_send, bx_recv, bz_send, bz_recv, back_give,
    *bufs,
):
    ag, landing = bufs[:PARTS], bufs[PARTS:]
    me, z, x, c = place()
    other = 1 - c
    sibling = seq_of(z, x, other)
    after = lax.rem(me + 1, NSEQ)
    before = lax.rem(me + NSEQ - 1, NSEQ)
    zs = (seq_of(z + 1, x, c), seq_of(z - 1, x, c))
    xs = tuple(seq_of(z, x + r, c) for r in range(1, NX))
    greet((after, before) + zs + xs)

    def lanes(p):
        return pl.ds(p * PART, PART)

    def columns(p):
        return slice(p * PART, (p + 1) * PART)

    def pair_copy(src, p):
        return remote(
            src.at[:, :, lanes(p)], ag[p].at[pl.ds(z * 8 + c * 4, 4)],
            pair_sem.at[0, p], pair_sem.at[1, p], sibling,
        )

    @pl.when(c == 0)
    def _():
        for p in range(PARTS):
            pair_copy(v_ref, p).start()
        for p in range(PARTS):
            ag[p][pl.ds(z * 8, 4)] = k_ref[:, :, columns(p)]

    @pl.when(c == 1)
    def _():
        for p in range(PARTS):
            pair_copy(k_ref, p).start()
        for p in range(PARTS):
            ag[p][pl.ds(z * 8 + 4, 4)] = v_ref[:, :, columns(p)]

    def z_piece(p, direction, step, half):
        origin = lax.rem(z + NZ - (step - 1), NZ) if direction == 0 else lax.rem(z + step - 1, NZ)
        piece = ag[p].at[pl.ds(origin * 8 + half * 4, 4)]
        return remote(
            piece,
            piece,
            z_send.at[p, direction, step - 1, half],
            z_recv.at[p, direction, step - 1, half],
            zs[direction],
        )

    def z_start(p):
        for direction in range(2):
            z_piece(p, direction, 1, c).start()
        pair_copy(v_ref, p).wait()
        for direction in range(2):
            z_piece(p, direction, 1, other).start()

    def z_step(p, step):
        for half in range(2):
            for direction in range(2):
                if step <= Z_LAST[direction, half]:
                    z_piece(p, direction, step, half).wait_recv()
                    if step + 1 <= Z_LAST[direction, half]:
                        z_piece(p, direction, step + 1, half).start()

    def x_copy(p, r):
        return remote(
            packed.at[p, pl.ds((r - 1) * CAP, CAP)],
            landing[p].at[pl.ds((NX - 1 - r) * CAP, CAP)],
            x_send.at[p, r - 1],
            x_recv.at[p, NX - 1 - r],
            xs[r - 1],
        )

    def x_start(p):
        for r in (2, 1, 3):
            @pl.loop(0, CAP, unroll=3)
            def _(j):
                n = (r - 1) * CAP + j
                packed[p, n] = ag[p][at_list[n]]

            x_copy(p, r).start()

    def chosen(p, slot):
        holder, at = block_place(table[(z * NX + x) * SLOTS + slot])
        return jnp.where(holder == x, ag[p][at], landing[p][pos_list[slot]])

    def handed(p):
        return remote(give.at[p], kv.at[p, c], give_sem.at[0, p], give_sem.at[1, p], sibling)

    def x_finish(p):
        for r in range(1, NX):
            x_copy(p, r).wait_recv()

        @pl.loop(0, REQ, unroll=2)
        def _(i):
            give[p, i] = chosen(p, other * (REQ + 2) + i)

        for i in range(2):
            value = chosen(p, REQ + i)
            give[p, REQ + i] = value
            kv[p, c, REQ + i] = value
        handed(p).start()

        @pl.loop(0, REQ, unroll=2)
        def _(i):
            kv[p, c, i] = chosen(p, c * (REQ + 2) + i)

    halos = []
    for number, ref in enumerate((k_ref, v_ref)):
        for side, (row, target) in enumerate(((BLK_DEV - 1, after), (0, before))):
            halos.append(
                remote(
                    ref.at[row], halo.at[number, side], halo_send.at[number, side],
                    halo_recv.at[number, side], target,
                )
            )

    scale = 1.0 / math.sqrt(HEAD_DIM)
    entry = lax.broadcasted_iota(jnp.int32, (BLK, 8 * BLK), 1) // BLK

    def attend_part(p):
        handed(p).wait()
        for number, ref in enumerate((k_ref, v_ref)):
            wide[number, 0] = halo[number, 0, :, columns(p)]
            wide[number, BLK_DEV + 1] = halo[number, 1, :, columns(p)]
            for i in range(BLK_DEV):
                wide[number, i + 1] = ref[i, :, columns(p)]
        window[...] = jnp.zeros_like(window)
        shared[...] = jnp.zeros_like(shared)

        @pl.loop(0, BLK_DEV)
        def _(b):
            def listed(number):
                return jnp.concatenate(
                    [wide[number, b + i] for i in range(3)]
                    + [kv[p, number, REQ + i] for i in range(2)]
                    + [kv[p, number, 3 * b + i] for i in range(3)],
                    axis=0,
                )

            keys = listed(0)
            values = listed(1)
            query = q_ref[b, :, columns(p)]
            grad = g_ref[b, :, columns(p)]
            low = jnp.where(me * BLK_DEV + b == 0, 0, -1)
            high = jnp.where(me * BLK_DEV + b == NSEQ * BLK_DEV - 1, 2, -1)
            scores = nt(query, keys) * scale
            scores = jnp.where((entry == low) | (entry == high), -jnp.inf, scores)
            row_max = jnp.max(scores, axis=1, keepdims=True)
            raw = jnp.exp(scores - row_max)
            weights = raw * (1.0 / jnp.sum(raw, axis=1, keepdims=True))
            weights_b = weights.astype(jnp.bfloat16)
            weight_grads = nt(grad, values)
            row_dot = jnp.sum(weights_b.astype(jnp.float32) * weight_grads, axis=1, keepdims=True)
            score_grads = (weights * (weight_grads - row_dot) * scale).astype(jnp.bfloat16)
            att_ref[b, :, columns(p)] = nn(weights_b, values).astype(jnp.bfloat16)
            qg_ref[b, :, columns(p)] = nn(score_grads, keys).astype(jnp.bfloat16)
            for number, made in enumerate((tn(score_grads, query), tn(weights_b, grad))):
                for i in range(3):
                    window[number, b + i] += made[i * BLK : (i + 1) * BLK]
                for i in range(2):
                    shared[number, i] += made[(3 + i) * BLK : (4 + i) * BLK]
                for i in range(3):
                    terms[p, number, 3 * b + i] = made[(5 + i) * BLK : (6 + i) * BLK].astype(
                        jnp.bfloat16
                    )

        for number in range(2):
            for i in range(2):
                terms[p, number, REQ + i] = shared[number, i].astype(jnp.bfloat16)
            rim[number, 0, :, columns(p)] = window[number, 0].astype(jnp.bfloat16)
            rim[number, 1, :, columns(p)] = window[number, BLK_DEV + 1].astype(jnp.bfloat16)
            for i in range(BLK_DEV):
                wacc_ref[number, i, :, columns(p)] = window[number, i + 1]
        pair(p).start()

    def pair(p):
        return remote(
            terms.at[p, other], theirs.at[p], back_pair.at[0, p], back_pair.at[1, p], sibling
        )

    def bx_copy(p, r):
        return remote(
            back_packed.at[p, pl.ds((r - 1) * CAP, CAP)],
            arrived.at[p, pl.ds((NX - 1 - r) * CAP, CAP)],
            bx_send.at[p, r - 1],
            bx_recv.at[p, NX - 1 - r],
            xs[r - 1],
        )

    def bx_start(p):
        @pl.loop(0, REQ, unroll=2)
        def _(i):
            own[p, c * (REQ + 2) + i] = terms[p, c, i]

        pair(p).wait_recv()

        @pl.loop(0, REQ, unroll=2)
        def _(i):
            own[p, other * (REQ + 2) + i] = theirs[p, i]

        for i in range(2):
            total = terms[p, c, REQ + i].astype(jnp.float32) + theirs[p, REQ + i].astype(
                jnp.float32
            )
            own[p, REQ + i] = total.astype(jnp.bfloat16)
        for r in (2, 1, 3):
            @pl.loop(0, CAP, unroll=3)
            def _(j):
                n = (r - 1) * CAP + j
                back_packed[p, n] = own[p, back_list[n]]

            bx_copy(p, r).start()

    chain[TERMS] = jnp.zeros((BLK, PART), jnp.float32)

    def land(p):
        @pl.loop(0, SLOTS, unroll=2)
        def _(n):
            chain[n] = own[p, n].astype(jnp.float32) + chain[prev[n]]

        for r in range(1, NX):
            bx_copy(p, r).wait_recv()

        @pl.loop(0, 3 * CAP, unroll=3)
        def _(n):
            chain[SLOTS + n] = arrived[p, n].astype(jnp.float32) + chain[prev[SLOTS + n]]

        @pl.loop(0, NZ * 8, unroll=4)
        def _(at):
            landed[p, at] = chain[last[at]]

    def piece(p, direction, distance, half):
        return remote(
            send_buf.at[p, direction, distance - 1, half],
            recv_buf.at[p, direction, distance - 1, half],
            bz_send.at[p, direction, distance - 1, half],
            bz_recv.at[p, direction, distance - 1, half],
            zs[direction],
        )

    def bz_step(p, distance):
        for half in range(2):
            for direction in range(2):
                if distance > Z_LAST[direction, half]:
                    continue
                target = lax.rem(z + (distance if direction == 0 else NZ - distance), NZ)
                first = target * 8 + half * 4
                waits = distance < Z_LAST[direction, half]
                if waits:
                    piece(p, direction, distance + 1, half).wait_recv()
                for i in range(BLK_DEV):
                    total = landed[p, first + i]
                    if waits:
                        total += recv_buf[p, direction, distance, half, i].astype(jnp.float32)
                    send_buf[p, direction, distance - 1, half, i] = total.astype(jnp.bfloat16)
                piece(p, direction, distance, half).start()

    def handed_back(p):
        return remote(
            give_back.at[p], out_ref.at[c, :, :, lanes(p)], back_give.at[0, p], back_give.at[1, p],
            sibling,
        )

    def bz_finish(p):
        for half in range(2):
            for direction in range(2):
                piece(p, direction, 1, half).wait_recv()

        def finished(half, i):
            total = landed[p, z * 8 + half * 4 + i]
            for direction in range(2):
                total += recv_buf[p, direction, 0, half, i].astype(jnp.float32)
            return total.astype(jnp.bfloat16)

        for i in range(BLK_DEV):
            give_back[p, i] = finished(other, i)
        handed_back(p).start()
        for i in range(BLK_DEV):
            out_ref[c, i, :, columns(p)] = finished(c, i)

    edges = []
    for number in range(2):
        for side, target in enumerate((after, before)):
            edges.append(
                remote(
                    rim.at[number, 1 - side], edge_ref.at[number, side],
                    rim_send.at[number, side], rim_recv.at[number, side], target,
                )
            )

    def turn_of(p, turn):
        step = turn - 2 * p
        if step == 0:
            z_start(p)
        if 1 <= step <= 4:
            z_step(p, step)
        if step == 4:
            x_start(p)
        if step == 7:
            x_finish(p)
        if step == 8:
            if p == 0:
                for copy in halos:
                    copy.wait()
            attend_part(p)
            if p == PARTS - 1:
                for copy in edges:
                    copy.start()
            bx_start(p)
        if step == 12:
            land(p)
        if 12 <= step <= 15:
            bz_step(p, 16 - step)
        if step == 16:
            bz_finish(p)

    for turn in range(2 * PARTS + 15):
        for p in range(PARTS):
            turn_of(p, turn)
        if turn == 3:
            for copy in halos:
                copy.start()

    for copy in edges:
        copy.wait()
    for p in range(PARTS):
        for (direction, half), most in Z_LAST.items():
            for step in range(1, most + 1):
                z_piece(p, direction, step, half).wait_send()
                piece(p, direction, step, half).wait_send()
        for r in range(1, NX):
            x_copy(p, r).wait_send()
            bx_copy(p, r).wait_send()
        pair(p).wait_send()
        handed_back(p).wait()


def layer(table, lists, q, g, k, v):
    features = k.shape[-1]
    vmem = pl.BlockSpec(memory_space=pltpu.VMEM)
    smem = pl.BlockSpec(memory_space=pltpu.SMEM)
    dma = pltpu.SemaphoreType.DMA
    bf16, f32 = jnp.bfloat16, jnp.float32

    def tiles(*lead, dtype=bf16, width=PART):
        return pltpu.VMEM((*lead, BLK, width), dtype)

    ring = tiles(PARTS, 2, 4, 2, BLK_DEV)
    return pl.pallas_call(
        layer_kernel,
        out_shape=(
            jax.ShapeDtypeStruct((BLK_DEV, BLK, features), bf16),
            jax.ShapeDtypeStruct((BLK_DEV, BLK, features), bf16),
            jax.ShapeDtypeStruct((2, BLK_DEV, BLK, features), f32),
            jax.ShapeDtypeStruct((2, BLK_DEV, BLK, features), bf16),
            jax.ShapeDtypeStruct((2, 2, BLK, features), bf16),
        ),
        in_specs=[smem] * 6 + [vmem] * 4,
        out_specs=(vmem,) * 5,
        scratch_shapes=[
            tiles(PARTS, 3 * CAP), tiles(PARTS, REQ + 2), tiles(PARTS, 2, REQ + 2),
            tiles(2, 2, width=features), tiles(2, BLK_DEV + 2),
            tiles(2, BLK_DEV + 2, dtype=f32), tiles(2, 2, dtype=f32),
            tiles(PARTS, 2, REQ + 2), tiles(2, 2, width=features),
            tiles(PARTS, REQ + 2), tiles(PARTS, SLOTS), tiles(PARTS, 3 * CAP),
            tiles(PARTS, 3 * CAP), tiles(TERMS + 1, dtype=f32),
            tiles(PARTS, NZ * 8, dtype=f32), ring, ring, tiles(PARTS, BLK_DEV),
            dma((2, PARTS)), dma((2, 2)), dma((2, 2)), dma((PARTS, 2, 4, 2)), dma((PARTS, 2, 4, 2)),
            dma((PARTS, 3)), dma((PARTS, 3)), dma((2, PARTS)),
            dma((2, PARTS)), dma((2, 2)), dma((2, 2)), dma((PARTS, 3)), dma((PARTS, 3)),
            dma((PARTS, 2, 4, 2)), dma((PARTS, 2, 4, 2)), dma((2, PARTS)),
        ]
        + [tiles(NZ * 8)] * PARTS
        + [tiles(3 * CAP)] * PARTS,
        compiler_params=pltpu.CompilerParams(
            collective_id=2, has_side_effects=True, vmem_limit_bytes=VMEM_LIMIT
        ),
        name="layer",
    )(table, *lists, q, g, k, v)


def per_device(queries, key_rows, value_rows, out_grad, random_blocks, global_blocks):
    row_count, features = queries.shape
    blocks = (BLK_DEV, BLK, features)
    lists = random_blocks.reshape(NZ * NX, NC, REQ)
    shared = jnp.broadcast_to(global_blocks[None], (NZ * NX, 2))
    table = jnp.concatenate([lists[:, 0], shared, lists[:, 1]], axis=1)
    k = key_rows.reshape(blocks)
    v = value_rows.reshape(blocks)
    q = queries.reshape(blocks)
    g = out_grad.reshape(blocks)
    *packed_lists, most = make_lists(table)

    def packed():
        attended, query_grad, *parts = layer(table.reshape(-1), packed_lists, q, g, k, v)
        return attended, query_grad, *joined(*parts)

    def unpacked():
        flat = table.reshape(-1)
        prev, last = plan(flat)
        slots, halo = gather(flat, k, v)
        attended, query_grad, wacc, terms, rims = attend(q, g, k, v, halo, slots)
        total, edges = send_back(prev, last, terms, rims)
        return attended, query_grad, *joined(wacc, total, edges)

    results = lax.cond(most[0] <= CAP, packed, unpacked)
    return tuple(result.reshape(row_count, features) for result in results)


def joined(wacc, total, edges):
    gradient = wacc + total.astype(jnp.float32)
    gradient = gradient.at[:, 0].add(edges[:, 0].astype(jnp.float32))
    gradient = gradient.at[:, BLK_DEV - 1].add(edges[:, 1].astype(jnp.float32))
    gradient = gradient.astype(jnp.bfloat16)
    return gradient[0], gradient[1]


def solution(mesh):
    in_specs = (
        P("seq", "head"),
        P("seq", "head"),
        P("seq", "head"),
        P("seq", "head"),
        P("head", None, None),
        P(),
    )
    out_specs = (P("seq", "head"), P("seq", "head"), P("seq", "head"), P("seq", "head"))
    return jax.shard_map(
        per_device, mesh=mesh, in_specs=in_specs, out_specs=out_specs, check_vma=False
    )
```

```python
import functools
import math

import jax
import jax.numpy as jnp
from jax import lax
from jax.experimental import pallas as pl
from jax.experimental.pallas import tpu as pltpu
from jax.sharding import PartitionSpec as P

HEAD_DIM = 128
BLK = 64
NZ = 8
NX = 4
NC = 2
NSEQ = NZ * NX * NC
BLK_DEV = 4
REQ = 12
SLOTS = 2 * REQ + 2
ENTRIES = NX * SLOTS
PARTS = 4
PART = 128
ROWS = BLK // 2
CAP = 15
TERMS = SLOTS + 3 * CAP
VMEM_LIMIT = 56 * 1024 * 1024


def seq_of(z, x, c):
    return (lax.rem(z + NZ, NZ) * NX + lax.rem(x + NX, NX)) * NC + c


def place():
    me = lax.axis_index("seq")
    z = me // (NX * NC)
    x = lax.rem(me // NC, NX)
    c = lax.rem(me, NC)
    return me, z, x, c


def remote(src, dst, send_sem, recv_sem, target):
    return pltpu.make_async_remote_copy(
        src_ref=src,
        dst_ref=dst,
        send_sem=send_sem,
        recv_sem=recv_sem,
        device_id={"seq": target},
        device_id_type=pl.DeviceIdType.MESH,
    )


def greet(partners):
    barrier = pltpu.get_barrier_semaphore()
    for partner in partners:
        pl.semaphore_signal(
            barrier, inc=1, device_id={"seq": partner}, device_id_type=pl.DeviceIdType.MESH
        )
    pl.semaphore_wait(barrier, len(partners))


def block_place(block):
    return lax.rem(lax.div(block, 8), NX), lax.div(block, 32) * 8 + lax.rem(block, 8)


Z_LAST = {(0, 0): 4, (0, 1): 3, (1, 0): 3, (1, 1): 4}


def gather_kernel(
    table, k_ref, v_ref, out_ref, halo_ref,
    s1_out, s1_in, s2_out, s2_in, s3_out, s3_in, give,
    pair_sem, halo_send, halo_recv, z_send, z_recv, x_send, x_recv, give_sem, *ag,
):
    me, z, x, c = place()
    other = 1 - c
    sibling = seq_of(z, x, other)
    after = lax.rem(me + 1, NSEQ)
    before = lax.rem(me + NSEQ - 1, NSEQ)
    xs = (seq_of(z, x + 1, c), seq_of(z, x - 1, c))
    zs = (seq_of(z + 1, x, c), seq_of(z - 1, x, c))
    greet((after, before, zs[0], zs[1], xs[0], xs[1]))

    def lanes(p):
        return pl.ds(p * PART, PART)

    def pair_copy(src, p):
        return remote(
            src.at[:, :, lanes(p)], ag[p].at[pl.ds(z * 8 + c * 4, 4)],
            pair_sem.at[0, p], pair_sem.at[1, p], sibling,
        )

    @pl.when(c == 0)
    def _():
        for p in range(PARTS):
            pair_copy(v_ref, p).start()
        for p in range(PARTS):
            ag[p][pl.ds(z * 8, 4)] = k_ref[:, :, p * PART : (p + 1) * PART]

    @pl.when(c == 1)
    def _():
        for p in range(PARTS):
            pair_copy(k_ref, p).start()
        for p in range(PARTS):
            ag[p][pl.ds(z * 8 + 4, 4)] = v_ref[:, :, p * PART : (p + 1) * PART]

    def z_piece(p, direction, step, half):
        origin = lax.rem(z + NZ - (step - 1), NZ) if direction == 0 else lax.rem(z + step - 1, NZ)
        piece = ag[p].at[pl.ds(origin * 8 + half * 4, 4)]
        return remote(
            piece,
            piece,
            z_send.at[p, direction, step - 1, half],
            z_recv.at[p, direction, step - 1, half],
            zs[direction],
        )

    def z_start(p):
        for direction in range(2):
            z_piece(p, direction, 1, c).start()
        pair_copy(v_ref, p).wait()
        for direction in range(2):
            z_piece(p, direction, 1, other).start()

    def z_step(p, step):
        for half in range(2):
            for direction in range(2):
                if step <= Z_LAST[direction, half]:
                    z_piece(p, direction, step, half).wait_recv()
                    if step + 1 <= Z_LAST[direction, half]:
                        z_piece(p, direction, step + 1, half).start()

    def wanted(p, chip, slot):
        source, at = block_place(table[(z * NX + lax.rem(chip + NX, NX)) * SLOTS + slot])
        return source, ag[p][at]

    def x_copy(p, number, g):
        src, dst, way = ((s1_out, s1_in, g), (s2_out, s2_in, g), (s3_out, s3_in, 1 - g))[number]
        return remote(
            src.at[p, g], dst.at[p, g], x_send.at[p, number, g], x_recv.at[p, number, g], xs[way]
        )

    def x_first(p):
        @pl.loop(0, SLOTS, unroll=2)
        def _(slot):
            mine = wanted(p, x + 2, slot)[1]
            s1_out[p, 0, slot] = mine[:ROWS]
            s1_out[p, 1, slot] = mine[ROWS:]

        for g in range(2):
            x_copy(p, 0, g).start()

        @pl.loop(0, SLOTS, unroll=2)
        def _(slot):
            s3_out[p, 0, slot] = wanted(p, x - 1, slot)[1][:ROWS]
            s3_out[p, 1, slot] = wanted(p, x + 1, slot)[1][ROWS:]

        for g in range(2):
            x_copy(p, 2, g).start()

    def x_second(p):
        for g in range(2):
            x_copy(p, 0, g).wait_recv()

        @pl.loop(0, SLOTS, unroll=2)
        def _(slot):
            source, mine = wanted(p, x + 1, slot)
            s2_out[p, 0, slot] = jnp.where(source == x, mine[:ROWS], s1_in[p, 0, slot])
            source, mine = wanted(p, x - 1, slot)
            s2_out[p, 1, slot] = jnp.where(source == x, mine[ROWS:], s1_in[p, 1, slot])

        for g in range(2):
            x_copy(p, 1, g).start()

    here = (lax.rem(x + 1, NX), lax.rem(x + NX - 1, NX))

    def chosen(p, slot):
        source, mine = wanted(p, x, slot)
        passed = [
            jnp.where(source == here[g], s3_in[p, g, slot], s2_in[p, g, slot]) for g in range(2)
        ]
        return jnp.where(source == x, mine, jnp.concatenate(passed, axis=0))

    def handed(p):
        return remote(
            give.at[p], out_ref.at[c, :, :, lanes(p)], give_sem.at[0, p], give_sem.at[1, p],
            sibling,
        )

    def finish(p):
        for number in (2, 1):
            for g in range(2):
                x_copy(p, number, g).wait_recv()
        columns = slice(p * PART, (p + 1) * PART)

        @pl.loop(0, REQ, unroll=2)
        def _(i):
            give[p, i] = chosen(p, other * (REQ + 2) + i)

        for i in range(2):
            value = chosen(p, REQ + i)
            give[p, REQ + i] = value
            out_ref[c, REQ + i, :, columns] = value
        handed(p).start()

        @pl.loop(0, REQ, unroll=2)
        def _(i):
            out_ref[c, i, :, columns] = chosen(p, c * (REQ + 2) + i)

    halos = []
    for number, ref in enumerate((k_ref, v_ref)):
        for side, (row, target) in enumerate(((BLK_DEV - 1, after), (0, before))):
            halos.append(
                remote(
                    ref.at[row], halo_ref.at[number, side], halo_send.at[number, side],
                    halo_recv.at[number, side], target,
                )
            )

    z_start(0)
    for step in range(1, 5):
        z_step(0, step)
    if PARTS > 1:
        z_start(1)
    x_first(0)
    for p in range(PARTS):
        more = p + 1 < PARTS
        if more:
            z_step(p + 1, 1)
            z_step(p + 1, 2)
        x_second(p)
        if more:
            z_step(p + 1, 3)
            z_step(p + 1, 4)
            if p + 2 < PARTS:
                z_start(p + 2)
            x_first(p + 1)
        else:
            for copy in halos:
                copy.start()
        finish(p)

    for copy in halos:
        copy.wait()
    for p in range(PARTS):
        for (direction, half), last in Z_LAST.items():
            for step in range(1, last + 1):
                z_piece(p, direction, step, half).wait_send()
        for number in range(3):
            for g in range(2):
                x_copy(p, number, g).wait_send()
        handed(p).wait()


def gather(table, k, v):
    features = k.shape[-1]
    big = pltpu.VMEM((PARTS, 2, SLOTS, ROWS, PART), jnp.bfloat16)
    vmem = pl.BlockSpec(memory_space=pltpu.VMEM)
    smem = pl.BlockSpec(memory_space=pltpu.SMEM)
    dma = pltpu.SemaphoreType.DMA
    return pl.pallas_call(
        gather_kernel,
        out_shape=(
            jax.ShapeDtypeStruct((2, REQ + 2, BLK, features), jnp.bfloat16),
            jax.ShapeDtypeStruct((2, 2, BLK, features), jnp.bfloat16),
        ),
        in_specs=[smem, vmem, vmem],
        out_specs=(vmem, vmem),
        scratch_shapes=[
            big, big, big, big, big, big,
            pltpu.VMEM((PARTS, REQ + 2, BLK, PART), jnp.bfloat16),
            dma((2, PARTS)), dma((2, 2)), dma((2, 2)), dma((PARTS, 2, 4, 2)), dma((PARTS, 2, 4, 2)),
            dma((PARTS, 3, 2)), dma((PARTS, 3, 2)), dma((2, PARTS)),
        ]
        + [pltpu.VMEM((NZ * 8, BLK, PART), jnp.bfloat16)] * PARTS,
        compiler_params=pltpu.CompilerParams(
            collective_id=0, has_side_effects=True, vmem_limit_bytes=VMEM_LIMIT
        ),
        name="gather_blocks",
    )(table, k, v)


def nt(a, b):
    return lax.dot_general(a, b, (((1,), (1,)), ((), ())), preferred_element_type=jnp.float32)


def tn(a, b):
    return lax.dot_general(a, b, (((0,), (0,)), ((), ())), preferred_element_type=jnp.float32)


def nn(a, b):
    return lax.dot_general(a, b, (((1,), (0,)), ((), ())), preferred_element_type=jnp.float32)


def attend_kernel(
    q_ref, g_ref, k_ref, v_ref, halo_ref, slot_ref,
    att_ref, qg_ref, wacc_ref, term_ref, rim_ref, acc, gacc,
):
    me = lax.axis_index("seq")
    features = q_ref.shape[-1]
    heads = features // HEAD_DIM
    scale = 1.0 / math.sqrt(HEAD_DIM)
    lane_head = lax.broadcasted_iota(jnp.int32, (BLK, features), 1) // HEAD_DIM
    acc[...] = jnp.zeros_like(acc)
    gacc[...] = jnp.zeros_like(gacc)

    def spread(rows):
        zero = jnp.zeros_like(rows)
        return jnp.concatenate(
            [jnp.where(lane_head == h, rows, zero) for h in range(heads)], axis=0
        )

    def diagonal(full):
        return jnp.concatenate(
            [
                full[h * BLK : (h + 1) * BLK, h * HEAD_DIM : (h + 1) * HEAD_DIM]
                for h in range(heads)
            ],
            axis=1,
        )

    for b in range(BLK_DEV):
        def listed(number, own):
            window = [
                halo_ref[number, 0] if b == 0 else own[b - 1],
                own[b],
                halo_ref[number, 1] if b == BLK_DEV - 1 else own[b + 1],
            ]
            extra = [slot_ref[number, REQ], slot_ref[number, REQ + 1]]
            random = [slot_ref[number, 3 * b + i] for i in range(3)]
            return jnp.concatenate(window + extra + random, axis=0)

        keys = listed(0, k_ref)
        values = listed(1, v_ref)
        query = spread(q_ref[b])
        grad = spread(g_ref[b])
        scores = nt(keys, query) * scale
        if b == 0:
            scores = jnp.concatenate(
                [jnp.where(me == 0, -jnp.inf, scores[:BLK]), scores[BLK:]], axis=0
            )
        if b == BLK_DEV - 1:
            scores = jnp.concatenate(
                [
                    scores[: 2 * BLK],
                    jnp.where(me == NSEQ - 1, -jnp.inf, scores[2 * BLK : 3 * BLK]),
                    scores[3 * BLK :],
                ],
                axis=0,
            )
        row_max = jnp.max(scores, axis=0, keepdims=True)
        raw = jnp.exp(scores - row_max)
        weights = raw * (1.0 / jnp.sum(raw, axis=0, keepdims=True))
        weights_b = weights.astype(jnp.bfloat16)
        weight_grads = nt(values, grad)
        row_dot = jnp.sum(weights_b.astype(jnp.float32) * weight_grads, axis=0, keepdims=True)
        score_grads = (weights * (weight_grads - row_dot) * scale).astype(jnp.bfloat16)
        att_ref[b] = diagonal(tn(weights_b, values)).astype(jnp.bfloat16)
        qg_ref[b] = diagonal(tn(score_grads, keys)).astype(jnp.bfloat16)
        for number, terms in enumerate((nn(score_grads, query), nn(weights_b, grad))):
            for i in range(3):
                acc[number, b + i] += terms[i * BLK : (i + 1) * BLK]
            for i in range(2):
                gacc[number, i] += terms[(3 + i) * BLK : (4 + i) * BLK]
            for i in range(3):
                term_ref[number, 3 * b + i] = terms[(5 + i) * BLK : (6 + i) * BLK].astype(
                    jnp.bfloat16
                )
    for number in range(2):
        for i in range(2):
            term_ref[number, REQ + i] = gacc[number, i].astype(jnp.bfloat16)
        rim_ref[number, 0] = acc[number, 0].astype(jnp.bfloat16)
        rim_ref[number, 1] = acc[number, BLK_DEV + 1].astype(jnp.bfloat16)
        for i in range(BLK_DEV):
            wacc_ref[number, i] = acc[number, i + 1]


def attend(q, g, k, v, halo, slots):
    features = q.shape[-1]
    vmem = pl.BlockSpec(memory_space=pltpu.VMEM)
    own = jax.ShapeDtypeStruct((BLK_DEV, BLK, features), jnp.bfloat16)
    return pl.pallas_call(
        attend_kernel,
        out_shape=(
            own,
            own,
            jax.ShapeDtypeStruct((2, BLK_DEV, BLK, features), jnp.float32),
            jax.ShapeDtypeStruct((2, REQ + 2, BLK, features), jnp.bfloat16),
            jax.ShapeDtypeStruct((2, 2, BLK, features), jnp.bfloat16),
        ),
        in_specs=[vmem] * 6,
        out_specs=(vmem,) * 5,
        scratch_shapes=[
            pltpu.VMEM((2, BLK_DEV + 2, BLK, features), jnp.float32),
            pltpu.VMEM((2, 2, BLK, features), jnp.float32),
        ],
        compiler_params=pltpu.CompilerParams(vmem_limit_bytes=VMEM_LIMIT),
        name="attend_blocks",
    )(q, g, k, v, halo, slots)


def plan_kernel(table, prev_ref, last_ref):
    me, z, x, c = place()

    @pl.loop(0, NZ * 8)
    def _(at):
        last_ref[at] = ENTRIES

    @pl.loop(0, ENTRIES)
    def _(n):
        source, at = block_place(table[z * ENTRIES + n])
        prev_ref[n] = ENTRIES

        @pl.when(source == x)
        def _():
            prev_ref[n] = last_ref[at]
            last_ref[at] = n


def plan(table):
    smem = pl.BlockSpec(memory_space=pltpu.SMEM)
    return pl.pallas_call(
        plan_kernel,
        out_shape=(
            jax.ShapeDtypeStruct((ENTRIES,), jnp.int32),
            jax.ShapeDtypeStruct((NZ * 8,), jnp.int32),
        ),
        in_specs=[smem],
        out_specs=(smem, smem),
        name="plan_sums",
    )(table)


def back_kernel(
    prev, last, term_ref, rim_ref, out_ref, edge_ref,
    theirs, everything, chain, landed, send_buf, recv_buf, give,
    pair_sem, rim_send, rim_recv, x_send, x_recv, z_send, z_recv, give_sem,
):
    me, z, x, c = place()
    other = 1 - c
    sibling = seq_of(z, x, other)
    after = lax.rem(me + 1, NSEQ)
    before = lax.rem(me + NSEQ - 1, NSEQ)
    xs = (seq_of(z, x + 1, c), seq_of(z, x - 1, c))
    zs = (seq_of(z + 1, x, c), seq_of(z - 1, x, c))
    greet((after, before, xs[0], xs[1], zs[0], zs[1]))

    def lanes(p):
        return pl.ds(p * PART, PART)

    def pair(p):
        return remote(
            term_ref.at[other, :, :, lanes(p)], theirs.at[p], pair_sem.at[0, p],
            pair_sem.at[1, p], sibling,
        )

    for p in range(PARTS):
        pair(p).start()

    def own(p, chip, g):
        base = lax.rem(chip + NX, NX) * SLOTS
        return everything.at[p, pl.ds(base + c * (REQ + 2), REQ), pl.ds(g * ROWS, ROWS)]

    def rest(p, chip, g):
        base = lax.rem(chip + NX, NX) * SLOTS
        return everything.at[p, pl.ds(base + other * REQ, REQ + 2), pl.ds(g * ROWS, ROWS)]

    def send(p, number, chip, which, g):
        ref = (own, rest)[which](p, chip, g)
        return remote(
            ref, ref, x_send.at[p, number, which, g], x_recv.at[p, number, which, g],
            xs[(g, 1 - g, g)[number]],
        )

    def x_first(p):
        columns = slice(p * PART, (p + 1) * PART)
        base = x * SLOTS

        @pl.loop(0, REQ, unroll=2)
        def _(i):
            everything[p, base + c * (REQ + 2) + i] = term_ref[c, i, :, columns]

        for number in range(2):
            for g in range(2):
                send(p, number, x, 0, g).start()
        pair(p).wait_recv()

        @pl.loop(0, REQ, unroll=2)
        def _(i):
            everything[p, base + other * (REQ + 2) + i] = theirs[p, i]

        for i in range(2):
            total = term_ref[c, REQ + i, :, columns].astype(jnp.float32) + theirs[
                p, REQ + i
            ].astype(jnp.float32)
            everything[p, base + REQ + i] = total.astype(jnp.bfloat16)
        for number in range(2):
            for g in range(2):
                send(p, number, x, 1, g).start()

    def x_second(p):
        for which in range(2):
            for g, behind in enumerate((x - 1, x + 1)):
                send(p, 0, behind, which, g).wait_recv()
                send(p, 2, behind, which, g).start()

    def x_wait(p, number):
        for which in range(2):
            for g in range(2):
                send(p, number, x, which, g).wait_recv()

    chain[ENTRIES] = jnp.zeros((BLK, PART), jnp.float32)

    def land(p):
        @pl.loop(0, ENTRIES, unroll=4)
        def _(n):
            chain[n] = everything[p, n].astype(jnp.float32) + chain[prev[n]]

        @pl.loop(0, NZ * 8, unroll=4)
        def _(at):
            landed[p, at] = chain[last[at]]

    def piece(p, direction, distance, half):
        return remote(
            send_buf.at[p, direction, distance - 1, half],
            recv_buf.at[p, direction, distance - 1, half],
            z_send.at[p, direction, distance - 1, half],
            z_recv.at[p, direction, distance - 1, half],
            zs[direction],
        )

    def z_step(p, distance):
        for half in range(2):
            for direction in range(2):
                if distance > Z_LAST[direction, half]:
                    continue
                target = lax.rem(z + (distance if direction == 0 else NZ - distance), NZ)
                first = target * 8 + half * 4
                waits = distance < Z_LAST[direction, half]
                if waits:
                    piece(p, direction, distance + 1, half).wait_recv()
                for i in range(BLK_DEV):
                    total = landed[p, first + i]
                    if waits:
                        total += recv_buf[p, direction, distance, half, i].astype(jnp.float32)
                    send_buf[p, direction, distance - 1, half, i] = total.astype(jnp.bfloat16)
                piece(p, direction, distance, half).start()

    def handed(p):
        return remote(
            give.at[p], out_ref.at[c, :, :, lanes(p)], give_sem.at[0, p], give_sem.at[1, p],
            sibling,
        )

    def finish(p):
        columns = slice(p * PART, (p + 1) * PART)
        for half in range(2):
            for direction in range(2):
                piece(p, direction, 1, half).wait_recv()

        def finished(half, i):
            total = landed[p, z * 8 + half * 4 + i]
            for direction in range(2):
                total += recv_buf[p, direction, 0, half, i].astype(jnp.float32)
            return total.astype(jnp.bfloat16)

        for i in range(BLK_DEV):
            give[p, i] = finished(other, i)
        handed(p).start()
        for i in range(BLK_DEV):
            out_ref[c, i, :, columns] = finished(c, i)

    edges = []
    for number in range(2):
        for side, target in enumerate((after, before)):
            edges.append(
                remote(
                    rim_ref.at[number, 1 - side], edge_ref.at[number, side],
                    rim_send.at[number, side], rim_recv.at[number, side], target,
                )
            )

    x_first(0)
    for p in range(PARTS):
        x_second(p)
        if p + 1 < PARTS:
            x_first(p + 1)
        else:
            for copy in edges:
                copy.start()
        if p:
            z_step(p - 1, 3)
        x_wait(p, 1)
        if p:
            z_step(p - 1, 2)
        x_wait(p, 2)
        if p:
            z_step(p - 1, 1)
        land(p)
        z_step(p, 4)
        if p:
            finish(p - 1)
    for distance in (3, 2, 1):
        z_step(PARTS - 1, distance)
    finish(PARTS - 1)

    for copy in edges:
        copy.wait()
    for p in range(PARTS):
        pair(p).wait_send()
        for number in range(3):
            for which in range(2):
                for g in range(2):
                    send(p, number, x, which, g).wait_send()
        for (direction, half), most in Z_LAST.items():
            for distance in range(1, most + 1):
                piece(p, direction, distance, half).wait_send()
        handed(p).wait()


def send_back(prev, last, terms, rims):
    features = terms.shape[-1]
    vmem = pl.BlockSpec(memory_space=pltpu.VMEM)
    smem = pl.BlockSpec(memory_space=pltpu.SMEM)
    dma = pltpu.SemaphoreType.DMA
    ring = pltpu.VMEM((PARTS, 2, 4, 2, BLK_DEV, BLK, PART), jnp.bfloat16)
    return pl.pallas_call(
        back_kernel,
        out_shape=(
            jax.ShapeDtypeStruct((2, BLK_DEV, BLK, features), jnp.bfloat16),
            jax.ShapeDtypeStruct((2, 2, BLK, features), jnp.bfloat16),
        ),
        in_specs=[smem, smem, vmem, vmem],
        out_specs=(vmem, vmem),
        scratch_shapes=[
            pltpu.VMEM((PARTS, REQ + 2, BLK, PART), jnp.bfloat16),
            pltpu.VMEM((PARTS, ENTRIES, BLK, PART), jnp.bfloat16),
            pltpu.VMEM((ENTRIES + 1, BLK, PART), jnp.float32),
            pltpu.VMEM((PARTS, NZ * 8, BLK, PART), jnp.float32),
            ring, ring,
            pltpu.VMEM((PARTS, BLK_DEV, BLK, PART), jnp.bfloat16),
            dma((2, PARTS)), dma((2, 2)), dma((2, 2)), dma((PARTS, 3, 2, 2)), dma((PARTS, 3, 2, 2)),
            dma((PARTS, 2, 4, 2)), dma((PARTS, 2, 4, 2)), dma((2, PARTS)),
        ],
        compiler_params=pltpu.CompilerParams(
            collective_id=1, has_side_effects=True, vmem_limit_bytes=VMEM_LIMIT
        ),
        name="send_back",
    )(prev, last, terms, rims)


def list_kernel(
    pairs, shared, wide_ref, at_ref, code_ref, back_ref, prev_ref, last_ref, most_ref, count
):
    me, z, x, c = place()

    source = lax.rem(lax.div(wide_ref[...], 8), NX)
    chip = lax.rem(lax.broadcasted_iota(jnp.int32, (NZ * NX, 1), 0), NX)
    holders = [block_place(shared[i])[0] for i in range(2)]
    most = jnp.zeros((NZ * NX, 1), jnp.int32)
    for s in range(NX):
        asked = jnp.sum((source == s).astype(jnp.int32), axis=1, keepdims=True)
        asked += sum((holder == s).astype(jnp.int32) for holder in holders)
        most = jnp.maximum(most, jnp.where(chip == s, 0, asked))
    most_ref[0] = jnp.max(most)

    @pl.loop(0, NZ * 8, unroll=8)
    def _(at):
        last_ref[at] = TERMS

    @pl.loop(0, 3 * CAP, unroll=5)
    def _(n):
        at_ref[n] = 0
        back_ref[n] = 0
        prev_ref[SLOTS + n] = TERMS

    for r in range(NX):
        count[r] = 0

    def visit_all(chip, visit):
        row = z * NX + lax.rem(chip, NX)

        @pl.loop(0, REQ, unroll=2)
        def _(i):
            visit(i, *block_place(pairs[row, i]))

        for i in range(2):
            visit(REQ + i, *block_place(shared[i]))

        @pl.loop(0, REQ, unroll=2)
        def _(i):
            visit(REQ + 2 + i, *block_place(pairs[row, REQ + i]))

    def request(slot, holder, at):
        r = lax.rem(holder - x + NX, NX)
        code_ref[slot] = at
        prev_ref[slot] = TERMS

        @pl.when(r == 0)
        def _():
            prev_ref[slot] = last_ref[at]
            last_ref[at] = slot

        @pl.when(r > 0)
        def _():
            j = count[r]
            count[r] = j + 1

            @pl.when(j < CAP)
            def _():
                code_ref[slot] = NZ * 8 + (r - 1) * CAP + j
                back_ref[(r - 1) * CAP + j] = slot

    visit_all(x, request)
    for r in range(1, NX):
        count[0] = 0

        def serve(slot, holder, at):
            j = count[0]

            @pl.when((holder == x) & (j < CAP))
            def _():
                n = (r - 1) * CAP + j
                count[0] = j + 1
                at_ref[n] = at
                prev_ref[SLOTS + n] = last_ref[at]
                last_ref[at] = SLOTS + n

        visit_all(x + r, serve)


def make_lists(pairs, shared):
    smem = pl.BlockSpec(memory_space=pltpu.SMEM)
    vmem = pl.BlockSpec(memory_space=pltpu.VMEM)
    sizes = (3 * CAP, SLOTS, 3 * CAP, TERMS, NZ * 8, 1)
    return pl.pallas_call(
        list_kernel,
        out_shape=tuple(jax.ShapeDtypeStruct((size,), jnp.int32) for size in sizes),
        in_specs=[smem, smem, vmem],
        out_specs=(smem,) * 6,
        scratch_shapes=[pltpu.SMEM((NX,), jnp.int32)],
        name="make_lists",
    )(pairs, shared, pairs)


ORDER = (
    ("z_start", 0), ("z_start", 1), ("z1", 0), ("z2", 0), ("z3", 0),
    ("z4", 0), ("z1", 1), ("x_start", 0), ("z2", 1), ("z3", 1),
    ("z4", 1), ("x_start", 1), ("z_start", 2), ("z_start", 3), ("x_finish", 0),
    ("attend", 0), ("z1", 3), ("back_x", 0), ("z2", 3), ("z3", 3),
    ("x_finish", 1), ("z4", 3), ("z1", 2), ("x_start", 3), ("land", 0),
    ("z2", 2), ("attend", 1), ("back_x", 1), ("b4", 0), ("z3", 2),
    ("b3", 0), ("x_finish", 3), ("attend", 3), ("z4", 2), ("x_start", 2),
    ("b2", 0), ("b1", 0), ("land", 1), ("b4", 1), ("back_x", 3),
    ("finish", 0), ("b3", 1), ("b2", 1), ("x_finish", 2), ("attend", 2),
    ("back_x", 2), ("b1", 1), ("land", 3), ("b4", 3), ("b3", 3),
    ("b2", 3), ("land", 2), ("b4", 2), ("b3", 2), ("finish", 1),
    ("b1", 3), ("b2", 2), ("finish", 3), ("b1", 2), ("finish", 2),
)


def layer_kernel(
    at_list, code_list, back_list, prev, last, q_ref, g_ref, k_ref, v_ref,
    att_ref, qg_ref, wacc_ref, out_ref, edge_ref,
    packed, give, kv, halo, wide, window, shared, terms, rim,
    theirs, own, back_packed, arrived, chain, landed, send_buf, recv_buf, give_back,
    pair_sem, halo_send, halo_recv, z_send, z_recv, x_send, x_recv, give_sem,
    back_pair, rim_send, rim_recv, bx_send, bx_recv, bz_send, bz_recv, back_give,
    *bufs,
):
    ag, landing = bufs[:PARTS], bufs[PARTS:]
    me, z, x, c = place()
    other = 1 - c
    sibling = seq_of(z, x, other)
    after = lax.rem(me + 1, NSEQ)
    before = lax.rem(me + NSEQ - 1, NSEQ)
    zs = (seq_of(z + 1, x, c), seq_of(z - 1, x, c))
    xs = tuple(seq_of(z, x + r, c) for r in range(1, NX))
    greet((after, before) + zs + xs)

    def lanes(p):
        return pl.ds(p * PART, PART)

    def columns(p):
        return slice(p * PART, (p + 1) * PART)

    def pair_copy(src, p):
        return remote(
            src.at[:, :, lanes(p)], ag[p].at[pl.ds(z * 8 + c * 4, 4)],
            pair_sem.at[0, p], pair_sem.at[1, p], sibling,
        )

    @pl.when(c == 0)
    def _():
        for p in range(PARTS):
            pair_copy(v_ref, p).start()
        for p in range(PARTS):
            ag[p][pl.ds(z * 8, 4)] = k_ref[:, :, columns(p)]

    @pl.when(c == 1)
    def _():
        for p in range(PARTS):
            pair_copy(k_ref, p).start()
        for p in range(PARTS):
            ag[p][pl.ds(z * 8 + 4, 4)] = v_ref[:, :, columns(p)]

    def z_piece(p, direction, step, half):
        origin = lax.rem(z + NZ - (step - 1), NZ) if direction == 0 else lax.rem(z + step - 1, NZ)
        piece = ag[p].at[pl.ds(origin * 8 + half * 4, 4)]
        return remote(
            piece,
            piece,
            z_send.at[p, direction, step - 1, half],
            z_recv.at[p, direction, step - 1, half],
            zs[direction],
        )

    def z_start(p):
        for direction in range(2):
            z_piece(p, direction, 1, c).start()
        pair_copy(v_ref, p).wait()
        for direction in range(2):
            z_piece(p, direction, 1, other).start()

    def z_step(p, step):
        for half in range(2):
            for direction in range(2):
                if step <= Z_LAST[direction, half]:
                    z_piece(p, direction, step, half).wait_recv()
                    if step + 1 <= Z_LAST[direction, half]:
                        z_piece(p, direction, step + 1, half).start()

    def x_copy(p, r):
        return remote(
            packed.at[p, pl.ds((r - 1) * CAP, CAP)],
            landing[p].at[pl.ds((NX - 1 - r) * CAP, CAP)],
            x_send.at[p, r - 1],
            x_recv.at[p, NX - 1 - r],
            xs[r - 1],
        )

    def x_start(p):
        for r in (2, 1, 3):
            @pl.loop(0, CAP, unroll=3)
            def _(j):
                n = (r - 1) * CAP + j
                packed[p, n] = ag[p][at_list[n]]

            x_copy(p, r).start()

    def chosen(p, slot):
        code = code_list[slot]
        held = ag[p][jnp.minimum(code, NZ * 8 - 1)]
        return jnp.where(code < NZ * 8, held, landing[p][jnp.maximum(code - NZ * 8, 0)])

    def handed(p):
        return remote(give.at[p], kv.at[p, c], give_sem.at[0, p], give_sem.at[1, p], sibling)

    def x_finish(p):
        for r in range(1, NX):
            x_copy(p, r).wait_recv()

        @pl.loop(0, REQ, unroll=2)
        def _(i):
            give[p, i] = chosen(p, other * (REQ + 2) + i)

        for i in range(2):
            value = chosen(p, REQ + i)
            give[p, REQ + i] = value
            kv[p, c, REQ + i] = value
        handed(p).start()

        @pl.loop(0, REQ, unroll=2)
        def _(i):
            kv[p, c, i] = chosen(p, c * (REQ + 2) + i)

    halos = []
    for number, ref in enumerate((k_ref, v_ref)):
        for side, (row, target) in enumerate(((BLK_DEV - 1, after), (0, before))):
            halos.append(
                remote(
                    ref.at[row], halo.at[number, side], halo_send.at[number, side],
                    halo_recv.at[number, side], target,
                )
            )

    scale = 1.0 / math.sqrt(HEAD_DIM)
    entry = lax.broadcasted_iota(jnp.int32, (BLK, 8 * BLK), 1) // BLK

    def attend_part(p):
        handed(p).wait()
        for number, ref in enumerate((k_ref, v_ref)):
            wide[number, 0] = halo[number, 0, :, columns(p)]
            wide[number, BLK_DEV + 1] = halo[number, 1, :, columns(p)]
            for i in range(BLK_DEV):
                wide[number, i + 1] = ref[i, :, columns(p)]
        window[...] = jnp.zeros_like(window)
        shared[...] = jnp.zeros_like(shared)

        @pl.loop(0, BLK_DEV)
        def _(b):
            def listed(number):
                return jnp.concatenate(
                    [wide[number, b + i] for i in range(3)]
                    + [kv[p, number, REQ + i] for i in range(2)]
                    + [kv[p, number, 3 * b + i] for i in range(3)],
                    axis=0,
                )

            keys = listed(0)
            values = listed(1)
            query = q_ref[b, :, columns(p)]
            grad = g_ref[b, :, columns(p)]
            low = jnp.where(me * BLK_DEV + b == 0, 0, -1)
            high = jnp.where(me * BLK_DEV + b == NSEQ * BLK_DEV - 1, 2, -1)
            scores = nt(query, keys) * scale
            scores = jnp.where((entry == low) | (entry == high), -jnp.inf, scores)
            row_max = jnp.max(scores, axis=1, keepdims=True)
            raw = jnp.exp(scores - row_max)
            weights = raw * (1.0 / jnp.sum(raw, axis=1, keepdims=True))
            weights_b = weights.astype(jnp.bfloat16)
            weight_grads = nt(grad, values)
            row_dot = jnp.sum(weights_b.astype(jnp.float32) * weight_grads, axis=1, keepdims=True)
            score_grads = (weights * (weight_grads - row_dot) * scale).astype(jnp.bfloat16)
            att_ref[b, :, columns(p)] = nn(weights_b, values).astype(jnp.bfloat16)
            qg_ref[b, :, columns(p)] = nn(score_grads, keys).astype(jnp.bfloat16)
            for number, made in enumerate((tn(score_grads, query), tn(weights_b, grad))):
                for i in range(3):
                    window[number, b + i] += made[i * BLK : (i + 1) * BLK]
                for i in range(2):
                    shared[number, i] += made[(3 + i) * BLK : (4 + i) * BLK]
                for i in range(3):
                    terms[p, number, 3 * b + i] = made[(5 + i) * BLK : (6 + i) * BLK].astype(
                        jnp.bfloat16
                    )

        for number in range(2):
            for i in range(2):
                terms[p, number, REQ + i] = shared[number, i].astype(jnp.bfloat16)
            rim[number, 0, :, columns(p)] = window[number, 0].astype(jnp.bfloat16)
            rim[number, 1, :, columns(p)] = window[number, BLK_DEV + 1].astype(jnp.bfloat16)
            for i in range(BLK_DEV):
                wacc_ref[number, i, :, columns(p)] = window[number, i + 1]
        pair(p).start()

    def pair(p):
        return remote(
            terms.at[p, other], theirs.at[p], back_pair.at[0, p], back_pair.at[1, p], sibling
        )

    def bx_copy(p, r):
        return remote(
            back_packed.at[p, pl.ds((r - 1) * CAP, CAP)],
            arrived.at[p, pl.ds((NX - 1 - r) * CAP, CAP)],
            bx_send.at[p, r - 1],
            bx_recv.at[p, NX - 1 - r],
            xs[r - 1],
        )

    def bx_start(p):
        @pl.loop(0, REQ, unroll=2)
        def _(i):
            own[p, c * (REQ + 2) + i] = terms[p, c, i]

        pair(p).wait_recv()

        @pl.loop(0, REQ, unroll=2)
        def _(i):
            own[p, other * (REQ + 2) + i] = theirs[p, i]

        for i in range(2):
            total = terms[p, c, REQ + i].astype(jnp.float32) + theirs[p, REQ + i].astype(
                jnp.float32
            )
            own[p, REQ + i] = total.astype(jnp.bfloat16)
        for r in (2, 1, 3):
            @pl.loop(0, CAP, unroll=3)
            def _(j):
                n = (r - 1) * CAP + j
                back_packed[p, n] = own[p, back_list[n]]

            bx_copy(p, r).start()

    chain[TERMS] = jnp.zeros((BLK, PART), jnp.float32)

    def land(p):
        @pl.loop(0, SLOTS, unroll=2)
        def _(n):
            chain[n] = own[p, n].astype(jnp.float32) + chain[prev[n]]

        for r in range(1, NX):
            bx_copy(p, r).wait_recv()

        @pl.loop(0, 3 * CAP, unroll=3)
        def _(n):
            chain[SLOTS + n] = arrived[p, n].astype(jnp.float32) + chain[prev[SLOTS + n]]

        @pl.loop(0, NZ * 8, unroll=4)
        def _(at):
            landed[p, at] = chain[last[at]]

    def piece(p, direction, distance, half):
        return remote(
            send_buf.at[p, direction, distance - 1, half],
            recv_buf.at[p, direction, distance - 1, half],
            bz_send.at[p, direction, distance - 1, half],
            bz_recv.at[p, direction, distance - 1, half],
            zs[direction],
        )

    def bz_step(p, distance):
        for half in range(2):
            for direction in range(2):
                if distance > Z_LAST[direction, half]:
                    continue
                target = lax.rem(z + (distance if direction == 0 else NZ - distance), NZ)
                first = target * 8 + half * 4
                waits = distance < Z_LAST[direction, half]
                if waits:
                    piece(p, direction, distance + 1, half).wait_recv()
                for i in range(BLK_DEV):
                    total = landed[p, first + i]
                    if waits:
                        total += recv_buf[p, direction, distance, half, i].astype(jnp.float32)
                    send_buf[p, direction, distance - 1, half, i] = total.astype(jnp.bfloat16)
                piece(p, direction, distance, half).start()

    def handed_back(p):
        return remote(
            give_back.at[p], out_ref.at[c, :, :, lanes(p)], back_give.at[0, p], back_give.at[1, p],
            sibling,
        )

    def bz_finish(p):
        for half in range(2):
            for direction in range(2):
                piece(p, direction, 1, half).wait_recv()

        def finished(half, i):
            total = landed[p, z * 8 + half * 4 + i]
            for direction in range(2):
                total += recv_buf[p, direction, 0, half, i].astype(jnp.float32)
            return total.astype(jnp.bfloat16)

        for i in range(BLK_DEV):
            give_back[p, i] = finished(other, i)
        handed_back(p).start()
        for i in range(BLK_DEV):
            out_ref[c, i, :, columns(p)] = finished(c, i)

    edges = []
    for number in range(2):
        for side, target in enumerate((after, before)):
            edges.append(
                remote(
                    rim.at[number, 1 - side], edge_ref.at[number, side],
                    rim_send.at[number, side], rim_recv.at[number, side], target,
                )
            )

    steps = {
        "z_start": z_start,
        "x_start": x_start,
        "x_finish": x_finish,
        "attend": attend_part,
        "back_x": bx_start,
        "land": land,
        "finish": bz_finish,
    }
    for i in range(1, 5):
        steps[f"z{i}"] = functools.partial(z_step, step=i)
        steps[f"b{i}"] = functools.partial(bz_step, distance=i)
    attended = 0
    for number, (name, p) in enumerate(ORDER):
        if name == "attend" and not attended:
            for copy in halos:
                copy.wait()
        steps[name](p)
        if number == 2:
            for copy in halos:
                copy.start()
        if name == "attend":
            attended += 1
            if attended == PARTS:
                for copy in edges:
                    copy.start()

    for copy in edges:
        copy.wait()
    for p in range(PARTS):
        for (direction, half), most in Z_LAST.items():
            for step in range(1, most + 1):
                z_piece(p, direction, step, half).wait_send()
                piece(p, direction, step, half).wait_send()
        for r in range(1, NX):
            x_copy(p, r).wait_send()
            bx_copy(p, r).wait_send()
        pair(p).wait_send()
        handed_back(p).wait()


def layer(lists, q, g, k, v):
    features = k.shape[-1]
    vmem = pl.BlockSpec(memory_space=pltpu.VMEM)
    smem = pl.BlockSpec(memory_space=pltpu.SMEM)
    dma = pltpu.SemaphoreType.DMA
    bf16, f32 = jnp.bfloat16, jnp.float32

    def tiles(*lead, dtype=bf16, width=PART):
        return pltpu.VMEM((*lead, BLK, width), dtype)

    ring = tiles(PARTS, 2, 4, 2, BLK_DEV)
    return pl.pallas_call(
        layer_kernel,
        out_shape=(
            jax.ShapeDtypeStruct((BLK_DEV, BLK, features), bf16),
            jax.ShapeDtypeStruct((BLK_DEV, BLK, features), bf16),
            jax.ShapeDtypeStruct((2, BLK_DEV, BLK, features), f32),
            jax.ShapeDtypeStruct((2, BLK_DEV, BLK, features), bf16),
            jax.ShapeDtypeStruct((2, 2, BLK, features), bf16),
        ),
        in_specs=[smem] * 5 + [vmem] * 4,
        out_specs=(vmem,) * 5,
        scratch_shapes=[
            tiles(PARTS, 3 * CAP), tiles(PARTS, REQ + 2), tiles(PARTS, 2, REQ + 2),
            tiles(2, 2, width=features), tiles(2, BLK_DEV + 2),
            tiles(2, BLK_DEV + 2, dtype=f32), tiles(2, 2, dtype=f32),
            tiles(PARTS, 2, REQ + 2), tiles(2, 2, width=features),
            tiles(PARTS, REQ + 2), tiles(PARTS, SLOTS), tiles(PARTS, 3 * CAP),
            tiles(PARTS, 3 * CAP), tiles(TERMS + 1, dtype=f32),
            tiles(PARTS, NZ * 8, dtype=f32), ring, ring, tiles(PARTS, BLK_DEV),
            dma((2, PARTS)), dma((2, 2)), dma((2, 2)), dma((PARTS, 2, 4, 2)), dma((PARTS, 2, 4, 2)),
            dma((PARTS, 3)), dma((PARTS, 3)), dma((2, PARTS)),
            dma((2, PARTS)), dma((2, 2)), dma((2, 2)), dma((PARTS, 3)), dma((PARTS, 3)),
            dma((PARTS, 2, 4, 2)), dma((PARTS, 2, 4, 2)), dma((2, PARTS)),
        ]
        + [tiles(NZ * 8)] * PARTS
        + [tiles(3 * CAP)] * PARTS,
        compiler_params=pltpu.CompilerParams(
            collective_id=2, has_side_effects=True, vmem_limit_bytes=VMEM_LIMIT
        ),
        name="layer",
    )(*lists, q, g, k, v)


def per_device(queries, key_rows, value_rows, out_grad, random_blocks, global_blocks):
    row_count, features = queries.shape
    blocks = (BLK_DEV, BLK, features)
    k = key_rows.reshape(blocks)
    v = value_rows.reshape(blocks)
    q = queries.reshape(blocks)
    g = out_grad.reshape(blocks)
    *packed_lists, most = make_lists(random_blocks.reshape(NZ * NX, 2 * REQ), global_blocks)

    def packed():
        attended, query_grad, *parts = layer(packed_lists, q, g, k, v)
        return attended, query_grad, *joined(*parts)

    def unpacked():
        lists = random_blocks.reshape(NZ * NX, NC, REQ)
        shared = jnp.broadcast_to(global_blocks[None], (NZ * NX, 2))
        flat = jnp.concatenate([lists[:, 0], shared, lists[:, 1]], axis=1).reshape(-1)
        prev, last = plan(flat)
        slots, halo = gather(flat, k, v)
        attended, query_grad, wacc, terms, rims = attend(q, g, k, v, halo, slots)
        total, edges = send_back(prev, last, terms, rims)
        return attended, query_grad, *joined(wacc, total, edges)

    results = lax.cond(most[0] <= CAP, packed, unpacked)
    return tuple(result.reshape(row_count, features) for result in results)


def joined(wacc, total, edges):
    gradient = wacc + total.astype(jnp.float32)
    gradient = gradient.at[:, 0].add(edges[:, 0].astype(jnp.float32))
    gradient = gradient.at[:, BLK_DEV - 1].add(edges[:, 1].astype(jnp.float32))
    gradient = gradient.astype(jnp.bfloat16)
    return gradient[0], gradient[1]


def solution(mesh):
    in_specs = (
        P("seq", "head"),
        P("seq", "head"),
        P("seq", "head"),
        P("seq", "head"),
        P("head", None, None),
        P(),
    )
    out_specs = (P("seq", "head"), P("seq", "head"), P("seq", "head"), P("seq", "head"))
    return jax.shard_map(
        per_device, mesh=mesh, in_specs=in_specs, out_specs=out_specs, check_vma=False
    )
```

```python
import functools
import math

import jax
import jax.numpy as jnp
from jax import lax
from jax.experimental import pallas as pl
from jax.experimental.pallas import tpu as pltpu
from jax.sharding import PartitionSpec as P

HEAD_DIM = 128
BLK = 64
NZ = 8
NX = 4
NC = 2
NSEQ = NZ * NX * NC
BLK_DEV = 4
REQ = 12
SLOTS = 2 * REQ + 2
ENTRIES = NX * SLOTS
PARTS = 4
PART = 128
ROWS = BLK // 2
CAP = 15
TERMS = SLOTS + 3 * CAP
VMEM_LIMIT = 56 * 1024 * 1024


def seq_of(z, x, c):
    return (lax.rem(z + NZ, NZ) * NX + lax.rem(x + NX, NX)) * NC + c


def place():
    me = lax.axis_index("seq")
    z = me // (NX * NC)
    x = lax.rem(me // NC, NX)
    c = lax.rem(me, NC)
    return me, z, x, c


def remote(src, dst, send_sem, recv_sem, target):
    return pltpu.make_async_remote_copy(
        src_ref=src,
        dst_ref=dst,
        send_sem=send_sem,
        recv_sem=recv_sem,
        device_id={"seq": target},
        device_id_type=pl.DeviceIdType.MESH,
    )


def greet(partners):
    barrier = pltpu.get_barrier_semaphore()
    for partner in partners:
        pl.semaphore_signal(
            barrier, inc=1, device_id={"seq": partner}, device_id_type=pl.DeviceIdType.MESH
        )
    pl.semaphore_wait(barrier, len(partners))


def block_place(block):
    return lax.rem(lax.div(block, 8), NX), lax.div(block, 32) * 8 + lax.rem(block, 8)


Z_LAST = {(0, 0): 4, (0, 1): 3, (1, 0): 3, (1, 1): 4}


def gather_kernel(
    table, k_ref, v_ref, out_ref, halo_ref,
    s1_out, s1_in, s2_out, s2_in, s3_out, s3_in, give,
    pair_sem, halo_send, halo_recv, z_send, z_recv, x_send, x_recv, give_sem, *ag,
):
    me, z, x, c = place()
    other = 1 - c
    sibling = seq_of(z, x, other)
    after = lax.rem(me + 1, NSEQ)
    before = lax.rem(me + NSEQ - 1, NSEQ)
    xs = (seq_of(z, x + 1, c), seq_of(z, x - 1, c))
    zs = (seq_of(z + 1, x, c), seq_of(z - 1, x, c))
    greet((after, before, zs[0], zs[1], xs[0], xs[1]))

    def lanes(p):
        return pl.ds(p * PART, PART)

    def pair_copy(src, p):
        return remote(
            src.at[:, :, lanes(p)], ag[p].at[pl.ds(z * 8 + c * 4, 4)],
            pair_sem.at[0, p], pair_sem.at[1, p], sibling,
        )

    @pl.when(c == 0)
    def _():
        for p in range(PARTS):
            pair_copy(v_ref, p).start()
        for p in range(PARTS):
            ag[p][pl.ds(z * 8, 4)] = k_ref[:, :, p * PART : (p + 1) * PART]

    @pl.when(c == 1)
    def _():
        for p in range(PARTS):
            pair_copy(k_ref, p).start()
        for p in range(PARTS):
            ag[p][pl.ds(z * 8 + 4, 4)] = v_ref[:, :, p * PART : (p + 1) * PART]

    def z_piece(p, direction, step, half):
        origin = lax.rem(z + NZ - (step - 1), NZ) if direction == 0 else lax.rem(z + step - 1, NZ)
        piece = ag[p].at[pl.ds(origin * 8 + half * 4, 4)]
        return remote(
            piece,
            piece,
            z_send.at[p, direction, step - 1, half],
            z_recv.at[p, direction, step - 1, half],
            zs[direction],
        )

    def z_start(p):
        for direction in range(2):
            z_piece(p, direction, 1, c).start()
        pair_copy(v_ref, p).wait()
        for direction in range(2):
            z_piece(p, direction, 1, other).start()

    def z_step(p, step):
        for half in range(2):
            for direction in range(2):
                if step <= Z_LAST[direction, half]:
                    z_piece(p, direction, step, half).wait_recv()
                    if step + 1 <= Z_LAST[direction, half]:
                        z_piece(p, direction, step + 1, half).start()

    def wanted(p, chip, slot):
        source, at = block_place(table[(z * NX + lax.rem(chip + NX, NX)) * SLOTS + slot])
        return source, ag[p][at]

    def x_copy(p, number, g):
        src, dst, way = ((s1_out, s1_in, g), (s2_out, s2_in, g), (s3_out, s3_in, 1 - g))[number]
        return remote(
            src.at[p, g], dst.at[p, g], x_send.at[p, number, g], x_recv.at[p, number, g], xs[way]
        )

    def x_first(p):
        @pl.loop(0, SLOTS, unroll=2)
        def _(slot):
            mine = wanted(p, x + 2, slot)[1]
            s1_out[p, 0, slot] = mine[:ROWS]
            s1_out[p, 1, slot] = mine[ROWS:]

        for g in range(2):
            x_copy(p, 0, g).start()

        @pl.loop(0, SLOTS, unroll=2)
        def _(slot):
            s3_out[p, 0, slot] = wanted(p, x - 1, slot)[1][:ROWS]
            s3_out[p, 1, slot] = wanted(p, x + 1, slot)[1][ROWS:]

        for g in range(2):
            x_copy(p, 2, g).start()

    def x_second(p):
        for g in range(2):
            x_copy(p, 0, g).wait_recv()

        @pl.loop(0, SLOTS, unroll=2)
        def _(slot):
            source, mine = wanted(p, x + 1, slot)
            s2_out[p, 0, slot] = jnp.where(source == x, mine[:ROWS], s1_in[p, 0, slot])
            source, mine = wanted(p, x - 1, slot)
            s2_out[p, 1, slot] = jnp.where(source == x, mine[ROWS:], s1_in[p, 1, slot])

        for g in range(2):
            x_copy(p, 1, g).start()

    here = (lax.rem(x + 1, NX), lax.rem(x + NX - 1, NX))

    def chosen(p, slot):
        source, mine = wanted(p, x, slot)
        passed = [
            jnp.where(source == here[g], s3_in[p, g, slot], s2_in[p, g, slot]) for g in range(2)
        ]
        return jnp.where(source == x, mine, jnp.concatenate(passed, axis=0))

    def handed(p):
        return remote(
            give.at[p], out_ref.at[c, :, :, lanes(p)], give_sem.at[0, p], give_sem.at[1, p],
            sibling,
        )

    def finish(p):
        for number in (2, 1):
            for g in range(2):
                x_copy(p, number, g).wait_recv()
        columns = slice(p * PART, (p + 1) * PART)

        @pl.loop(0, REQ, unroll=2)
        def _(i):
            give[p, i] = chosen(p, other * (REQ + 2) + i)

        for i in range(2):
            value = chosen(p, REQ + i)
            give[p, REQ + i] = value
            out_ref[c, REQ + i, :, columns] = value
        handed(p).start()

        @pl.loop(0, REQ, unroll=2)
        def _(i):
            out_ref[c, i, :, columns] = chosen(p, c * (REQ + 2) + i)

    halos = []
    for number, ref in enumerate((k_ref, v_ref)):
        for side, (row, target) in enumerate(((BLK_DEV - 1, after), (0, before))):
            halos.append(
                remote(
                    ref.at[row], halo_ref.at[number, side], halo_send.at[number, side],
                    halo_recv.at[number, side], target,
                )
            )

    z_start(0)
    for step in range(1, 5):
        z_step(0, step)
    if PARTS > 1:
        z_start(1)
    x_first(0)
    for p in range(PARTS):
        more = p + 1 < PARTS
        if more:
            z_step(p + 1, 1)
            z_step(p + 1, 2)
        x_second(p)
        if more:
            z_step(p + 1, 3)
            z_step(p + 1, 4)
            if p + 2 < PARTS:
                z_start(p + 2)
            x_first(p + 1)
        else:
            for copy in halos:
                copy.start()
        finish(p)

    for copy in halos:
        copy.wait()
    for p in range(PARTS):
        for (direction, half), last in Z_LAST.items():
            for step in range(1, last + 1):
                z_piece(p, direction, step, half).wait_send()
        for number in range(3):
            for g in range(2):
                x_copy(p, number, g).wait_send()
        handed(p).wait()


def gather(table, k, v):
    features = k.shape[-1]
    big = pltpu.VMEM((PARTS, 2, SLOTS, ROWS, PART), jnp.bfloat16)
    vmem = pl.BlockSpec(memory_space=pltpu.VMEM)
    smem = pl.BlockSpec(memory_space=pltpu.SMEM)
    dma = pltpu.SemaphoreType.DMA
    return pl.pallas_call(
        gather_kernel,
        out_shape=(
            jax.ShapeDtypeStruct((2, REQ + 2, BLK, features), jnp.bfloat16),
            jax.ShapeDtypeStruct((2, 2, BLK, features), jnp.bfloat16),
        ),
        in_specs=[smem, vmem, vmem],
        out_specs=(vmem, vmem),
        scratch_shapes=[
            big, big, big, big, big, big,
            pltpu.VMEM((PARTS, REQ + 2, BLK, PART), jnp.bfloat16),
            dma((2, PARTS)), dma((2, 2)), dma((2, 2)), dma((PARTS, 2, 4, 2)), dma((PARTS, 2, 4, 2)),
            dma((PARTS, 3, 2)), dma((PARTS, 3, 2)), dma((2, PARTS)),
        ]
        + [pltpu.VMEM((NZ * 8, BLK, PART), jnp.bfloat16)] * PARTS,
        compiler_params=pltpu.CompilerParams(
            collective_id=0, has_side_effects=True, vmem_limit_bytes=VMEM_LIMIT
        ),
        name="gather_blocks",
    )(table, k, v)


def nt(a, b):
    return lax.dot_general(a, b, (((1,), (1,)), ((), ())), preferred_element_type=jnp.float32)


def tn(a, b):
    return lax.dot_general(a, b, (((0,), (0,)), ((), ())), preferred_element_type=jnp.float32)


def nn(a, b):
    return lax.dot_general(a, b, (((1,), (0,)), ((), ())), preferred_element_type=jnp.float32)


def attend_kernel(
    q_ref, g_ref, k_ref, v_ref, halo_ref, slot_ref,
    att_ref, qg_ref, wacc_ref, term_ref, rim_ref, acc, gacc,
):
    me = lax.axis_index("seq")
    features = q_ref.shape[-1]
    heads = features // HEAD_DIM
    scale = 1.0 / math.sqrt(HEAD_DIM)
    lane_head = lax.broadcasted_iota(jnp.int32, (BLK, features), 1) // HEAD_DIM
    acc[...] = jnp.zeros_like(acc)
    gacc[...] = jnp.zeros_like(gacc)

    def spread(rows):
        zero = jnp.zeros_like(rows)
        return jnp.concatenate(
            [jnp.where(lane_head == h, rows, zero) for h in range(heads)], axis=0
        )

    def diagonal(full):
        return jnp.concatenate(
            [
                full[h * BLK : (h + 1) * BLK, h * HEAD_DIM : (h + 1) * HEAD_DIM]
                for h in range(heads)
            ],
            axis=1,
        )

    for b in range(BLK_DEV):
        def listed(number, own):
            window = [
                halo_ref[number, 0] if b == 0 else own[b - 1],
                own[b],
                halo_ref[number, 1] if b == BLK_DEV - 1 else own[b + 1],
            ]
            extra = [slot_ref[number, REQ], slot_ref[number, REQ + 1]]
            random = [slot_ref[number, 3 * b + i] for i in range(3)]
            return jnp.concatenate(window + extra + random, axis=0)

        keys = listed(0, k_ref)
        values = listed(1, v_ref)
        query = spread(q_ref[b])
        grad = spread(g_ref[b])
        scores = nt(keys, query) * scale
        if b == 0:
            scores = jnp.concatenate(
                [jnp.where(me == 0, -jnp.inf, scores[:BLK]), scores[BLK:]], axis=0
            )
        if b == BLK_DEV - 1:
            scores = jnp.concatenate(
                [
                    scores[: 2 * BLK],
                    jnp.where(me == NSEQ - 1, -jnp.inf, scores[2 * BLK : 3 * BLK]),
                    scores[3 * BLK :],
                ],
                axis=0,
            )
        row_max = jnp.max(scores, axis=0, keepdims=True)
        raw = jnp.exp(scores - row_max)
        weights = raw * (1.0 / jnp.sum(raw, axis=0, keepdims=True))
        weights_b = weights.astype(jnp.bfloat16)
        weight_grads = nt(values, grad)
        row_dot = jnp.sum(weights_b.astype(jnp.float32) * weight_grads, axis=0, keepdims=True)
        score_grads = (weights * (weight_grads - row_dot) * scale).astype(jnp.bfloat16)
        att_ref[b] = diagonal(tn(weights_b, values)).astype(jnp.bfloat16)
        qg_ref[b] = diagonal(tn(score_grads, keys)).astype(jnp.bfloat16)
        for number, terms in enumerate((nn(score_grads, query), nn(weights_b, grad))):
            for i in range(3):
                acc[number, b + i] += terms[i * BLK : (i + 1) * BLK]
            for i in range(2):
                gacc[number, i] += terms[(3 + i) * BLK : (4 + i) * BLK]
            for i in range(3):
                term_ref[number, 3 * b + i] = terms[(5 + i) * BLK : (6 + i) * BLK].astype(
                    jnp.bfloat16
                )
    for number in range(2):
        for i in range(2):
            term_ref[number, REQ + i] = gacc[number, i].astype(jnp.bfloat16)
        rim_ref[number, 0] = acc[number, 0].astype(jnp.bfloat16)
        rim_ref[number, 1] = acc[number, BLK_DEV + 1].astype(jnp.bfloat16)
        for i in range(BLK_DEV):
            wacc_ref[number, i] = acc[number, i + 1]


def attend(q, g, k, v, halo, slots):
    features = q.shape[-1]
    vmem = pl.BlockSpec(memory_space=pltpu.VMEM)
    own = jax.ShapeDtypeStruct((BLK_DEV, BLK, features), jnp.bfloat16)
    return pl.pallas_call(
        attend_kernel,
        out_shape=(
            own,
            own,
            jax.ShapeDtypeStruct((2, BLK_DEV, BLK, features), jnp.float32),
            jax.ShapeDtypeStruct((2, REQ + 2, BLK, features), jnp.bfloat16),
            jax.ShapeDtypeStruct((2, 2, BLK, features), jnp.bfloat16),
        ),
        in_specs=[vmem] * 6,
        out_specs=(vmem,) * 5,
        scratch_shapes=[
            pltpu.VMEM((2, BLK_DEV + 2, BLK, features), jnp.float32),
            pltpu.VMEM((2, 2, BLK, features), jnp.float32),
        ],
        compiler_params=pltpu.CompilerParams(vmem_limit_bytes=VMEM_LIMIT),
        name="attend_blocks",
    )(q, g, k, v, halo, slots)


def plan_kernel(table, prev_ref, last_ref):
    me, z, x, c = place()

    @pl.loop(0, NZ * 8)
    def _(at):
        last_ref[at] = ENTRIES

    @pl.loop(0, ENTRIES)
    def _(n):
        source, at = block_place(table[z * ENTRIES + n])
        prev_ref[n] = ENTRIES

        @pl.when(source == x)
        def _():
            prev_ref[n] = last_ref[at]
            last_ref[at] = n


def plan(table):
    smem = pl.BlockSpec(memory_space=pltpu.SMEM)
    return pl.pallas_call(
        plan_kernel,
        out_shape=(
            jax.ShapeDtypeStruct((ENTRIES,), jnp.int32),
            jax.ShapeDtypeStruct((NZ * 8,), jnp.int32),
        ),
        in_specs=[smem],
        out_specs=(smem, smem),
        name="plan_sums",
    )(table)


def back_kernel(
    prev, last, term_ref, rim_ref, out_ref, edge_ref,
    theirs, everything, chain, landed, send_buf, recv_buf, give,
    pair_sem, rim_send, rim_recv, x_send, x_recv, z_send, z_recv, give_sem,
):
    me, z, x, c = place()
    other = 1 - c
    sibling = seq_of(z, x, other)
    after = lax.rem(me + 1, NSEQ)
    before = lax.rem(me + NSEQ - 1, NSEQ)
    xs = (seq_of(z, x + 1, c), seq_of(z, x - 1, c))
    zs = (seq_of(z + 1, x, c), seq_of(z - 1, x, c))
    greet((after, before, xs[0], xs[1], zs[0], zs[1]))

    def lanes(p):
        return pl.ds(p * PART, PART)

    def pair(p):
        return remote(
            term_ref.at[other, :, :, lanes(p)], theirs.at[p], pair_sem.at[0, p],
            pair_sem.at[1, p], sibling,
        )

    for p in range(PARTS):
        pair(p).start()

    def own(p, chip, g):
        base = lax.rem(chip + NX, NX) * SLOTS
        return everything.at[p, pl.ds(base + c * (REQ + 2), REQ), pl.ds(g * ROWS, ROWS)]

    def rest(p, chip, g):
        base = lax.rem(chip + NX, NX) * SLOTS
        return everything.at[p, pl.ds(base + other * REQ, REQ + 2), pl.ds(g * ROWS, ROWS)]

    def send(p, number, chip, which, g):
        ref = (own, rest)[which](p, chip, g)
        return remote(
            ref, ref, x_send.at[p, number, which, g], x_recv.at[p, number, which, g],
            xs[(g, 1 - g, g)[number]],
        )

    def x_first(p):
        columns = slice(p * PART, (p + 1) * PART)
        base = x * SLOTS

        @pl.loop(0, REQ, unroll=2)
        def _(i):
            everything[p, base + c * (REQ + 2) + i] = term_ref[c, i, :, columns]

        for number in range(2):
            for g in range(2):
                send(p, number, x, 0, g).start()
        pair(p).wait_recv()

        @pl.loop(0, REQ, unroll=2)
        def _(i):
            everything[p, base + other * (REQ + 2) + i] = theirs[p, i]

        for i in range(2):
            total = term_ref[c, REQ + i, :, columns].astype(jnp.float32) + theirs[
                p, REQ + i
            ].astype(jnp.float32)
            everything[p, base + REQ + i] = total.astype(jnp.bfloat16)
        for number in range(2):
            for g in range(2):
                send(p, number, x, 1, g).start()

    def x_second(p):
        for which in range(2):
            for g, behind in enumerate((x - 1, x + 1)):
                send(p, 0, behind, which, g).wait_recv()
                send(p, 2, behind, which, g).start()

    def x_wait(p, number):
        for which in range(2):
            for g in range(2):
                send(p, number, x, which, g).wait_recv()

    chain[ENTRIES] = jnp.zeros((BLK, PART), jnp.float32)

    def land(p):
        @pl.loop(0, ENTRIES, unroll=4)
        def _(n):
            chain[n] = everything[p, n].astype(jnp.float32) + chain[prev[n]]

        @pl.loop(0, NZ * 8, unroll=4)
        def _(at):
            landed[p, at] = chain[last[at]]

    def piece(p, direction, distance, half):
        return remote(
            send_buf.at[p, direction, distance - 1, half],
            recv_buf.at[p, direction, distance - 1, half],
            z_send.at[p, direction, distance - 1, half],
            z_recv.at[p, direction, distance - 1, half],
            zs[direction],
        )

    def z_step(p, distance):
        for half in range(2):
            for direction in range(2):
                if distance > Z_LAST[direction, half]:
                    continue
                target = lax.rem(z + (distance if direction == 0 else NZ - distance), NZ)
                first = target * 8 + half * 4
                waits = distance < Z_LAST[direction, half]
                if waits:
                    piece(p, direction, distance + 1, half).wait_recv()
                for i in range(BLK_DEV):
                    total = landed[p, first + i]
                    if waits:
                        total += recv_buf[p, direction, distance, half, i].astype(jnp.float32)
                    send_buf[p, direction, distance - 1, half, i] = total.astype(jnp.bfloat16)
                piece(p, direction, distance, half).start()

    def handed(p):
        return remote(
            give.at[p], out_ref.at[c, :, :, lanes(p)], give_sem.at[0, p], give_sem.at[1, p],
            sibling,
        )

    def finish(p):
        columns = slice(p * PART, (p + 1) * PART)
        for half in range(2):
            for direction in range(2):
                piece(p, direction, 1, half).wait_recv()

        def finished(half, i):
            total = landed[p, z * 8 + half * 4 + i]
            for direction in range(2):
                total += recv_buf[p, direction, 0, half, i].astype(jnp.float32)
            return total.astype(jnp.bfloat16)

        for i in range(BLK_DEV):
            give[p, i] = finished(other, i)
        handed(p).start()
        for i in range(BLK_DEV):
            out_ref[c, i, :, columns] = finished(c, i)

    edges = []
    for number in range(2):
        for side, target in enumerate((after, before)):
            edges.append(
                remote(
                    rim_ref.at[number, 1 - side], edge_ref.at[number, side],
                    rim_send.at[number, side], rim_recv.at[number, side], target,
                )
            )

    x_first(0)
    for p in range(PARTS):
        x_second(p)
        if p + 1 < PARTS:
            x_first(p + 1)
        else:
            for copy in edges:
                copy.start()
        if p:
            z_step(p - 1, 3)
        x_wait(p, 1)
        if p:
            z_step(p - 1, 2)
        x_wait(p, 2)
        if p:
            z_step(p - 1, 1)
        land(p)
        z_step(p, 4)
        if p:
            finish(p - 1)
    for distance in (3, 2, 1):
        z_step(PARTS - 1, distance)
    finish(PARTS - 1)

    for copy in edges:
        copy.wait()
    for p in range(PARTS):
        pair(p).wait_send()
        for number in range(3):
            for which in range(2):
                for g in range(2):
                    send(p, number, x, which, g).wait_send()
        for (direction, half), most in Z_LAST.items():
            for distance in range(1, most + 1):
                piece(p, direction, distance, half).wait_send()
        handed(p).wait()


def send_back(prev, last, terms, rims):
    features = terms.shape[-1]
    vmem = pl.BlockSpec(memory_space=pltpu.VMEM)
    smem = pl.BlockSpec(memory_space=pltpu.SMEM)
    dma = pltpu.SemaphoreType.DMA
    ring = pltpu.VMEM((PARTS, 2, 4, 2, BLK_DEV, BLK, PART), jnp.bfloat16)
    return pl.pallas_call(
        back_kernel,
        out_shape=(
            jax.ShapeDtypeStruct((2, BLK_DEV, BLK, features), jnp.bfloat16),
            jax.ShapeDtypeStruct((2, 2, BLK, features), jnp.bfloat16),
        ),
        in_specs=[smem, smem, vmem, vmem],
        out_specs=(vmem, vmem),
        scratch_shapes=[
            pltpu.VMEM((PARTS, REQ + 2, BLK, PART), jnp.bfloat16),
            pltpu.VMEM((PARTS, ENTRIES, BLK, PART), jnp.bfloat16),
            pltpu.VMEM((ENTRIES + 1, BLK, PART), jnp.float32),
            pltpu.VMEM((PARTS, NZ * 8, BLK, PART), jnp.float32),
            ring, ring,
            pltpu.VMEM((PARTS, BLK_DEV, BLK, PART), jnp.bfloat16),
            dma((2, PARTS)), dma((2, 2)), dma((2, 2)), dma((PARTS, 3, 2, 2)), dma((PARTS, 3, 2, 2)),
            dma((PARTS, 2, 4, 2)), dma((PARTS, 2, 4, 2)), dma((2, PARTS)),
        ],
        compiler_params=pltpu.CompilerParams(
            collective_id=1, has_side_effects=True, vmem_limit_bytes=VMEM_LIMIT
        ),
        name="send_back",
    )(prev, last, terms, rims)


def list_kernel(
    pairs, shared, wide_ref, at_ref, code_ref, back_ref, prev_ref, last_ref, most_ref, count
):
    me, z, x, c = place()

    source = lax.rem(lax.div(wide_ref[...], 8), NX)
    chip = lax.rem(lax.broadcasted_iota(jnp.int32, (NZ * NX, 1), 0), NX)
    holders = [block_place(shared[i])[0] for i in range(2)]
    most = jnp.zeros((NZ * NX, 1), jnp.int32)
    for s in range(NX):
        asked = jnp.sum((source == s).astype(jnp.int32), axis=1, keepdims=True)
        asked += sum((holder == s).astype(jnp.int32) for holder in holders)
        most = jnp.maximum(most, jnp.where(chip == s, 0, asked))
    most_ref[0] = jnp.max(most)

    @pl.loop(0, NZ * 8, unroll=8)
    def _(at):
        last_ref[at] = TERMS

    @pl.loop(0, 3 * CAP, unroll=5)
    def _(n):
        at_ref[n] = 0
        back_ref[n] = 0
        prev_ref[SLOTS + n] = TERMS

    for r in range(NX):
        count[r] = 0

    def visit_all(chip, visit):
        row = z * NX + lax.rem(chip, NX)

        @pl.loop(0, REQ, unroll=2)
        def _(i):
            visit(i, *block_place(pairs[row, i]))

        for i in range(2):
            visit(REQ + i, *block_place(shared[i]))

        @pl.loop(0, REQ, unroll=2)
        def _(i):
            visit(REQ + 2 + i, *block_place(pairs[row, REQ + i]))

    def request(slot, holder, at):
        r = lax.rem(holder - x + NX, NX)
        code_ref[slot] = at
        prev_ref[slot] = TERMS

        @pl.when(r == 0)
        def _():
            prev_ref[slot] = last_ref[at]
            last_ref[at] = slot

        @pl.when(r > 0)
        def _():
            j = count[r]
            count[r] = j + 1

            @pl.when(j < CAP)
            def _():
                code_ref[slot] = NZ * 8 + (r - 1) * CAP + j
                back_ref[(r - 1) * CAP + j] = slot

    visit_all(x, request)
    for r in range(1, NX):
        count[0] = 0

        def serve(slot, holder, at):
            j = count[0]

            @pl.when((holder == x) & (j < CAP))
            def _():
                n = (r - 1) * CAP + j
                count[0] = j + 1
                at_ref[n] = at
                prev_ref[SLOTS + n] = last_ref[at]
                last_ref[at] = SLOTS + n

        visit_all(x + r, serve)


def make_lists(pairs, shared):
    smem = pl.BlockSpec(memory_space=pltpu.SMEM)
    vmem = pl.BlockSpec(memory_space=pltpu.VMEM)
    sizes = (3 * CAP, SLOTS, 3 * CAP, TERMS, NZ * 8, 1)
    return pl.pallas_call(
        list_kernel,
        out_shape=tuple(jax.ShapeDtypeStruct((size,), jnp.int32) for size in sizes),
        in_specs=[smem, smem, vmem],
        out_specs=(smem,) * 6,
        scratch_shapes=[pltpu.SMEM((NX,), jnp.int32)],
        name="make_lists",
    )(pairs, shared, pairs)


ORDER = (
    ("z_start", 0), ("z_start", 1), ("z1", 0), ("z2", 0), ("z1", 1),
    ("z3", 0), ("z4", 0), ("x_start", 0), ("z2", 1), ("z_start", 2),
    ("z3", 1), ("z1", 2), ("z4", 1), ("z_start", 3), ("x_start", 1),
    ("x_finish", 0), ("attend", 0), ("z2", 2), ("back_x", 0), ("z1", 3),
    ("z3", 2), ("z2", 3), ("z4", 2), ("x_start", 2), ("x_finish", 1),
    ("z3", 3), ("land", 0), ("attend", 1), ("z4", 3), ("back_x", 1),
    ("b4", 0), ("x_start", 3), ("x_finish", 2), ("attend", 2), ("back_x", 2),
    ("b3", 0), ("land", 1), ("b4", 1), ("b2", 0), ("b3", 1),
    ("b2", 1), ("x_finish", 3), ("b1", 0), ("attend", 3), ("b1", 1),
    ("back_x", 3), ("land", 2), ("finish", 0), ("b4", 2), ("b3", 2),
    ("b2", 2), ("land", 3), ("b4", 3), ("b1", 2), ("b3", 3),
    ("b2", 3), ("finish", 2), ("finish", 1), ("b1", 3), ("finish", 3),
)


def layer_kernel(
    at_list, code_list, back_list, prev, last, q_ref, g_ref, k_ref, v_ref,
    att_ref, qg_ref, wacc_ref, out_ref, edge_ref,
    packed, give, kv, halo, wide, window, shared, terms, rim,
    theirs, own, back_packed, arrived, chain, landed, send_buf, recv_buf, give_back,
    pair_sem, halo_send, halo_recv, z_send, z_recv, x_send, x_recv, give_sem,
    back_pair, rim_send, rim_recv, bx_send, bx_recv, bz_send, bz_recv, back_give,
    *bufs,
):
    ag, landing = bufs[:PARTS], bufs[PARTS:]
    me, z, x, c = place()
    other = 1 - c
    sibling = seq_of(z, x, other)
    after = lax.rem(me + 1, NSEQ)
    before = lax.rem(me + NSEQ - 1, NSEQ)
    zs = (seq_of(z + 1, x, c), seq_of(z - 1, x, c))
    xs = tuple(seq_of(z, x + r, c) for r in range(1, NX))
    greet((after, before) + zs + xs)

    def lanes(p):
        return pl.ds(p * PART, PART)

    def columns(p):
        return slice(p * PART, (p + 1) * PART)

    def pair_copy(src, p):
        return remote(
            src.at[:, :, lanes(p)], ag[p].at[pl.ds(z * 8 + c * 4, 4)],
            pair_sem.at[0, p], pair_sem.at[1, p], sibling,
        )

    @pl.when(c == 0)
    def _():
        for p in range(PARTS):
            pair_copy(v_ref, p).start()
        for p in range(PARTS):
            ag[p][pl.ds(z * 8, 4)] = k_ref[:, :, columns(p)]

    @pl.when(c == 1)
    def _():
        for p in range(PARTS):
            pair_copy(k_ref, p).start()
        for p in range(PARTS):
            ag[p][pl.ds(z * 8 + 4, 4)] = v_ref[:, :, columns(p)]

    def z_piece(p, direction, step, half):
        origin = lax.rem(z + NZ - (step - 1), NZ) if direction == 0 else lax.rem(z + step - 1, NZ)
        piece = ag[p].at[pl.ds(origin * 8 + half * 4, 4)]
        return remote(
            piece,
            piece,
            z_send.at[p, direction, step - 1, half],
            z_recv.at[p, direction, step - 1, half],
            zs[direction],
        )

    def z_start(p):
        for direction in range(2):
            z_piece(p, direction, 1, c).start()
        pair_copy(v_ref, p).wait()
        for direction in range(2):
            z_piece(p, direction, 1, other).start()

    def z_step(p, step):
        for half in range(2):
            for direction in range(2):
                if step <= Z_LAST[direction, half]:
                    z_piece(p, direction, step, half).wait_recv()
                    if step + 1 <= Z_LAST[direction, half]:
                        z_piece(p, direction, step + 1, half).start()

    def x_copy(p, r):
        return remote(
            packed.at[p, pl.ds((r - 1) * CAP, CAP)],
            landing[p].at[pl.ds((NX - 1 - r) * CAP, CAP)],
            x_send.at[p, r - 1],
            x_recv.at[p, NX - 1 - r],
            xs[r - 1],
        )

    def x_start(p):
        for r in (2, 1, 3):
            @pl.loop(0, CAP, unroll=3)
            def _(j):
                n = (r - 1) * CAP + j
                packed[p, n] = ag[p][at_list[n]]

            x_copy(p, r).start()

    def chosen(p, slot):
        code = code_list[slot]
        held = ag[p][jnp.minimum(code, NZ * 8 - 1)]
        return jnp.where(code < NZ * 8, held, landing[p][jnp.maximum(code - NZ * 8, 0)])

    def handed(p):
        return remote(give.at[p], kv.at[p, c], give_sem.at[0, p], give_sem.at[1, p], sibling)

    def x_finish(p):
        for r in range(1, NX):
            x_copy(p, r).wait_recv()

        @pl.loop(0, REQ, unroll=2)
        def _(i):
            give[p, i] = chosen(p, other * (REQ + 2) + i)

        for i in range(2):
            value = chosen(p, REQ + i)
            give[p, REQ + i] = value
            kv[p, c, REQ + i] = value
        handed(p).start()

        @pl.loop(0, REQ, unroll=2)
        def _(i):
            kv[p, c, i] = chosen(p, c * (REQ + 2) + i)

    halos = []
    for number, ref in enumerate((k_ref, v_ref)):
        for side, (row, target) in enumerate(((BLK_DEV - 1, after), (0, before))):
            halos.append(
                remote(
                    ref.at[row], halo.at[number, side], halo_send.at[number, side],
                    halo_recv.at[number, side], target,
                )
            )

    scale = 1.0 / math.sqrt(HEAD_DIM)
    entry = lax.broadcasted_iota(jnp.int32, (BLK, 8 * BLK), 1) // BLK

    def attend_part(p):
        handed(p).wait()
        for number, ref in enumerate((k_ref, v_ref)):
            wide[number, 0] = halo[number, 0, :, columns(p)]
            wide[number, BLK_DEV + 1] = halo[number, 1, :, columns(p)]
            for i in range(BLK_DEV):
                wide[number, i + 1] = ref[i, :, columns(p)]
        window[...] = jnp.zeros_like(window)
        shared[...] = jnp.zeros_like(shared)

        @pl.loop(0, BLK_DEV)
        def _(b):
            def listed(number):
                return jnp.concatenate(
                    [wide[number, b + i] for i in range(3)]
                    + [kv[p, number, REQ + i] for i in range(2)]
                    + [kv[p, number, 3 * b + i] for i in range(3)],
                    axis=0,
                )

            keys = listed(0)
            values = listed(1)
            query = q_ref[b, :, columns(p)]
            grad = g_ref[b, :, columns(p)]
            low = jnp.where(me * BLK_DEV + b == 0, 0, -1)
            high = jnp.where(me * BLK_DEV + b == NSEQ * BLK_DEV - 1, 2, -1)
            scores = nt(query, keys) * scale
            scores = jnp.where((entry == low) | (entry == high), -jnp.inf, scores)
            row_max = jnp.max(scores, axis=1, keepdims=True)
            raw = jnp.exp(scores - row_max)
            weights = raw * (1.0 / jnp.sum(raw, axis=1, keepdims=True))
            weights_b = weights.astype(jnp.bfloat16)
            weight_grads = nt(grad, values)
            row_dot = jnp.sum(weights_b.astype(jnp.float32) * weight_grads, axis=1, keepdims=True)
            score_grads = (weights * (weight_grads - row_dot) * scale).astype(jnp.bfloat16)
            att_ref[b, :, columns(p)] = nn(weights_b, values).astype(jnp.bfloat16)
            qg_ref[b, :, columns(p)] = nn(score_grads, keys).astype(jnp.bfloat16)
            for number, made in enumerate((tn(score_grads, query), tn(weights_b, grad))):
                for i in range(3):
                    window[number, b + i] += made[i * BLK : (i + 1) * BLK]
                for i in range(2):
                    shared[number, i] += made[(3 + i) * BLK : (4 + i) * BLK]
                for i in range(3):
                    terms[p, number, 3 * b + i] = made[(5 + i) * BLK : (6 + i) * BLK].astype(
                        jnp.bfloat16
                    )

        for number in range(2):
            for i in range(2):
                terms[p, number, REQ + i] = shared[number, i].astype(jnp.bfloat16)
            rim[number, 0, :, columns(p)] = window[number, 0].astype(jnp.bfloat16)
            rim[number, 1, :, columns(p)] = window[number, BLK_DEV + 1].astype(jnp.bfloat16)
            for i in range(BLK_DEV):
                wacc_ref[number, i, :, columns(p)] = window[number, i + 1]
        pair(p).start()

    def pair(p):
        return remote(
            terms.at[p, other], theirs.at[p], back_pair.at[0, p], back_pair.at[1, p], sibling
        )

    def bx_copy(p, r):
        return remote(
            back_packed.at[p, pl.ds((r - 1) * CAP, CAP)],
            arrived.at[p, pl.ds((NX - 1 - r) * CAP, CAP)],
            bx_send.at[p, r - 1],
            bx_recv.at[p, NX - 1 - r],
            xs[r - 1],
        )

    def bx_start(p):
        @pl.loop(0, REQ, unroll=2)
        def _(i):
            own[p, c * (REQ + 2) + i] = terms[p, c, i]

        pair(p).wait_recv()

        @pl.loop(0, REQ, unroll=2)
        def _(i):
            own[p, other * (REQ + 2) + i] = theirs[p, i]

        for i in range(2):
            total = terms[p, c, REQ + i].astype(jnp.float32) + theirs[p, REQ + i].astype(
                jnp.float32
            )
            own[p, REQ + i] = total.astype(jnp.bfloat16)
        for r in (2, 1, 3):
            @pl.loop(0, CAP, unroll=3)
            def _(j):
                n = (r - 1) * CAP + j
                back_packed[p, n] = own[p, back_list[n]]

            bx_copy(p, r).start()

    chain[TERMS] = jnp.zeros((BLK, PART), jnp.float32)

    def land(p):
        @pl.loop(0, SLOTS, unroll=2)
        def _(n):
            chain[n] = own[p, n].astype(jnp.float32) + chain[prev[n]]

        for r in range(1, NX):
            bx_copy(p, r).wait_recv()

        @pl.loop(0, 3 * CAP, unroll=3)
        def _(n):
            chain[SLOTS + n] = arrived[p, n].astype(jnp.float32) + chain[prev[SLOTS + n]]

        @pl.loop(0, NZ * 8, unroll=4)
        def _(at):
            landed[p, at] = chain[last[at]]

    def piece(p, direction, distance, half):
        return remote(
            send_buf.at[p, direction, distance - 1, half],
            recv_buf.at[p, direction, distance - 1, half],
            bz_send.at[p, direction, distance - 1, half],
            bz_recv.at[p, direction, distance - 1, half],
            zs[direction],
        )

    def bz_step(p, distance):
        for half in range(2):
            for direction in range(2):
                if distance > Z_LAST[direction, half]:
                    continue
                target = lax.rem(z + (distance if direction == 0 else NZ - distance), NZ)
                first = target * 8 + half * 4
                waits = distance < Z_LAST[direction, half]
                if waits:
                    piece(p, direction, distance + 1, half).wait_recv()
                for i in range(BLK_DEV):
                    total = landed[p, first + i]
                    if waits:
                        total += recv_buf[p, direction, distance, half, i].astype(jnp.float32)
                    send_buf[p, direction, distance - 1, half, i] = total.astype(jnp.bfloat16)
                piece(p, direction, distance, half).start()

    def handed_back(p):
        return remote(
            give_back.at[p], out_ref.at[c, :, :, lanes(p)], back_give.at[0, p], back_give.at[1, p],
            sibling,
        )

    def bz_finish(p):
        for half in range(2):
            for direction in range(2):
                piece(p, direction, 1, half).wait_recv()

        def finished(half, i):
            total = landed[p, z * 8 + half * 4 + i]
            for direction in range(2):
                total += recv_buf[p, direction, 0, half, i].astype(jnp.float32)
            return total.astype(jnp.bfloat16)

        for i in range(BLK_DEV):
            give_back[p, i] = finished(other, i)
        handed_back(p).start()
        for i in range(BLK_DEV):
            out_ref[c, i, :, columns(p)] = finished(c, i)

    edges = []
    for number in range(2):
        for side, target in enumerate((after, before)):
            edges.append(
                remote(
                    rim.at[number, 1 - side], edge_ref.at[number, side],
                    rim_send.at[number, side], rim_recv.at[number, side], target,
                )
            )

    steps = {
        "z_start": z_start,
        "x_start": x_start,
        "x_finish": x_finish,
        "attend": attend_part,
        "back_x": bx_start,
        "land": land,
        "finish": bz_finish,
    }
    for i in range(1, 5):
        steps[f"z{i}"] = functools.partial(z_step, step=i)
        steps[f"b{i}"] = functools.partial(bz_step, distance=i)
    attended = 0
    for number, (name, p) in enumerate(ORDER):
        if name == "attend" and not attended:
            for copy in halos:
                copy.wait()
        steps[name](p)
        if number == 2:
            for copy in halos:
                copy.start()
        if name == "attend":
            attended += 1
            if attended == PARTS:
                for copy in edges:
                    copy.start()

    for copy in edges:
        copy.wait()
    for p in range(PARTS):
        for (direction, half), most in Z_LAST.items():
            for step in range(1, most + 1):
                z_piece(p, direction, step, half).wait_send()
                piece(p, direction, step, half).wait_send()
        for r in range(1, NX):
            x_copy(p, r).wait_send()
            bx_copy(p, r).wait_send()
        pair(p).wait_send()
        handed_back(p).wait()


def layer(lists, q, g, k, v):
    features = k.shape[-1]
    vmem = pl.BlockSpec(memory_space=pltpu.VMEM)
    smem = pl.BlockSpec(memory_space=pltpu.SMEM)
    dma = pltpu.SemaphoreType.DMA
    bf16, f32 = jnp.bfloat16, jnp.float32

    def tiles(*lead, dtype=bf16, width=PART):
        return pltpu.VMEM((*lead, BLK, width), dtype)

    ring = tiles(PARTS, 2, 4, 2, BLK_DEV)
    return pl.pallas_call(
        layer_kernel,
        out_shape=(
            jax.ShapeDtypeStruct((BLK_DEV, BLK, features), bf16),
            jax.ShapeDtypeStruct((BLK_DEV, BLK, features), bf16),
            jax.ShapeDtypeStruct((2, BLK_DEV, BLK, features), f32),
            jax.ShapeDtypeStruct((2, BLK_DEV, BLK, features), bf16),
            jax.ShapeDtypeStruct((2, 2, BLK, features), bf16),
        ),
        in_specs=[smem] * 5 + [vmem] * 4,
        out_specs=(vmem,) * 5,
        scratch_shapes=[
            tiles(PARTS, 3 * CAP), tiles(PARTS, REQ + 2), tiles(PARTS, 2, REQ + 2),
            tiles(2, 2, width=features), tiles(2, BLK_DEV + 2),
            tiles(2, BLK_DEV + 2, dtype=f32), tiles(2, 2, dtype=f32),
            tiles(PARTS, 2, REQ + 2), tiles(2, 2, width=features),
            tiles(PARTS, REQ + 2), tiles(PARTS, SLOTS), tiles(PARTS, 3 * CAP),
            tiles(PARTS, 3 * CAP), tiles(TERMS + 1, dtype=f32),
            tiles(PARTS, NZ * 8, dtype=f32), ring, ring, tiles(PARTS, BLK_DEV),
            dma((2, PARTS)), dma((2, 2)), dma((2, 2)), dma((PARTS, 2, 4, 2)), dma((PARTS, 2, 4, 2)),
            dma((PARTS, 3)), dma((PARTS, 3)), dma((2, PARTS)),
            dma((2, PARTS)), dma((2, 2)), dma((2, 2)), dma((PARTS, 3)), dma((PARTS, 3)),
            dma((PARTS, 2, 4, 2)), dma((PARTS, 2, 4, 2)), dma((2, PARTS)),
        ]
        + [tiles(NZ * 8)] * PARTS
        + [tiles(3 * CAP)] * PARTS,
        compiler_params=pltpu.CompilerParams(
            collective_id=2, has_side_effects=True, vmem_limit_bytes=VMEM_LIMIT
        ),
        name="layer",
    )(*lists, q, g, k, v)


def per_device(queries, key_rows, value_rows, out_grad, random_blocks, global_blocks):
    row_count, features = queries.shape
    blocks = (BLK_DEV, BLK, features)
    k = key_rows.reshape(blocks)
    v = value_rows.reshape(blocks)
    q = queries.reshape(blocks)
    g = out_grad.reshape(blocks)
    *packed_lists, most = make_lists(random_blocks.reshape(NZ * NX, 2 * REQ), global_blocks)

    def packed():
        attended, query_grad, *parts = layer(packed_lists, q, g, k, v)
        return attended, query_grad, *joined(*parts)

    def unpacked():
        lists = random_blocks.reshape(NZ * NX, NC, REQ)
        shared = jnp.broadcast_to(global_blocks[None], (NZ * NX, 2))
        flat = jnp.concatenate([lists[:, 0], shared, lists[:, 1]], axis=1).reshape(-1)
        prev, last = plan(flat)
        slots, halo = gather(flat, k, v)
        attended, query_grad, wacc, terms, rims = attend(q, g, k, v, halo, slots)
        total, edges = send_back(prev, last, terms, rims)
        return attended, query_grad, *joined(wacc, total, edges)

    results = lax.cond(most[0] <= CAP, packed, unpacked)
    return tuple(result.reshape(row_count, features) for result in results)


def joined(wacc, total, edges):
    gradient = wacc + total.astype(jnp.float32)
    gradient = gradient.at[:, 0].add(edges[:, 0].astype(jnp.float32))
    gradient = gradient.at[:, BLK_DEV - 1].add(edges[:, 1].astype(jnp.float32))
    gradient = gradient.astype(jnp.bfloat16)
    return gradient[0], gradient[1]


def solution(mesh):
    in_specs = (
        P("seq", "head"),
        P("seq", "head"),
        P("seq", "head"),
        P("seq", "head"),
        P("head", None, None),
        P(),
    )
    out_specs = (P("seq", "head"), P("seq", "head"), P("seq", "head"), P("seq", "head"))
    return jax.shard_map(
        per_device, mesh=mesh, in_specs=in_specs, out_specs=out_specs, check_vma=False
    )
```

```python
import functools
import math

import jax
import jax.numpy as jnp
from jax import lax
from jax.experimental import pallas as pl
from jax.experimental.pallas import tpu as pltpu
from jax.sharding import PartitionSpec as P

HEAD_DIM = 128
BLK = 64
NZ = 8
NX = 4
NC = 2
NSEQ = NZ * NX * NC
BLK_DEV = 4
REQ = 12
SLOTS = 2 * REQ + 2
ENTRIES = NX * SLOTS
PARTS = 4
PART = 128
ROWS = BLK // 2
CAP = 15
TERMS = SLOTS + 3 * CAP
VMEM_LIMIT = 56 * 1024 * 1024


def seq_of(z, x, c):
    return (lax.rem(z + NZ, NZ) * NX + lax.rem(x + NX, NX)) * NC + c


def place():
    me = lax.axis_index("seq")
    z = me // (NX * NC)
    x = lax.rem(me // NC, NX)
    c = lax.rem(me, NC)
    return me, z, x, c


def remote(src, dst, send_sem, recv_sem, target):
    return pltpu.make_async_remote_copy(
        src_ref=src,
        dst_ref=dst,
        send_sem=send_sem,
        recv_sem=recv_sem,
        device_id={"seq": target},
        device_id_type=pl.DeviceIdType.MESH,
    )


def greet(partners):
    barrier = pltpu.get_barrier_semaphore()
    for partner in partners:
        pl.semaphore_signal(
            barrier, inc=1, device_id={"seq": partner}, device_id_type=pl.DeviceIdType.MESH
        )
    pl.semaphore_wait(barrier, len(partners))


def block_place(block):
    return lax.rem(lax.div(block, 8), NX), lax.div(block, 32) * 8 + lax.rem(block, 8)


Z_LAST = {(0, 0): 4, (0, 1): 3, (1, 0): 3, (1, 1): 4}


def gather_kernel(
    table, k_ref, v_ref, out_ref, halo_ref,
    s1_out, s1_in, s2_out, s2_in, s3_out, s3_in, give,
    pair_sem, halo_send, halo_recv, z_send, z_recv, x_send, x_recv, give_sem, *ag,
):
    me, z, x, c = place()
    other = 1 - c
    sibling = seq_of(z, x, other)
    after = lax.rem(me + 1, NSEQ)
    before = lax.rem(me + NSEQ - 1, NSEQ)
    xs = (seq_of(z, x + 1, c), seq_of(z, x - 1, c))
    zs = (seq_of(z + 1, x, c), seq_of(z - 1, x, c))
    greet((after, before, zs[0], zs[1], xs[0], xs[1]))

    def lanes(p):
        return pl.ds(p * PART, PART)

    def pair_copy(src, p):
        return remote(
            src.at[:, :, lanes(p)], ag[p].at[pl.ds(z * 8 + c * 4, 4)],
            pair_sem.at[0, p], pair_sem.at[1, p], sibling,
        )

    @pl.when(c == 0)
    def _():
        for p in range(PARTS):
            pair_copy(v_ref, p).start()
        for p in range(PARTS):
            ag[p][pl.ds(z * 8, 4)] = k_ref[:, :, p * PART : (p + 1) * PART]

    @pl.when(c == 1)
    def _():
        for p in range(PARTS):
            pair_copy(k_ref, p).start()
        for p in range(PARTS):
            ag[p][pl.ds(z * 8 + 4, 4)] = v_ref[:, :, p * PART : (p + 1) * PART]

    def z_piece(p, direction, step, half):
        origin = lax.rem(z + NZ - (step - 1), NZ) if direction == 0 else lax.rem(z + step - 1, NZ)
        piece = ag[p].at[pl.ds(origin * 8 + half * 4, 4)]
        return remote(
            piece,
            piece,
            z_send.at[p, direction, step - 1, half],
            z_recv.at[p, direction, step - 1, half],
            zs[direction],
        )

    def z_start(p):
        for direction in range(2):
            z_piece(p, direction, 1, c).start()
        pair_copy(v_ref, p).wait()
        for direction in range(2):
            z_piece(p, direction, 1, other).start()

    def z_step(p, step):
        for half in range(2):
            for direction in range(2):
                if step <= Z_LAST[direction, half]:
                    z_piece(p, direction, step, half).wait_recv()
                    if step + 1 <= Z_LAST[direction, half]:
                        z_piece(p, direction, step + 1, half).start()

    def wanted(p, chip, slot):
        source, at = block_place(table[(z * NX + lax.rem(chip + NX, NX)) * SLOTS + slot])
        return source, ag[p][at]

    def x_copy(p, number, g):
        src, dst, way = ((s1_out, s1_in, g), (s2_out, s2_in, g), (s3_out, s3_in, 1 - g))[number]
        return remote(
            src.at[p, g], dst.at[p, g], x_send.at[p, number, g], x_recv.at[p, number, g], xs[way]
        )

    def x_first(p):
        @pl.loop(0, SLOTS, unroll=2)
        def _(slot):
            mine = wanted(p, x + 2, slot)[1]
            s1_out[p, 0, slot] = mine[:ROWS]
            s1_out[p, 1, slot] = mine[ROWS:]

        for g in range(2):
            x_copy(p, 0, g).start()

        @pl.loop(0, SLOTS, unroll=2)
        def _(slot):
            s3_out[p, 0, slot] = wanted(p, x - 1, slot)[1][:ROWS]
            s3_out[p, 1, slot] = wanted(p, x + 1, slot)[1][ROWS:]

        for g in range(2):
            x_copy(p, 2, g).start()

    def x_second(p):
        for g in range(2):
            x_copy(p, 0, g).wait_recv()

        @pl.loop(0, SLOTS, unroll=2)
        def _(slot):
            source, mine = wanted(p, x + 1, slot)
            s2_out[p, 0, slot] = jnp.where(source == x, mine[:ROWS], s1_in[p, 0, slot])
            source, mine = wanted(p, x - 1, slot)
            s2_out[p, 1, slot] = jnp.where(source == x, mine[ROWS:], s1_in[p, 1, slot])

        for g in range(2):
            x_copy(p, 1, g).start()

    here = (lax.rem(x + 1, NX), lax.rem(x + NX - 1, NX))

    def chosen(p, slot):
        source, mine = wanted(p, x, slot)
        passed = [
            jnp.where(source == here[g], s3_in[p, g, slot], s2_in[p, g, slot]) for g in range(2)
        ]
        return jnp.where(source == x, mine, jnp.concatenate(passed, axis=0))

    def handed(p):
        return remote(
            give.at[p], out_ref.at[c, :, :, lanes(p)], give_sem.at[0, p], give_sem.at[1, p],
            sibling,
        )

    def finish(p):
        for number in (2, 1):
            for g in range(2):
                x_copy(p, number, g).wait_recv()
        columns = slice(p * PART, (p + 1) * PART)

        @pl.loop(0, REQ, unroll=2)
        def _(i):
            give[p, i] = chosen(p, other * (REQ + 2) + i)

        for i in range(2):
            value = chosen(p, REQ + i)
            give[p, REQ + i] = value
            out_ref[c, REQ + i, :, columns] = value
        handed(p).start()

        @pl.loop(0, REQ, unroll=2)
        def _(i):
            out_ref[c, i, :, columns] = chosen(p, c * (REQ + 2) + i)

    halos = []
    for number, ref in enumerate((k_ref, v_ref)):
        for side, (row, target) in enumerate(((BLK_DEV - 1, after), (0, before))):
            halos.append(
                remote(
                    ref.at[row], halo_ref.at[number, side], halo_send.at[number, side],
                    halo_recv.at[number, side], target,
                )
            )

    z_start(0)
    for step in range(1, 5):
        z_step(0, step)
    if PARTS > 1:
        z_start(1)
    x_first(0)
    for p in range(PARTS):
        more = p + 1 < PARTS
        if more:
            z_step(p + 1, 1)
            z_step(p + 1, 2)
        x_second(p)
        if more:
            z_step(p + 1, 3)
            z_step(p + 1, 4)
            if p + 2 < PARTS:
                z_start(p + 2)
            x_first(p + 1)
        else:
            for copy in halos:
                copy.start()
        finish(p)

    for copy in halos:
        copy.wait()
    for p in range(PARTS):
        for (direction, half), last in Z_LAST.items():
            for step in range(1, last + 1):
                z_piece(p, direction, step, half).wait_send()
        for number in range(3):
            for g in range(2):
                x_copy(p, number, g).wait_send()
        handed(p).wait()


def gather(table, k, v):
    features = k.shape[-1]
    big = pltpu.VMEM((PARTS, 2, SLOTS, ROWS, PART), jnp.bfloat16)
    vmem = pl.BlockSpec(memory_space=pltpu.VMEM)
    smem = pl.BlockSpec(memory_space=pltpu.SMEM)
    dma = pltpu.SemaphoreType.DMA
    return pl.pallas_call(
        gather_kernel,
        out_shape=(
            jax.ShapeDtypeStruct((2, REQ + 2, BLK, features), jnp.bfloat16),
            jax.ShapeDtypeStruct((2, 2, BLK, features), jnp.bfloat16),
        ),
        in_specs=[smem, vmem, vmem],
        out_specs=(vmem, vmem),
        scratch_shapes=[
            big, big, big, big, big, big,
            pltpu.VMEM((PARTS, REQ + 2, BLK, PART), jnp.bfloat16),
            dma((2, PARTS)), dma((2, 2)), dma((2, 2)), dma((PARTS, 2, 4, 2)), dma((PARTS, 2, 4, 2)),
            dma((PARTS, 3, 2)), dma((PARTS, 3, 2)), dma((2, PARTS)),
        ]
        + [pltpu.VMEM((NZ * 8, BLK, PART), jnp.bfloat16)] * PARTS,
        compiler_params=pltpu.CompilerParams(
            collective_id=0, has_side_effects=True, vmem_limit_bytes=VMEM_LIMIT
        ),
        name="gather_blocks",
    )(table, k, v)


def nt(a, b):
    return lax.dot_general(a, b, (((1,), (1,)), ((), ())), preferred_element_type=jnp.float32)


def tn(a, b):
    return lax.dot_general(a, b, (((0,), (0,)), ((), ())), preferred_element_type=jnp.float32)


def nn(a, b):
    return lax.dot_general(a, b, (((1,), (0,)), ((), ())), preferred_element_type=jnp.float32)


def attend_kernel(
    q_ref, g_ref, k_ref, v_ref, halo_ref, slot_ref,
    att_ref, qg_ref, wacc_ref, term_ref, rim_ref, acc, gacc,
):
    me = lax.axis_index("seq")
    features = q_ref.shape[-1]
    heads = features // HEAD_DIM
    scale = 1.0 / math.sqrt(HEAD_DIM)
    lane_head = lax.broadcasted_iota(jnp.int32, (BLK, features), 1) // HEAD_DIM
    acc[...] = jnp.zeros_like(acc)
    gacc[...] = jnp.zeros_like(gacc)

    def spread(rows):
        zero = jnp.zeros_like(rows)
        return jnp.concatenate(
            [jnp.where(lane_head == h, rows, zero) for h in range(heads)], axis=0
        )

    def diagonal(full):
        return jnp.concatenate(
            [
                full[h * BLK : (h + 1) * BLK, h * HEAD_DIM : (h + 1) * HEAD_DIM]
                for h in range(heads)
            ],
            axis=1,
        )

    for b in range(BLK_DEV):
        def listed(number, own):
            window = [
                halo_ref[number, 0] if b == 0 else own[b - 1],
                own[b],
                halo_ref[number, 1] if b == BLK_DEV - 1 else own[b + 1],
            ]
            extra = [slot_ref[number, REQ], slot_ref[number, REQ + 1]]
            random = [slot_ref[number, 3 * b + i] for i in range(3)]
            return jnp.concatenate(window + extra + random, axis=0)

        keys = listed(0, k_ref)
        values = listed(1, v_ref)
        query = spread(q_ref[b])
        grad = spread(g_ref[b])
        scores = nt(keys, query) * scale
        if b == 0:
            scores = jnp.concatenate(
                [jnp.where(me == 0, -jnp.inf, scores[:BLK]), scores[BLK:]], axis=0
            )
        if b == BLK_DEV - 1:
            scores = jnp.concatenate(
                [
                    scores[: 2 * BLK],
                    jnp.where(me == NSEQ - 1, -jnp.inf, scores[2 * BLK : 3 * BLK]),
                    scores[3 * BLK :],
                ],
                axis=0,
            )
        row_max = jnp.max(scores, axis=0, keepdims=True)
        raw = jnp.exp(scores - row_max)
        weights = raw * (1.0 / jnp.sum(raw, axis=0, keepdims=True))
        weights_b = weights.astype(jnp.bfloat16)
        weight_grads = nt(values, grad)
        row_dot = jnp.sum(weights_b.astype(jnp.float32) * weight_grads, axis=0, keepdims=True)
        score_grads = (weights * (weight_grads - row_dot) * scale).astype(jnp.bfloat16)
        att_ref[b] = diagonal(tn(weights_b, values)).astype(jnp.bfloat16)
        qg_ref[b] = diagonal(tn(score_grads, keys)).astype(jnp.bfloat16)
        for number, terms in enumerate((nn(score_grads, query), nn(weights_b, grad))):
            for i in range(3):
                acc[number, b + i] += terms[i * BLK : (i + 1) * BLK]
            for i in range(2):
                gacc[number, i] += terms[(3 + i) * BLK : (4 + i) * BLK]
            for i in range(3):
                term_ref[number, 3 * b + i] = terms[(5 + i) * BLK : (6 + i) * BLK].astype(
                    jnp.bfloat16
                )
    for number in range(2):
        for i in range(2):
            term_ref[number, REQ + i] = gacc[number, i].astype(jnp.bfloat16)
        rim_ref[number, 0] = acc[number, 0].astype(jnp.bfloat16)
        rim_ref[number, 1] = acc[number, BLK_DEV + 1].astype(jnp.bfloat16)
        for i in range(BLK_DEV):
            wacc_ref[number, i] = acc[number, i + 1]


def attend(q, g, k, v, halo, slots):
    features = q.shape[-1]
    vmem = pl.BlockSpec(memory_space=pltpu.VMEM)
    own = jax.ShapeDtypeStruct((BLK_DEV, BLK, features), jnp.bfloat16)
    return pl.pallas_call(
        attend_kernel,
        out_shape=(
            own,
            own,
            jax.ShapeDtypeStruct((2, BLK_DEV, BLK, features), jnp.float32),
            jax.ShapeDtypeStruct((2, REQ + 2, BLK, features), jnp.bfloat16),
            jax.ShapeDtypeStruct((2, 2, BLK, features), jnp.bfloat16),
        ),
        in_specs=[vmem] * 6,
        out_specs=(vmem,) * 5,
        scratch_shapes=[
            pltpu.VMEM((2, BLK_DEV + 2, BLK, features), jnp.float32),
            pltpu.VMEM((2, 2, BLK, features), jnp.float32),
        ],
        compiler_params=pltpu.CompilerParams(vmem_limit_bytes=VMEM_LIMIT),
        name="attend_blocks",
    )(q, g, k, v, halo, slots)


def plan_kernel(table, prev_ref, last_ref):
    me, z, x, c = place()

    @pl.loop(0, NZ * 8)
    def _(at):
        last_ref[at] = ENTRIES

    @pl.loop(0, ENTRIES)
    def _(n):
        source, at = block_place(table[z * ENTRIES + n])
        prev_ref[n] = ENTRIES

        @pl.when(source == x)
        def _():
            prev_ref[n] = last_ref[at]
            last_ref[at] = n


def plan(table):
    smem = pl.BlockSpec(memory_space=pltpu.SMEM)
    return pl.pallas_call(
        plan_kernel,
        out_shape=(
            jax.ShapeDtypeStruct((ENTRIES,), jnp.int32),
            jax.ShapeDtypeStruct((NZ * 8,), jnp.int32),
        ),
        in_specs=[smem],
        out_specs=(smem, smem),
        name="plan_sums",
    )(table)


def back_kernel(
    prev, last, term_ref, rim_ref, out_ref, edge_ref,
    theirs, everything, chain, landed, send_buf, recv_buf, give,
    pair_sem, rim_send, rim_recv, x_send, x_recv, z_send, z_recv, give_sem,
):
    me, z, x, c = place()
    other = 1 - c
    sibling = seq_of(z, x, other)
    after = lax.rem(me + 1, NSEQ)
    before = lax.rem(me + NSEQ - 1, NSEQ)
    xs = (seq_of(z, x + 1, c), seq_of(z, x - 1, c))
    zs = (seq_of(z + 1, x, c), seq_of(z - 1, x, c))
    greet((after, before, xs[0], xs[1], zs[0], zs[1]))

    def lanes(p):
        return pl.ds(p * PART, PART)

    def pair(p):
        return remote(
            term_ref.at[other, :, :, lanes(p)], theirs.at[p], pair_sem.at[0, p],
            pair_sem.at[1, p], sibling,
        )

    for p in range(PARTS):
        pair(p).start()

    def own(p, chip, g):
        base = lax.rem(chip + NX, NX) * SLOTS
        return everything.at[p, pl.ds(base + c * (REQ + 2), REQ), pl.ds(g * ROWS, ROWS)]

    def rest(p, chip, g):
        base = lax.rem(chip + NX, NX) * SLOTS
        return everything.at[p, pl.ds(base + other * REQ, REQ + 2), pl.ds(g * ROWS, ROWS)]

    def send(p, number, chip, which, g):
        ref = (own, rest)[which](p, chip, g)
        return remote(
            ref, ref, x_send.at[p, number, which, g], x_recv.at[p, number, which, g],
            xs[(g, 1 - g, g)[number]],
        )

    def x_first(p):
        columns = slice(p * PART, (p + 1) * PART)
        base = x * SLOTS

        @pl.loop(0, REQ, unroll=2)
        def _(i):
            everything[p, base + c * (REQ + 2) + i] = term_ref[c, i, :, columns]

        for number in range(2):
            for g in range(2):
                send(p, number, x, 0, g).start()
        pair(p).wait_recv()

        @pl.loop(0, REQ, unroll=2)
        def _(i):
            everything[p, base + other * (REQ + 2) + i] = theirs[p, i]

        for i in range(2):
            total = term_ref[c, REQ + i, :, columns].astype(jnp.float32) + theirs[
                p, REQ + i
            ].astype(jnp.float32)
            everything[p, base + REQ + i] = total.astype(jnp.bfloat16)
        for number in range(2):
            for g in range(2):
                send(p, number, x, 1, g).start()

    def x_second(p):
        for which in range(2):
            for g, behind in enumerate((x - 1, x + 1)):
                send(p, 0, behind, which, g).wait_recv()
                send(p, 2, behind, which, g).start()

    def x_wait(p, number):
        for which in range(2):
            for g in range(2):
                send(p, number, x, which, g).wait_recv()

    chain[ENTRIES] = jnp.zeros((BLK, PART), jnp.float32)

    def land(p):
        @pl.loop(0, ENTRIES, unroll=4)
        def _(n):
            chain[n] = everything[p, n].astype(jnp.float32) + chain[prev[n]]

        @pl.loop(0, NZ * 8, unroll=4)
        def _(at):
            landed[p, at] = chain[last[at]]

    def piece(p, direction, distance, half):
        return remote(
            send_buf.at[p, direction, distance - 1, half],
            recv_buf.at[p, direction, distance - 1, half],
            z_send.at[p, direction, distance - 1, half],
            z_recv.at[p, direction, distance - 1, half],
            zs[direction],
        )

    def z_step(p, distance):
        for half in range(2):
            for direction in range(2):
                if distance > Z_LAST[direction, half]:
                    continue
                target = lax.rem(z + (distance if direction == 0 else NZ - distance), NZ)
                first = target * 8 + half * 4
                waits = distance < Z_LAST[direction, half]
                if waits:
                    piece(p, direction, distance + 1, half).wait_recv()
                for i in range(BLK_DEV):
                    total = landed[p, first + i]
                    if waits:
                        total += recv_buf[p, direction, distance, half, i].astype(jnp.float32)
                    send_buf[p, direction, distance - 1, half, i] = total.astype(jnp.bfloat16)
                piece(p, direction, distance, half).start()

    def handed(p):
        return remote(
            give.at[p], out_ref.at[c, :, :, lanes(p)], give_sem.at[0, p], give_sem.at[1, p],
            sibling,
        )

    def finish(p):
        columns = slice(p * PART, (p + 1) * PART)
        for half in range(2):
            for direction in range(2):
                piece(p, direction, 1, half).wait_recv()

        def finished(half, i):
            total = landed[p, z * 8 + half * 4 + i]
            for direction in range(2):
                total += recv_buf[p, direction, 0, half, i].astype(jnp.float32)
            return total.astype(jnp.bfloat16)

        for i in range(BLK_DEV):
            give[p, i] = finished(other, i)
        handed(p).start()
        for i in range(BLK_DEV):
            out_ref[c, i, :, columns] = finished(c, i)

    edges = []
    for number in range(2):
        for side, target in enumerate((after, before)):
            edges.append(
                remote(
                    rim_ref.at[number, 1 - side], edge_ref.at[number, side],
                    rim_send.at[number, side], rim_recv.at[number, side], target,
                )
            )

    x_first(0)
    for p in range(PARTS):
        x_second(p)
        if p + 1 < PARTS:
            x_first(p + 1)
        else:
            for copy in edges:
                copy.start()
        if p:
            z_step(p - 1, 3)
        x_wait(p, 1)
        if p:
            z_step(p - 1, 2)
        x_wait(p, 2)
        if p:
            z_step(p - 1, 1)
        land(p)
        z_step(p, 4)
        if p:
            finish(p - 1)
    for distance in (3, 2, 1):
        z_step(PARTS - 1, distance)
    finish(PARTS - 1)

    for copy in edges:
        copy.wait()
    for p in range(PARTS):
        pair(p).wait_send()
        for number in range(3):
            for which in range(2):
                for g in range(2):
                    send(p, number, x, which, g).wait_send()
        for (direction, half), most in Z_LAST.items():
            for distance in range(1, most + 1):
                piece(p, direction, distance, half).wait_send()
        handed(p).wait()


def send_back(prev, last, terms, rims):
    features = terms.shape[-1]
    vmem = pl.BlockSpec(memory_space=pltpu.VMEM)
    smem = pl.BlockSpec(memory_space=pltpu.SMEM)
    dma = pltpu.SemaphoreType.DMA
    ring = pltpu.VMEM((PARTS, 2, 4, 2, BLK_DEV, BLK, PART), jnp.bfloat16)
    return pl.pallas_call(
        back_kernel,
        out_shape=(
            jax.ShapeDtypeStruct((2, BLK_DEV, BLK, features), jnp.bfloat16),
            jax.ShapeDtypeStruct((2, 2, BLK, features), jnp.bfloat16),
        ),
        in_specs=[smem, smem, vmem, vmem],
        out_specs=(vmem, vmem),
        scratch_shapes=[
            pltpu.VMEM((PARTS, REQ + 2, BLK, PART), jnp.bfloat16),
            pltpu.VMEM((PARTS, ENTRIES, BLK, PART), jnp.bfloat16),
            pltpu.VMEM((ENTRIES + 1, BLK, PART), jnp.float32),
            pltpu.VMEM((PARTS, NZ * 8, BLK, PART), jnp.float32),
            ring, ring,
            pltpu.VMEM((PARTS, BLK_DEV, BLK, PART), jnp.bfloat16),
            dma((2, PARTS)), dma((2, 2)), dma((2, 2)), dma((PARTS, 3, 2, 2)), dma((PARTS, 3, 2, 2)),
            dma((PARTS, 2, 4, 2)), dma((PARTS, 2, 4, 2)), dma((2, PARTS)),
        ],
        compiler_params=pltpu.CompilerParams(
            collective_id=1, has_side_effects=True, vmem_limit_bytes=VMEM_LIMIT
        ),
        name="send_back",
    )(prev, last, terms, rims)


def list_kernel(
    pairs, shared, wide_ref, at_ref, code_ref, back_ref, prev_ref, last_ref, most_ref, count
):
    me, z, x, c = place()

    source = lax.rem(lax.div(wide_ref[...], 8), NX)
    chip = lax.rem(lax.broadcasted_iota(jnp.int32, (NZ * NX, 1), 0), NX)
    holders = [block_place(shared[i])[0] for i in range(2)]
    most = jnp.zeros((NZ * NX, 1), jnp.int32)
    for s in range(NX):
        asked = jnp.sum((source == s).astype(jnp.int32), axis=1, keepdims=True)
        asked += sum((holder == s).astype(jnp.int32) for holder in holders)
        most = jnp.maximum(most, jnp.where(chip == s, 0, asked))
    most_ref[0] = jnp.max(most)

    @pl.loop(0, NZ * 8, unroll=8)
    def _(at):
        last_ref[at] = TERMS

    last_ref[NZ * 8] = TERMS

    @pl.loop(0, 3 * CAP, unroll=5)
    def _(n):
        at_ref[n] = 0
        back_ref[n] = 0
        prev_ref[SLOTS + n] = TERMS

    for r in range(NX):
        count[r] = 0

    def visit_all(chip, visit):
        row = z * NX + lax.rem(chip, NX)

        @pl.loop(0, REQ, unroll=4)
        def _(i):
            visit(i, *block_place(pairs[row, i]))

        for i in range(2):
            visit(REQ + i, *block_place(shared[i]))

        @pl.loop(0, REQ, unroll=4)
        def _(i):
            visit(REQ + 2 + i, *block_place(pairs[row, REQ + i]))

    def request(slot, holder, at):
        r = lax.rem(holder - x + NX, NX)
        j = count[r]
        count[r] = j + 1
        fits = (r > 0) & (j < CAP)
        n = jnp.where(fits, (r - 1) * CAP + j, 3 * CAP)
        code_ref[slot] = jnp.where(fits, NZ * 8 + n, at)
        back_ref[n] = slot
        chained = jnp.where(r == 0, at, NZ * 8)
        prev_ref[slot] = jnp.where(r == 0, last_ref[chained], TERMS)
        last_ref[chained] = slot

    visit_all(x, request)
    for r in range(1, NX):
        count[0] = 0

        def serve(slot, holder, at):
            j = count[0]
            hit = (holder == x) & (j < CAP)
            count[0] = j + hit.astype(jnp.int32)
            n = jnp.where(hit, (r - 1) * CAP + j, 3 * CAP)
            at_ref[n] = at
            chained = jnp.where(hit, at, NZ * 8)
            prev_ref[SLOTS + n] = last_ref[chained]
            last_ref[chained] = SLOTS + n

        visit_all(x + r, serve)


def make_lists(pairs, shared):
    smem = pl.BlockSpec(memory_space=pltpu.SMEM)
    vmem = pl.BlockSpec(memory_space=pltpu.VMEM)
    sizes = (3 * CAP + 1, SLOTS, 3 * CAP + 1, TERMS + 1, NZ * 8 + 1, 1)
    return pl.pallas_call(
        list_kernel,
        out_shape=tuple(jax.ShapeDtypeStruct((size,), jnp.int32) for size in sizes),
        in_specs=[smem, smem, vmem],
        out_specs=(smem,) * 6,
        scratch_shapes=[pltpu.SMEM((NX,), jnp.int32)],
        name="make_lists",
    )(pairs, shared, pairs)


ORDER = (
    ("z_start", 0), ("z_start", 1), ("z1", 0), ("z2", 0), ("z3", 0),
    ("z4", 0), ("z1", 1), ("x_start", 0), ("z2", 1), ("z3", 1),
    ("z4", 1), ("x_start", 1), ("z_start", 2), ("z_start", 3), ("x_finish", 0),
    ("attend", 0), ("z1", 3), ("back_x", 0), ("z2", 3), ("z3", 3),
    ("x_finish", 1), ("z4", 3), ("z1", 2), ("x_start", 3), ("land", 0),
    ("z2", 2), ("attend", 1), ("back_x", 1), ("b4", 0), ("z3", 2),
    ("b3", 0), ("x_finish", 3), ("attend", 3), ("z4", 2), ("x_start", 2),
    ("b2", 0), ("b1", 0), ("land", 1), ("b4", 1), ("back_x", 3),
    ("finish", 0), ("b3", 1), ("b2", 1), ("x_finish", 2), ("attend", 2),
    ("back_x", 2), ("b1", 1), ("land", 3), ("b4", 3), ("b3", 3),
    ("b2", 3), ("land", 2), ("b4", 2), ("b3", 2), ("finish", 1),
    ("b1", 3), ("b2", 2), ("finish", 3), ("b1", 2), ("finish", 2),
)


def layer_kernel(
    at_list, code_list, back_list, prev, last, q_ref, g_ref, k_ref, v_ref,
    att_ref, qg_ref, wacc_ref, out_ref, edge_ref,
    packed, give, kv, halo, wide, window, shared, terms, rim,
    theirs, own, back_packed, arrived, chain, landed, send_buf, recv_buf, give_back,
    pair_sem, halo_send, halo_recv, z_send, z_recv, x_send, x_recv, give_sem,
    back_pair, rim_send, rim_recv, bx_send, bx_recv, bz_send, bz_recv, back_give,
    *bufs,
):
    ag, landing = bufs[:PARTS], bufs[PARTS:]
    me, z, x, c = place()
    other = 1 - c
    sibling = seq_of(z, x, other)
    after = lax.rem(me + 1, NSEQ)
    before = lax.rem(me + NSEQ - 1, NSEQ)
    zs = (seq_of(z + 1, x, c), seq_of(z - 1, x, c))
    xs = tuple(seq_of(z, x + r, c) for r in range(1, NX))
    greet((after, before) + zs + xs)

    def lanes(p):
        return pl.ds(p * PART, PART)

    def columns(p):
        return slice(p * PART, (p + 1) * PART)

    def pair_copy(src, p):
        return remote(
            src.at[:, :, lanes(p)], ag[p].at[pl.ds(z * 8 + c * 4, 4)],
            pair_sem.at[0, p], pair_sem.at[1, p], sibling,
        )

    @pl.when(c == 0)
    def _():
        for p in range(PARTS):
            pair_copy(v_ref, p).start()
        for p in range(PARTS):
            ag[p][pl.ds(z * 8, 4)] = k_ref[:, :, columns(p)]

    @pl.when(c == 1)
    def _():
        for p in range(PARTS):
            pair_copy(k_ref, p).start()
        for p in range(PARTS):
            ag[p][pl.ds(z * 8 + 4, 4)] = v_ref[:, :, columns(p)]

    def z_piece(p, direction, step, half):
        origin = lax.rem(z + NZ - (step - 1), NZ) if direction == 0 else lax.rem(z + step - 1, NZ)
        piece = ag[p].at[pl.ds(origin * 8 + half * 4, 4)]
        return remote(
            piece,
            piece,
            z_send.at[p, direction, step - 1, half],
            z_recv.at[p, direction, step - 1, half],
            zs[direction],
        )

    def z_start(p):
        for direction in range(2):
            z_piece(p, direction, 1, c).start()
        pair_copy(v_ref, p).wait()
        for direction in range(2):
            z_piece(p, direction, 1, other).start()

    def z_step(p, step):
        for half in range(2):
            for direction in range(2):
                if step <= Z_LAST[direction, half]:
                    z_piece(p, direction, step, half).wait_recv()
                    if step + 1 <= Z_LAST[direction, half]:
                        z_piece(p, direction, step + 1, half).start()

    def x_copy(p, r):
        return remote(
            packed.at[p, pl.ds((r - 1) * CAP, CAP)],
            landing[p].at[pl.ds((NX - 1 - r) * CAP, CAP)],
            x_send.at[p, r - 1],
            x_recv.at[p, NX - 1 - r],
            xs[r - 1],
        )

    def x_start(p):
        for r in (1, 3, 2):
            @pl.loop(0, CAP, unroll=3)
            def _(j):
                n = (r - 1) * CAP + j
                packed[p, n] = ag[p][at_list[n]]

            x_copy(p, r).start()

    def chosen(p, slot):
        code = code_list[slot]
        held = ag[p][jnp.minimum(code, NZ * 8 - 1)]
        return jnp.where(code < NZ * 8, held, landing[p][jnp.maximum(code - NZ * 8, 0)])

    def handed(p):
        return remote(give.at[p], kv.at[p, c], give_sem.at[0, p], give_sem.at[1, p], sibling)

    def x_finish(p):
        for r in range(1, NX):
            x_copy(p, r).wait_recv()

        @pl.loop(0, REQ, unroll=2)
        def _(i):
            give[p, i] = chosen(p, other * (REQ + 2) + i)

        for i in range(2):
            value = chosen(p, REQ + i)
            give[p, REQ + i] = value
            kv[p, c, REQ + i] = value
        handed(p).start()

        @pl.loop(0, REQ, unroll=2)
        def _(i):
            kv[p, c, i] = chosen(p, c * (REQ + 2) + i)

    halos = []
    for number, ref in enumerate((k_ref, v_ref)):
        for side, (row, target) in enumerate(((BLK_DEV - 1, after), (0, before))):
            halos.append(
                remote(
                    ref.at[row], halo.at[number, side], halo_send.at[number, side],
                    halo_recv.at[number, side], target,
                )
            )

    scale = 1.0 / math.sqrt(HEAD_DIM)
    entry = lax.broadcasted_iota(jnp.int32, (BLK, 8 * BLK), 1) // BLK

    def attend_part(p):
        handed(p).wait()
        for number, ref in enumerate((k_ref, v_ref)):
            wide[number, 0] = halo[number, 0, :, columns(p)]
            wide[number, BLK_DEV + 1] = halo[number, 1, :, columns(p)]
            for i in range(BLK_DEV):
                wide[number, i + 1] = ref[i, :, columns(p)]
        window[...] = jnp.zeros_like(window)
        shared[...] = jnp.zeros_like(shared)

        @pl.loop(0, BLK_DEV)
        def _(b):
            def listed(number):
                return jnp.concatenate(
                    [wide[number, b + i] for i in range(3)]
                    + [kv[p, number, REQ + i] for i in range(2)]
                    + [kv[p, number, 3 * b + i] for i in range(3)],
                    axis=0,
                )

            keys = listed(0)
            values = listed(1)
            query = q_ref[b, :, columns(p)]
            grad = g_ref[b, :, columns(p)]
            low = jnp.where(me * BLK_DEV + b == 0, 0, -1)
            high = jnp.where(me * BLK_DEV + b == NSEQ * BLK_DEV - 1, 2, -1)
            scores = nt(query, keys) * scale
            scores = jnp.where((entry == low) | (entry == high), -jnp.inf, scores)
            row_max = jnp.max(scores, axis=1, keepdims=True)
            raw = jnp.exp(scores - row_max)
            weights = raw * (1.0 / jnp.sum(raw, axis=1, keepdims=True))
            weights_b = weights.astype(jnp.bfloat16)
            weight_grads = nt(grad, values)
            row_dot = jnp.sum(weights_b.astype(jnp.float32) * weight_grads, axis=1, keepdims=True)
            score_grads = (weights * (weight_grads - row_dot) * scale).astype(jnp.bfloat16)
            att_ref[b, :, columns(p)] = nn(weights_b, values).astype(jnp.bfloat16)
            qg_ref[b, :, columns(p)] = nn(score_grads, keys).astype(jnp.bfloat16)
            for number, made in enumerate((tn(score_grads, query), tn(weights_b, grad))):
                for i in range(3):
                    window[number, b + i] += made[i * BLK : (i + 1) * BLK]
                for i in range(2):
                    shared[number, i] += made[(3 + i) * BLK : (4 + i) * BLK]
                for i in range(3):
                    terms[p, number, 3 * b + i] = made[(5 + i) * BLK : (6 + i) * BLK].astype(
                        jnp.bfloat16
                    )

        for number in range(2):
            for i in range(2):
                terms[p, number, REQ + i] = shared[number, i].astype(jnp.bfloat16)
            rim[number, 0, :, columns(p)] = window[number, 0].astype(jnp.bfloat16)
            rim[number, 1, :, columns(p)] = window[number, BLK_DEV + 1].astype(jnp.bfloat16)
            for i in range(BLK_DEV):
                wacc_ref[number, i, :, columns(p)] = window[number, i + 1]
        pair(p).start()

    def pair(p):
        return remote(
            terms.at[p, other], theirs.at[p], back_pair.at[0, p], back_pair.at[1, p], sibling
        )

    def bx_copy(p, r):
        return remote(
            back_packed.at[p, pl.ds((r - 1) * CAP, CAP)],
            arrived.at[p, pl.ds((NX - 1 - r) * CAP, CAP)],
            bx_send.at[p, r - 1],
            bx_recv.at[p, NX - 1 - r],
            xs[r - 1],
        )

    def bx_start(p):
        @pl.loop(0, REQ, unroll=2)
        def _(i):
            own[p, c * (REQ + 2) + i] = terms[p, c, i]

        pair(p).wait_recv()

        @pl.loop(0, REQ, unroll=2)
        def _(i):
            own[p, other * (REQ + 2) + i] = theirs[p, i]

        for i in range(2):
            total = terms[p, c, REQ + i].astype(jnp.float32) + theirs[p, REQ + i].astype(
                jnp.float32
            )
            own[p, REQ + i] = total.astype(jnp.bfloat16)
        for r in (1, 3, 2):
            @pl.loop(0, CAP, unroll=3)
            def _(j):
                n = (r - 1) * CAP + j
                back_packed[p, n] = own[p, back_list[n]]

            bx_copy(p, r).start()

    chain[TERMS] = jnp.zeros((BLK, PART), jnp.float32)

    def land(p):
        @pl.loop(0, SLOTS, unroll=2)
        def _(n):
            chain[n] = own[p, n].astype(jnp.float32) + chain[prev[n]]

        for r in range(1, NX):
            bx_copy(p, r).wait_recv()

        @pl.loop(0, 3 * CAP, unroll=3)
        def _(n):
            chain[SLOTS + n] = arrived[p, n].astype(jnp.float32) + chain[prev[SLOTS + n]]

        @pl.loop(0, NZ * 8, unroll=4)
        def _(at):
            landed[p, at] = chain[last[at]]

    def piece(p, direction, distance, half):
        return remote(
            send_buf.at[p, direction, distance - 1, half],
            recv_buf.at[p, direction, distance - 1, half],
            bz_send.at[p, direction, distance - 1, half],
            bz_recv.at[p, direction, distance - 1, half],
            zs[direction],
        )

    def bz_step(p, distance):
        for half in range(2):
            for direction in range(2):
                if distance > Z_LAST[direction, half]:
                    continue
                target = lax.rem(z + (distance if direction == 0 else NZ - distance), NZ)
                first = target * 8 + half * 4
                waits = distance < Z_LAST[direction, half]
                if waits:
                    piece(p, direction, distance + 1, half).wait_recv()
                for i in range(BLK_DEV):
                    total = landed[p, first + i]
                    if waits:
                        total += recv_buf[p, direction, distance, half, i].astype(jnp.float32)
                    send_buf[p, direction, distance - 1, half, i] = total.astype(jnp.bfloat16)
                piece(p, direction, distance, half).start()

    def handed_back(p):
        return remote(
            give_back.at[p], out_ref.at[c, :, :, lanes(p)], back_give.at[0, p], back_give.at[1, p],
            sibling,
        )

    def bz_finish(p):
        for half in range(2):
            for direction in range(2):
                piece(p, direction, 1, half).wait_recv()

        def finished(half, i):
            total = landed[p, z * 8 + half * 4 + i]
            for direction in range(2):
                total += recv_buf[p, direction, 0, half, i].astype(jnp.float32)
            return total.astype(jnp.bfloat16)

        for i in range(BLK_DEV):
            give_back[p, i] = finished(other, i)
        handed_back(p).start()
        for i in range(BLK_DEV):
            out_ref[c, i, :, columns(p)] = finished(c, i)

    edges = []
    for number in range(2):
        for side, target in enumerate((after, before)):
            edges.append(
                remote(
                    rim.at[number, 1 - side], edge_ref.at[number, side],
                    rim_send.at[number, side], rim_recv.at[number, side], target,
                )
            )

    steps = {
        "z_start": z_start,
        "x_start": x_start,
        "x_finish": x_finish,
        "attend": attend_part,
        "back_x": bx_start,
        "land": land,
        "finish": bz_finish,
    }
    for i in range(1, 5):
        steps[f"z{i}"] = functools.partial(z_step, step=i)
        steps[f"b{i}"] = functools.partial(bz_step, distance=i)
    attended = 0
    for number, (name, p) in enumerate(ORDER):
        if name == "attend" and not attended:
            for copy in halos:
                copy.wait()
        steps[name](p)
        if number == 2:
            for copy in halos:
                copy.start()
        if name == "attend":
            attended += 1
            if attended == PARTS:
                for copy in edges:
                    copy.start()

    for copy in edges:
        copy.wait()
    for p in range(PARTS):
        for (direction, half), most in Z_LAST.items():
            for step in range(1, most + 1):
                z_piece(p, direction, step, half).wait_send()
                piece(p, direction, step, half).wait_send()
        for r in range(1, NX):
            x_copy(p, r).wait_send()
            bx_copy(p, r).wait_send()
        pair(p).wait_send()
        handed_back(p).wait()


def layer(lists, q, g, k, v):
    features = k.shape[-1]
    vmem = pl.BlockSpec(memory_space=pltpu.VMEM)
    smem = pl.BlockSpec(memory_space=pltpu.SMEM)
    dma = pltpu.SemaphoreType.DMA
    bf16, f32 = jnp.bfloat16, jnp.float32

    def tiles(*lead, dtype=bf16, width=PART):
        return pltpu.VMEM((*lead, BLK, width), dtype)

    ring = tiles(PARTS, 2, 4, 2, BLK_DEV)
    return pl.pallas_call(
        layer_kernel,
        out_shape=(
            jax.ShapeDtypeStruct((BLK_DEV, BLK, features), bf16),
            jax.ShapeDtypeStruct((BLK_DEV, BLK, features), bf16),
            jax.ShapeDtypeStruct((2, BLK_DEV, BLK, features), f32),
            jax.ShapeDtypeStruct((2, BLK_DEV, BLK, features), bf16),
            jax.ShapeDtypeStruct((2, 2, BLK, features), bf16),
        ),
        in_specs=[smem] * 5 + [vmem] * 4,
        out_specs=(vmem,) * 5,
        scratch_shapes=[
            tiles(PARTS, 3 * CAP), tiles(PARTS, REQ + 2), tiles(PARTS, 2, REQ + 2),
            tiles(2, 2, width=features), tiles(2, BLK_DEV + 2),
            tiles(2, BLK_DEV + 2, dtype=f32), tiles(2, 2, dtype=f32),
            tiles(PARTS, 2, REQ + 2), tiles(2, 2, width=features),
            tiles(PARTS, REQ + 2), tiles(PARTS, SLOTS), tiles(PARTS, 3 * CAP),
            tiles(PARTS, 3 * CAP), tiles(TERMS + 1, dtype=f32),
            tiles(PARTS, NZ * 8, dtype=f32), ring, ring, tiles(PARTS, BLK_DEV),
            dma((2, PARTS)), dma((2, 2)), dma((2, 2)), dma((PARTS, 2, 4, 2)), dma((PARTS, 2, 4, 2)),
            dma((PARTS, 3)), dma((PARTS, 3)), dma((2, PARTS)),
            dma((2, PARTS)), dma((2, 2)), dma((2, 2)), dma((PARTS, 3)), dma((PARTS, 3)),
            dma((PARTS, 2, 4, 2)), dma((PARTS, 2, 4, 2)), dma((2, PARTS)),
        ]
        + [tiles(NZ * 8)] * PARTS
        + [tiles(3 * CAP)] * PARTS,
        compiler_params=pltpu.CompilerParams(
            collective_id=2, has_side_effects=True, vmem_limit_bytes=VMEM_LIMIT
        ),
        name="layer",
    )(*lists, q, g, k, v)


def per_device(queries, key_rows, value_rows, out_grad, random_blocks, global_blocks):
    row_count, features = queries.shape
    blocks = (BLK_DEV, BLK, features)
    k = key_rows.reshape(blocks)
    v = value_rows.reshape(blocks)
    q = queries.reshape(blocks)
    g = out_grad.reshape(blocks)
    *packed_lists, most = make_lists(random_blocks.reshape(NZ * NX, 2 * REQ), global_blocks)

    def packed():
        attended, query_grad, *parts = layer(packed_lists, q, g, k, v)
        return attended, query_grad, *joined(*parts)

    def unpacked():
        lists = random_blocks.reshape(NZ * NX, NC, REQ)
        shared = jnp.broadcast_to(global_blocks[None], (NZ * NX, 2))
        flat = jnp.concatenate([lists[:, 0], shared, lists[:, 1]], axis=1).reshape(-1)
        prev, last = plan(flat)
        slots, halo = gather(flat, k, v)
        attended, query_grad, wacc, terms, rims = attend(q, g, k, v, halo, slots)
        total, edges = send_back(prev, last, terms, rims)
        return attended, query_grad, *joined(wacc, total, edges)

    results = lax.cond(most[0] <= CAP, packed, unpacked)
    return tuple(result.reshape(row_count, features) for result in results)


def joined(wacc, total, edges):
    gradient = wacc + total.astype(jnp.float32)
    gradient = gradient.at[:, 0].add(edges[:, 0].astype(jnp.float32))
    gradient = gradient.at[:, BLK_DEV - 1].add(edges[:, 1].astype(jnp.float32))
    gradient = gradient.astype(jnp.bfloat16)
    return gradient[0], gradient[1]


def solution(mesh):
    in_specs = (
        P("seq", "head"),
        P("seq", "head"),
        P("seq", "head"),
        P("seq", "head"),
        P("head", None, None),
        P(),
    )
    out_specs = (P("seq", "head"), P("seq", "head"), P("seq", "head"), P("seq", "head"))
    return jax.shard_map(
        per_device, mesh=mesh, in_specs=in_specs, out_specs=out_specs, check_vma=False
    )
```
